32 devices in a mesh: row: 4 (over z), col: 8 (over y, x, core).
Axes of the slice: x: 2, y: 2, z: 4, core: 2. Of those that a mesh axis runs over, the one named last changes fastest.
Arguments:
- pair: bfloat16 [512, 512, 128], P('row', 'col'), may hold values from -6 to 6
- grad_x: bfloat16 [512, 512, 64], P('row', 'col'), may hold values from -0.19921875 to 0.19921875
- norm_gain: float32 [128], replicated, may hold values from 0.1 to 1.9
- norm_bias: float32 [128], replicated, may hold values from -3 to 3
- proj_weight: bfloat16 [128, 256], replicated, may hold values from -0.5 to 0.5
- tile_mask: int32 [4, 4], replicated, may hold values 0 or 1
Outputs:
- grad_pair: bfloat16 [512, 512, 128], P('row', 'col')
The draws below stay inside these ranges and needn't reach their ends.
All inputs are finite; a program needn't handle non-finite values.
Results may differ from the reference program's by a relative error of at most 0.012.
Values may be sent and summed in bfloat16 or wider, within the bound.
No kernel may reach another device: no remote copies, remote signals or barrier semaphores. Data moves between devices by JAX's collectives and lax.ppermute only.
A program may use at most 128 MiB of HBM per device.

```python
import jax
import jax.numpy as jnp
from jax import lax

C = 128
H = 64
BLK = 128
N = 512
TILE_R = 128
NB = 4
N_ROW = 4


def plant(drawn, rng, least, top_value):
    longest = drawn.shape.index(max(drawn.shape))
    spots = []
    for shift in (0, 1):
        where = [jax.random.randint(jax.random.fold_in(rng, axis), (), 0, length) for axis, length in enumerate(drawn.shape)]
        where[longest] = (where[longest] + shift) % drawn.shape[longest]
        spots.append(tuple(where))
    return drawn.at[spots[0]].set(least).at[spots[1]].set(top_value)


def shard_levels(key, extent, cuts, low, high):
    level = 1.0
    for dim, blocks in cuts:
        heights = jax.random.uniform(jax.random.fold_in(jax.random.fold_in(key, 6), dim), (blocks,), jnp.float32, low / len(cuts), high / len(cuts))
        level = level * jnp.repeat(jnp.exp(heights), extent[dim] // blocks).reshape((-1,) + (1,) * (len(extent) - 1 - dim))
    return level


def noise(rng, shape, deviation, reach, pieces=(), kind=jnp.bfloat16):
    drawn = deviation * jax.random.normal(rng, shape, jnp.float32)
    if pieces:
        drawn = drawn * shard_levels(rng, shape, pieces, -0.22, 0.18)
    return jnp.clip(drawn, -reach, reach).astype(kind)


def setup_inputs(seed: int = 0) -> dict:
    seeds = jax.random.split(jax.random.key(seed), 7)
    pair = noise(seeds[0], (N, N, C), 1.0, 6.0, ((0, 4), (1, 8)))
    grad_x = noise(seeds[1], (N, N, H), 0.03125, 0.19921875, ((0, 4), (1, 8)))
    norm_gain = jnp.clip(1.0 + 0.18 * jax.random.normal(seeds[2], (C,), jnp.float32), 0.1, 1.9)
    norm_bias = noise(seeds[3], (C,), 0.5, 3.0, (), jnp.float32)
    proj_weight = noise(seeds[4], (C, 4 * H), C ** -0.5, 0.5)
    tile_mask = plant((jax.random.randint(seeds[5], (NB, NB), 0, 4) < 3).astype(jnp.int32), jax.random.fold_in(seeds[5], 1), 0, 1)
    return dict(pair=pair, grad_x=grad_x, norm_gain=norm_gain, norm_bias=norm_bias, proj_weight=proj_weight, tile_mask=tile_mask)


def normalize(pair, norm_gain, norm_bias):
    values = pair.astype(jnp.float32)
    centred = values - lax.optimization_barrier(jnp.mean(values, axis=-1, keepdims=True))
    variance = lax.optimization_barrier(jnp.mean(centred * centred, axis=-1, keepdims=True))
    inverse = lax.rsqrt(variance + 1e-05)
    scaled = centred * inverse
    normed = (scaled * norm_gain + norm_bias).astype(jnp.bfloat16)
    return (scaled, inverse, normed)

def reference(pair, grad_x, norm_gain, norm_bias, proj_weight, tile_mask):
    scaled, inverse, normed = normalize(pair, norm_gain, norm_bias)
    projected = jnp.dot(normed.reshape(N * N, C), proj_weight, preferred_element_type=jnp.float32).reshape(N, N, 4 * H)
    block_ids = (jnp.arange(N) // BLK).astype(jnp.int32)
    valid_tile = tile_mask[block_ids][:, block_ids].astype(jnp.float32)[:, :, None]
    lin_left = projected[:, :, 0:H]
    gate_left = projected[:, :, H:2 * H]
    lin_right = projected[:, :, 2 * H:3 * H]
    gate_right = projected[:, :, 3 * H:4 * H]
    sig_left = jax.nn.sigmoid(gate_left)
    sig_right = jax.nn.sigmoid(gate_right)
    left_act = (valid_tile * sig_left * lin_left).astype(jnp.bfloat16)
    right_act = (valid_tile * sig_right * lin_right).astype(jnp.bfloat16)
    grad_wide = grad_x.astype(jnp.float32)
    left_wide = left_act.astype(jnp.float32)
    grad_left = jnp.einsum('ijc,jkc->ikc', grad_wide, right_act.astype(jnp.float32))

    def add_group(group, total):
        grad_rows = lax.dynamic_slice_in_dim(grad_wide, group * TILE_R, TILE_R, 0)
        left_rows = lax.dynamic_slice_in_dim(left_wide, group * TILE_R, TILE_R, 0)
        partial_sum = jnp.einsum('ijc,ikc->jkc', grad_rows, left_rows).astype(jnp.bfloat16)
        partial_sum = lax.optimization_barrier(partial_sum)
        return total + partial_sum.astype(jnp.float32)
    grad_right = lax.fori_loop(0, N_ROW, add_group, jnp.zeros((N, N, H), jnp.float32))
    grad_proj = jnp.concatenate([grad_left * valid_tile * sig_left, grad_left * valid_tile * lin_left * sig_left * (1.0 - sig_left), grad_right * valid_tile * sig_right, grad_right * valid_tile * lin_right * sig_right * (1.0 - sig_right)], axis=-1).astype(jnp.bfloat16)
    grad_normed = jnp.dot(grad_proj.reshape(N * N, 4 * H), proj_weight.T, preferred_element_type=jnp.float32).reshape(N, N, C)
    scaled_grad = grad_normed * norm_gain
    result = inverse * (scaled_grad - lax.optimization_barrier(jnp.mean(scaled_grad, axis=-1, keepdims=True)) - scaled * lax.optimization_barrier(jnp.mean(scaled_grad * scaled, axis=-1, keepdims=True)))
    return result.astype(jnp.bfloat16)
```

```python
import functools

import jax
import jax.numpy as jnp
from jax import lax
from jax.experimental import pallas as pl
from jax.experimental.pallas import tpu as pltpu
from jax.sharding import PartitionSpec as P

BLK = 128
CHUNKS = 2
SUBS = 2
VMEM_LIMIT = 48 * 1024 * 1024


def exchange(value, axis, size, mask):
    return lax.ppermute(value, axis, [(d, d ^ mask) for d in range(size)])


def gather_columns(block, size, order):
    slots = {0: block}
    for bit in order:
        for m in list(slots):
            slots[m | bit] = exchange(slots[m], "col", size, bit)
    return [slots[m] for m in range(size)]


def copy_panel(g_refs, panel, sems, col, subs, slots):
    copies = []
    sub_len, cols = g_refs[0].shape[0], g_refs[0].shape[1]
    for s in range(subs):
        for m in range(slots):
            place = pl.multiple_of(jnp.bitwise_xor(col, m) * cols, cols)
            copies.append(
                pltpu.make_async_copy(
                    g_refs[s * slots + m],
                    panel.at[pl.ds(s * sub_len, sub_len), pl.ds(place, cols), :],
                    sems.at[s * slots + m],
                )
            )
    return copies


def partial_kernel(subs, slots, n, ids, left, *refs):
    g_refs, outs, (panel, sems) = refs[: subs * slots], refs[subs * slots : subs * slots + n], refs[subs * slots + n :]
    row, col = ids[0], ids[1]
    copies = copy_panel(g_refs, panel, sems, col, subs, slots)
    for c in copies:
        c.start()
    for c in copies:
        c.wait()
    rows = left.shape[2]

    def body(c, carry):
        lhs = left[c]
        for s in range(n):
            b = lax.rem(row + s, n)
            rhs = panel[c, pl.ds(pl.multiple_of(b * rows, rows), rows), :]
            out = lax.dot_general(lhs, rhs, (((1,), (1,)), ((), ())), preferred_element_type=jnp.float32)
            outs[s][c] = out.astype(jnp.bfloat16)
        return carry

    lax.fori_loop(0, left.shape[0], body, 0, unroll=4)


def partial_products(ids, left, g_slots, n):
    subs, slots = len(g_slots), len(g_slots[0])
    chans, ks, rows = left.shape
    sub_len, cols, _ = g_slots[0][0].shape
    flat = [g for sub in g_slots for g in sub]
    out = jax.ShapeDtypeStruct((chans, ks, rows), jnp.bfloat16)
    return pl.pallas_call(
        functools.partial(partial_kernel, subs, slots, n),
        out_shape=[out] * n,
        in_specs=[pl.BlockSpec(memory_space=pltpu.SMEM), pl.BlockSpec(memory_space=pltpu.VMEM)]
        + [pl.BlockSpec(memory_space=pl.ANY)] * len(flat),
        out_specs=[pl.BlockSpec(memory_space=pltpu.VMEM)] * n,
        scratch_shapes=[
            pltpu.VMEM((chans, slots * cols, rows), jnp.bfloat16),
            pltpu.SemaphoreType.DMA((len(flat),)),
        ],
        compiler_params=pltpu.CompilerParams(vmem_limit_bytes=VMEM_LIMIT),
        cost_estimate=pl.CostEstimate(
            flops=2 * chans * ks * rows * n * rows, bytes_accessed=2 * chans * rows * (slots * cols + ks * (n + 1)), transcendentals=0
        ),
        name="right_partials",
    )(ids, left, *flat)


def left_kernel(subs, slots, n, ids, own, *refs):
    ups, downs, refs = refs[: n - 1], refs[n - 1 : 2 * n - 2], refs[2 * n - 2 :]
    g_refs, (out, panel, acts, sems, act_sems) = refs[: subs * slots], refs[subs * slots :]
    row, col = ids[0], ids[1]
    copies = copy_panel(g_refs, panel, sems, col, subs, slots)
    for c in copies:
        c.start()
    rows = own.shape[2]

    def place(b):
        return acts.at[:, :, pl.ds(pl.multiple_of(b * rows, rows), rows)]

    moved = [(None, pltpu.make_async_copy(own, place(row), act_sems.at[0]))]
    for h in range(1, n):
        moved.append((row >= h, pltpu.make_async_copy(ups[h - 1], place(jnp.maximum(row - h, 0)), act_sems.at[h])))
        moved.append(
            (row + h < n, pltpu.make_async_copy(downs[h - 1], place(jnp.minimum(row + h, n - 1)), act_sems.at[n - 1 + h]))
        )
    for use, c in moved:
        if use is None:
            c.start()
        else:
            pl.when(use)(c.start)
    for use, c in moved:
        if use is None:
            c.wait()
        else:
            pl.when(use)(c.wait)
    for c in copies:
        c.wait()

    def body(c, carry):
        out[c] = jnp.dot(acts[c], panel[c], preferred_element_type=jnp.float32)
        return carry

    lax.fori_loop(0, out.shape[0], body, 0, unroll=4)


def left_products(ids, own, ups, downs, g_slots, n):
    subs, slots = len(g_slots), len(g_slots[0])
    chans, ks, rows = own.shape
    sub_len, cols, _ = g_slots[0][0].shape
    flat = [g for sub in g_slots for g in sub]
    return pl.pallas_call(
        functools.partial(left_kernel, subs, slots, n),
        out_shape=jax.ShapeDtypeStruct((chans, ks, rows), jnp.float32),
        in_specs=[pl.BlockSpec(memory_space=pltpu.SMEM)] + [pl.BlockSpec(memory_space=pl.ANY)] * (2 * n - 1 + len(flat)),
        out_specs=pl.BlockSpec(memory_space=pltpu.VMEM),
        scratch_shapes=[
            pltpu.VMEM((chans, slots * cols, rows), jnp.bfloat16),
            pltpu.VMEM((chans, ks, n * rows), jnp.bfloat16),
            pltpu.SemaphoreType.DMA((len(flat),)),
            pltpu.SemaphoreType.DMA((2 * n - 1,)),
        ],
        compiler_params=pltpu.CompilerParams(vmem_limit_bytes=VMEM_LIMIT),
        cost_estimate=pl.CostEstimate(
            flops=2 * chans * ks * rows * n * rows, bytes_accessed=2 * chans * rows * (slots * cols + ks * (n + 2)), transcendentals=0
        ),
        name="left_products",
    )(ids, own, *ups, *downs, *flat)


def shards(pair, grad_x, norm_gain, norm_bias, proj_weight, tile_mask):
    row_count, col_count, _ = pair.shape
    hidden = grad_x.shape[2]
    n, n_col = lax.axis_size("row"), lax.axis_size("col")
    row, col = lax.axis_index("row"), lax.axis_index("col")
    ids = jnp.stack([row, col]).astype(jnp.int32)
    part = hidden // CHUNKS
    sub = part // SUBS

    grad_t = jnp.transpose(grad_x, (2, 1, 0))
    bits = [1 << b for b in range(1, n_col.bit_length() - 1)]
    g_slots = []
    for chunk in range(CHUNKS):
        subs = []
        for s in range(SUBS):
            first = chunk * part + s * sub
            turn = s % max(len(bits), 1)
            order = bits[turn:] + bits[:turn] + [1]
            subs.append(gather_columns(grad_t[first : first + sub], n_col, order))
        g_slots.append(subs)

    values = jnp.transpose(pair, (1, 2, 0)).astype(jnp.float32)
    centred = values - jnp.mean(values, axis=1, keepdims=True)
    inverse = lax.rsqrt(jnp.mean(centred * centred, axis=1, keepdims=True) + 1e-05)
    scaled = centred * inverse
    normed = (scaled * norm_gain[None, :, None] + norm_bias[None, :, None]).astype(jnp.bfloat16)
    projected = jnp.einsum("kca,cd->kda", normed, proj_weight, preferred_element_type=jnp.float32)
    row_block = (row * row_count + jnp.arange(row_count, dtype=jnp.int32)) // BLK
    col_block = (col * col_count + jnp.arange(col_count, dtype=jnp.int32)) // BLK
    blocks = jnp.arange(tile_mask.shape[0], dtype=jnp.int32)
    row_onehot = (row_block[:, None] == blocks[None, :]).astype(jnp.float32)
    col_onehot = (col_block[:, None] == blocks[None, :]).astype(jnp.float32)
    valid = jnp.dot(jnp.dot(col_onehot, tile_mask.astype(jnp.float32).T), row_onehot.T)[:, None, :]
    lin_left = projected[:, 0:hidden]
    gate_left = projected[:, hidden : 2 * hidden]
    lin_right = projected[:, 2 * hidden : 3 * hidden]
    gate_right = projected[:, 3 * hidden : 4 * hidden]
    sig_left = jax.nn.sigmoid(gate_left)
    sig_right = jax.nn.sigmoid(gate_right)
    left_act = jnp.transpose((valid * sig_left * lin_left).astype(jnp.bfloat16), (1, 0, 2))
    right_act = jnp.transpose((valid * sig_right * lin_right).astype(jnp.bfloat16), (1, 0, 2))

    lefts, rights = [], []
    for chunk in range(CHUNKS):
        cut = slice(chunk * part, (chunk + 1) * part)
        own = right_act[cut]
        ups, downs = [], []
        up, down = own, own
        for h in range(1, n):
            up = lax.ppermute(up, "row", [(r, r + 1) for r in range(h - 1, n - 1)])
            down = lax.ppermute(down, "row", [(r, r - 1) for r in range(1, n - h + 1)])
            ups.append(up)
            downs.append(down)
        partials = partial_products(ids, left_act[cut], g_slots[chunk], n)
        up = down = None
        for step in range(1, n):
            away = n - step
            up_sum, down_sum = partials[away], partials[n - away]
            if up is not None:
                up_sum = (up_sum.astype(jnp.float32) + up.astype(jnp.float32)).astype(jnp.bfloat16)
                down_sum = (down_sum.astype(jnp.float32) + down.astype(jnp.float32)).astype(jnp.bfloat16)
            up = lax.ppermute(up_sum, "row", [(r, r + 1) for r in range(step)])
            down = lax.ppermute(down_sum, "row", [(r, r - 1) for r in range(n - step, n)])
        rights.append((partials[0], up, down))
        lefts.append(left_products(ids, own, ups, downs, g_slots[chunk], n))

    grad_left = jnp.transpose(jnp.concatenate(lefts, axis=0), (1, 0, 2))
    grad_right = jnp.concatenate(
        [p.astype(jnp.float32) + u.astype(jnp.float32) + d.astype(jnp.float32) for p, u, d in rights], axis=0
    )
    grad_right = jnp.transpose(grad_right, (1, 0, 2))
    grad_proj = jnp.concatenate(
        [
            grad_left * valid * sig_left,
            grad_left * valid * lin_left * sig_left * (1.0 - sig_left),
            grad_right * valid * sig_right,
            grad_right * valid * lin_right * sig_right * (1.0 - sig_right),
        ],
        axis=1,
    ).astype(jnp.bfloat16)
    grad_normed = jnp.einsum("kda,cd->kca", grad_proj, proj_weight, preferred_element_type=jnp.float32)
    scaled_grad = grad_normed * norm_gain[None, :, None]
    result = inverse * (
        scaled_grad
        - jnp.mean(scaled_grad, axis=1, keepdims=True)
        - scaled * jnp.mean(scaled_grad * scaled, axis=1, keepdims=True)
    )
    return jnp.transpose(result.astype(jnp.bfloat16), (2, 0, 1))


def solution(mesh):
    placed = (P("row", "col", None), P("row", "col", None), P(), P(), P(), P())
    return jax.shard_map(
        shards, mesh=mesh, in_specs=placed, out_specs=P("row", "col", None), check_vma=False
    )
```

```python
import functools

import jax
import jax.numpy as jnp
from jax import lax
from jax.experimental import pallas as pl
from jax.experimental.pallas import tpu as pltpu
from jax.sharding import PartitionSpec as P

BLK = 128
CHUNKS = 2
STEP = 8
KEYS = 16
VMEM_LIMIT = 48 * 1024 * 1024
PARAMS = pltpu.CompilerParams(vmem_limit_bytes=VMEM_LIMIT)
BY_LAST = (((1,), (1,)), ((), ()))


def identity(size):
    return (
        lax.broadcasted_iota(jnp.int32, (size, size), 0) == lax.broadcasted_iota(jnp.int32, (size, size), 1)
    ).astype(jnp.bfloat16)


def column(vector_ref, rows):
    return jnp.broadcast_to(vector_ref[...], (rows, vector_ref.shape[1])).T


def unit_mask(mask_ref, rows, cols):
    row, col = lax.axis_index("row"), lax.axis_index("col")
    return mask_ref[(row * rows) // BLK, (col * cols) // BLK].astype(jnp.float32)


def spread(pair_ref, wide):
    rows, keys, chans = pair_ref.shape
    wide[...] = pair_ref[...].astype(jnp.float32).reshape(rows * keys, chans)


def normalize(wide, eye, key, keys, rows):
    cells = wide[pl.ds(key, rows, stride=keys), :].astype(jnp.bfloat16)
    values = lax.dot_general(eye, cells, BY_LAST, preferred_element_type=jnp.float32)
    centred = values - jnp.mean(values, axis=0, keepdims=True)
    inverse = lax.rsqrt(jnp.mean(centred * centred, axis=0, keepdims=True) + 1e-05)
    return centred * inverse, inverse


def front_kernel(mask, pair, gain, bias, weight, *refs):
    outs, (wide, flat, gain_col, bias_col, weight_t) = refs[:CHUNKS], refs[CHUNKS:]
    rows, keys, chans = pair.shape
    hidden = weight.shape[1] // 2
    part = hidden // CHUNKS

    @pl.when(pl.program_id(0) == 0)
    def _():
        gain_col[...] = column(gain, rows)
        bias_col[...] = column(bias, rows)
        weight_t[...] = weight[...].astype(jnp.float32).T.astype(jnp.bfloat16)

    cols = pl.num_programs(0) * keys
    valid = unit_mask(mask, rows, cols)
    eye = identity(chans)
    spread(pair, wide)
    for key in range(keys):
        scaled, _ = normalize(wide, eye, key, keys, rows)
        normed = (scaled * gain_col[...] + bias_col[...]).astype(jnp.bfloat16)
        projected = jnp.dot(weight_t[...], normed, preferred_element_type=jnp.float32)
        flat[pl.ds(key, hidden, stride=keys), :] = valid * jax.nn.sigmoid(projected[hidden:]) * projected[:hidden]
    for chunk in range(CHUNKS):
        outs[chunk][...] = (
            flat[chunk * part * keys : (chunk + 1) * part * keys, :].reshape(part, keys, rows).astype(jnp.bfloat16)
        )


def front(pair, gain, bias, proj_weight, tile_mask, side):
    rows, cols, chans = pair.shape
    width = proj_weight.shape[1] // 2
    part = width // 2 // CHUNKS
    whole = lambda shape: pl.BlockSpec(shape, lambda g: (0, 0))
    return pl.pallas_call(
        front_kernel,
        out_shape=[jax.ShapeDtypeStruct((part, cols, rows), jnp.bfloat16)] * CHUNKS,
        grid=(cols // KEYS,),
        in_specs=[
            pl.BlockSpec(memory_space=pltpu.SMEM),
            pl.BlockSpec((rows, KEYS, chans), lambda g: (0, g, 0)),
            whole((1, chans)),
            whole((1, chans)),
            pl.BlockSpec((chans, width), lambda g: (0, side)),
        ],
        out_specs=[pl.BlockSpec((part, KEYS, rows), lambda g: (0, g, 0))] * CHUNKS,
        scratch_shapes=[
            pltpu.VMEM((rows * KEYS, chans), jnp.float32),
            pltpu.VMEM((width // 2 * KEYS, rows), jnp.float32),
            pltpu.VMEM((chans, rows), jnp.float32),
            pltpu.VMEM((chans, rows), jnp.float32),
            pltpu.VMEM((width, chans), jnp.bfloat16),
        ],
        compiler_params=PARAMS,
        cost_estimate=pl.CostEstimate(
            flops=4 * rows * cols * chans * width, bytes_accessed=6 * rows * cols * chans, transcendentals=rows * cols * width
        ),
        name="left_front" if side == 0 else "right_front",
    )(tile_mask, pair, gain, bias, proj_weight)


def tail_kernel(mask, pair, gain, bias, weight, *refs):
    lefts, refs = refs[:CHUNKS], refs[CHUNKS:]
    rights, refs = refs[: 3 * CHUNKS], refs[3 * CHUNKS :]
    out, wide, right_flat, left_flat, gain_col, bias_col, weight_t = refs
    rows, keys, chans = pair.shape
    hidden = weight.shape[1] // 4
    part = hidden // CHUNKS

    @pl.when(pl.program_id(0) == 0)
    def _():
        gain_col[...] = column(gain, rows)
        bias_col[...] = column(bias, rows)
        weight_t[...] = weight[...].astype(jnp.float32).T.astype(jnp.bfloat16)

    cols = pl.num_programs(0) * keys
    valid = unit_mask(mask, rows, cols)
    eye = identity(chans)
    row_eye = eye if rows == chans else identity(rows)
    spread(pair, wide)
    for chunk in range(CHUNKS):
        own, up, down = (rights[i * CHUNKS + chunk][...].astype(jnp.float32) for i in range(3))
        place = slice(chunk * part * keys, (chunk + 1) * part * keys)
        right_flat[place, :] = (own + up + down).reshape(part * keys, rows)
        left_flat[place, :] = lefts[chunk][...].reshape(part * keys, rows)
    for key in range(keys):
        scaled, inverse = normalize(wide, eye, key, keys, rows)
        normed = (scaled * gain_col[...] + bias_col[...]).astype(jnp.bfloat16)
        projected = jnp.dot(weight_t[...], normed, preferred_element_type=jnp.float32)
        grads = []
        for side, source in enumerate((left_flat, right_flat)):
            lin = projected[2 * side * hidden : (2 * side + 1) * hidden]
            sig = jax.nn.sigmoid(projected[(2 * side + 1) * hidden : (2 * side + 2) * hidden])
            through = source[pl.ds(key, hidden, stride=keys), :] * valid * sig
            grads += [through.astype(jnp.bfloat16), (through * lin * (1.0 - sig)).astype(jnp.bfloat16)]
        grad_normed = jnp.dot(weight[...], jnp.concatenate(grads, axis=0), preferred_element_type=jnp.float32)
        scaled_grad = grad_normed * gain_col[...]
        result = inverse * (
            scaled_grad
            - jnp.mean(scaled_grad, axis=0, keepdims=True)
            - scaled * jnp.mean(scaled_grad * scaled, axis=0, keepdims=True)
        )
        wide[pl.ds(key, rows, stride=keys), :] = lax.dot_general(
            row_eye, result.astype(jnp.bfloat16), BY_LAST, preferred_element_type=jnp.float32
        )
    out[...] = wide[...].reshape(rows, keys, chans).astype(jnp.bfloat16)


def tail(pair, gain, bias, proj_weight, tile_mask, lefts, rights):
    rows, cols, chans = pair.shape
    width = proj_weight.shape[1]
    part = width // 4 // CHUNKS
    whole = lambda shape: pl.BlockSpec(shape, lambda g: (0, 0))
    cells = pl.BlockSpec((rows, KEYS, chans), lambda g: (0, g, 0))
    small = pl.BlockSpec((part, KEYS, rows), lambda g: (0, g, 0))
    return pl.pallas_call(
        tail_kernel,
        out_shape=jax.ShapeDtypeStruct(pair.shape, jnp.bfloat16),
        grid=(cols // KEYS,),
        in_specs=[
            pl.BlockSpec(memory_space=pltpu.SMEM),
            cells,
            whole((1, chans)),
            whole((1, chans)),
            whole((chans, width)),
        ]
        + [small] * (4 * CHUNKS),
        out_specs=cells,
        scratch_shapes=[
            pltpu.VMEM((rows * KEYS, chans), jnp.float32),
            pltpu.VMEM((width // 4 * KEYS, rows), jnp.float32),
            pltpu.VMEM((width // 4 * KEYS, rows), jnp.float32),
            pltpu.VMEM((chans, rows), jnp.float32),
            pltpu.VMEM((chans, rows), jnp.float32),
            pltpu.VMEM((width, chans), jnp.bfloat16),
        ],
        compiler_params=PARAMS,
        cost_estimate=pl.CostEstimate(
            flops=8 * rows * cols * chans * width, bytes_accessed=10 * rows * cols * chans, transcendentals=rows * cols * width
        ),
        name="tail",
    )(tile_mask, pair, gain, bias, proj_weight, *lefts, *rights)


def column_devices(n_col):
    return [m for m in range(0, n_col, 2)] + [m for m in range(1, n_col, 2)]


def gather_columns(block, n_col):
    def exchange(value, mask):
        return lax.ppermute(value, "col", [(d, d ^ mask) for d in range(n_col)])

    same = [block] + [exchange(block, m) for m in range(2, n_col, 2)]
    return same + [exchange(value, 1) for value in same]


def load_panel(blocks, panel, sems, first, chans, masks):
    col = lax.axis_index("col")
    cols = blocks[0].shape[1]
    copies = []
    for p, m in enumerate(masks):
        place = pl.multiple_of(jnp.bitwise_xor(col, m) * cols, cols)
        copies.append(
            pltpu.make_async_copy(
                blocks[p].at[pl.ds(first, chans)], panel.at[pl.ds(first, chans), pl.ds(place, cols), :], sems.at[p]
            )
        )
    return copies


def fill_panel(blocks, panel, sems, masks):
    steps = pl.num_programs(0)
    step = pl.program_id(0)
    total = panel.shape[0] // STEP

    @pl.when(step == 0)
    def _():
        for g in range(total):
            for c in load_panel(blocks, panel, sems.at[g], g * STEP, STEP, masks):
                c.start()

    for c in load_panel(blocks, panel, sems.at[step], pl.multiple_of(step * STEP, STEP), STEP, masks):
        c.wait()
    del steps


def partial_kernel(n, masks, left, *refs):
    blocks, refs = refs[: len(masks)], refs[len(masks) :]
    outs, (panel, sems) = refs[:n], refs[n:]
    fill_panel(blocks, panel, sems, masks)
    row = lax.axis_index("row")
    rows = left.shape[2]
    first = pl.program_id(0) * STEP
    for c in range(STEP):
        lhs = left[c]
        for s in range(n):
            b = lax.rem(row + s, n)
            rhs = panel[first + c, pl.ds(pl.multiple_of(b * rows, rows), rows), :]
            outs[s][c] = lax.dot_general(lhs, rhs, BY_LAST, preferred_element_type=jnp.float32).astype(jnp.bfloat16)


def partial_products(left, blocks, n):
    chans, ks, rows = left.shape
    masks = column_devices(len(blocks))
    total = len(blocks) * blocks[0].shape[1]
    small = pl.BlockSpec((STEP, ks, rows), lambda g: (g, 0, 0))
    return pl.pallas_call(
        functools.partial(partial_kernel, n, masks),
        out_shape=[jax.ShapeDtypeStruct((chans, ks, rows), jnp.bfloat16)] * n,
        grid=(chans // STEP,),
        in_specs=[small] + [pl.BlockSpec(memory_space=pl.ANY)] * len(masks),
        out_specs=[small] * n,
        scratch_shapes=[
            pltpu.VMEM((chans, total, rows), jnp.bfloat16),
            pltpu.SemaphoreType.DMA((chans // STEP, len(masks))),
        ],
        compiler_params=PARAMS,
        cost_estimate=pl.CostEstimate(
            flops=2 * chans * ks * rows * total, bytes_accessed=2 * chans * rows * (total + ks * (n + 1)), transcendentals=0
        ),
        name="right_partials",
    )(left, *blocks)


def left_kernel(n, masks, own, *refs):
    ups, downs, refs = refs[: n - 1], refs[n - 1 : 2 * n - 2], refs[2 * n - 2 :]
    blocks, (out, panel, sems) = refs[: len(masks)], refs[len(masks) :]
    fill_panel(blocks, panel, sems, masks)
    row = lax.axis_index("row")
    rows = own.shape[2]
    first = pl.program_id(0) * STEP
    for c in range(STEP):
        acts, grads = [], []
        for s in range(n):
            b = lax.rem(row + s, n)
            grads.append(panel[first + c, pl.ds(pl.multiple_of(b * rows, rows), rows), :])
            acts.append(own[c] if s == 0 else jnp.where(row + s < n, downs[s - 1][c], ups[n - s - 1][c]))
        out[c] = jnp.dot(
            jnp.concatenate(acts, axis=1), jnp.concatenate(grads, axis=0), preferred_element_type=jnp.float32
        )


def left_products(own, ups, downs, blocks, n):
    chans, ks, rows = own.shape
    masks = column_devices(len(blocks))
    total = len(blocks) * blocks[0].shape[1]
    small = pl.BlockSpec((STEP, ks, rows), lambda g: (g, 0, 0))
    return pl.pallas_call(
        functools.partial(left_kernel, n, masks),
        out_shape=jax.ShapeDtypeStruct((chans, ks, rows), jnp.float32),
        grid=(chans // STEP,),
        in_specs=[small] * (2 * n - 1) + [pl.BlockSpec(memory_space=pl.ANY)] * len(masks),
        out_specs=small,
        scratch_shapes=[
            pltpu.VMEM((chans, total, rows), jnp.bfloat16),
            pltpu.SemaphoreType.DMA((chans // STEP, len(masks))),
        ],
        compiler_params=PARAMS,
        cost_estimate=pl.CostEstimate(
            flops=2 * chans * ks * rows * total, bytes_accessed=2 * chans * rows * (total + ks * (n + 2)), transcendentals=0
        ),
        name="left_products",
    )(own, *ups, *downs, *blocks)


def shards(pair, grad_x, norm_gain, norm_bias, proj_weight, tile_mask):
    hidden = grad_x.shape[2]
    n, n_col = lax.axis_size("row"), lax.axis_size("col")
    part = hidden // CHUNKS
    gain, bias = norm_gain[None, :], norm_bias[None, :]

    grad_t = jnp.transpose(grad_x, (2, 1, 0))
    blocks = [gather_columns(grad_t[chunk * part : (chunk + 1) * part], n_col) for chunk in range(CHUNKS)]

    owns = front(pair, gain, bias, proj_weight, tile_mask, 1)
    left_acts = front(pair, gain, bias, proj_weight, tile_mask, 0)

    ups, downs = [], []
    for own in owns:
        up_list, down_list = [], []
        up, down = own, own
        for h in range(1, n):
            up = lax.ppermute(up, "row", [(r, r + 1) for r in range(h - 1, n - 1)])
            down = lax.ppermute(down, "row", [(r, r - 1) for r in range(1, n - h + 1)])
            up_list.append(up)
            down_list.append(down)
        ups.append(up_list)
        downs.append(down_list)

    partials, up_sums, down_sums, firsts = [], [], [], []
    for chunk in range(CHUNKS):
        sums = partial_products(left_acts[chunk], blocks[chunk], n)
        up = down = None
        for step in range(1, n):
            away = n - step
            up_sum, down_sum = sums[away], sums[n - away]
            if up is not None:
                up_sum = (up_sum.astype(jnp.float32) + up.astype(jnp.float32)).astype(jnp.bfloat16)
                down_sum = (down_sum.astype(jnp.float32) + down.astype(jnp.float32)).astype(jnp.bfloat16)
            up = lax.ppermute(up_sum, "row", [(r, r + 1) for r in range(step)])
            down = lax.ppermute(down_sum, "row", [(r, r - 1) for r in range(n - step, n)])
            if step == 1:
                firsts.append(up)
        partials.append(sums[0])
        up_sums.append(up)
        down_sums.append(down)

    lefts = []
    for chunk in range(CHUNKS):
        own, _ = lax.optimization_barrier((owns[chunk], firsts[chunk]))
        lefts.append(left_products(own, ups[chunk], downs[chunk], blocks[chunk], n))

    return tail(pair, gain, bias, proj_weight, tile_mask, lefts, partials + up_sums + down_sums)


def solution(mesh):
    placed = (P("row", "col", None), P("row", "col", None), P(), P(), P(), P())
    return jax.shard_map(
        shards, mesh=mesh, in_specs=placed, out_specs=P("row", "col", None), check_vma=False
    )
```

```python
import functools

import jax
import jax.numpy as jnp
from jax import lax
from jax.experimental import pallas as pl
from jax.experimental.pallas import tpu as pltpu
from jax.sharding import PartitionSpec as P

BLK = 128
CHUNKS = 2
STEP = 8
KEYS = 16
VMEM_LIMIT = 48 * 1024 * 1024
PARAMS = pltpu.CompilerParams(vmem_limit_bytes=VMEM_LIMIT)
BY_LAST = (((1,), (1,)), ((), ()))


def identity(size):
    return (
        lax.broadcasted_iota(jnp.int32, (size, size), 0) == lax.broadcasted_iota(jnp.int32, (size, size), 1)
    ).astype(jnp.bfloat16)


def column(vector_ref, rows):
    return jnp.broadcast_to(vector_ref[...], (rows, vector_ref.shape[1])).T


def unit_mask(mask_ref, rows, cols):
    row, col = lax.axis_index("row"), lax.axis_index("col")
    return mask_ref[(row * rows) // BLK, (col * cols) // BLK].astype(jnp.float32)


def turn(pair, flipped, turned):
    flipped[...] = jnp.transpose(pair[...], (1, 0, 2))
    eye = identity(pair.shape[2])
    for key in range(pair.shape[1]):
        turned[key] = lax.dot_general(eye, flipped[key], BY_LAST, preferred_element_type=jnp.float32)


def normalize(values):
    centred = values - jnp.mean(values, axis=1, keepdims=True)
    inverse = lax.rsqrt(jnp.mean(centred * centred, axis=1, keepdims=True) + 1e-05)
    return centred * inverse, inverse


def set_columns(gain, bias, weight, gain_col, bias_col, weight_t):
    @pl.when(pl.program_id(0) == 0)
    def _():
        gain_col[...] = column(gain, gain_col.shape[1])
        bias_col[...] = column(bias, bias_col.shape[1])
        weight_t[...] = weight[...].astype(jnp.float32).T.astype(jnp.bfloat16)


def front_kernel(mask, pair, gain, bias, weight, *refs):
    outs, (flipped, turned, normed, acts, gain_col, bias_col, weight_t) = refs[:CHUNKS], refs[CHUNKS:]
    rows, keys, _ = pair.shape
    hidden = weight.shape[1] // 2
    part = hidden // CHUNKS
    set_columns(gain, bias, weight, gain_col, bias_col, weight_t)
    valid = unit_mask(mask, rows, pl.num_programs(0) * keys)
    turn(pair, flipped, turned)
    scaled, _ = normalize(turned[...])
    normed[...] = (scaled * gain_col[...] + bias_col[...]).astype(jnp.bfloat16)
    for key in range(keys):
        projected = jnp.dot(weight_t[...], normed[key], preferred_element_type=jnp.float32)
        acts[key] = (valid * jax.nn.sigmoid(projected[hidden:]) * projected[:hidden]).astype(jnp.bfloat16)
    whole = jnp.transpose(acts[...], (1, 0, 2))
    for chunk in range(CHUNKS):
        outs[chunk][...] = whole[chunk * part : (chunk + 1) * part]


def front(pair, gain, bias, proj_weight, tile_mask, side):
    rows, cols, chans = pair.shape
    width = proj_weight.shape[1] // 2
    part = width // 2 // CHUNKS
    whole = lambda shape: pl.BlockSpec(shape, lambda g: (0, 0))
    return pl.pallas_call(
        front_kernel,
        out_shape=[jax.ShapeDtypeStruct((part, cols, rows), jnp.bfloat16)] * CHUNKS,
        grid=(cols // KEYS,),
        in_specs=[
            pl.BlockSpec(memory_space=pltpu.SMEM),
            pl.BlockSpec((rows, KEYS, chans), lambda g: (0, g, 0)),
            whole((1, chans)),
            whole((1, chans)),
            pl.BlockSpec((chans, width), lambda g: (0, side)),
        ],
        out_specs=[pl.BlockSpec((part, KEYS, rows), lambda g: (0, g, 0))] * CHUNKS,
        scratch_shapes=[
            pltpu.VMEM((KEYS, rows, chans), jnp.bfloat16),
            pltpu.VMEM((KEYS, chans, rows), jnp.float32),
            pltpu.VMEM((KEYS, chans, rows), jnp.bfloat16),
            pltpu.VMEM((KEYS, width // 2, rows), jnp.bfloat16),
            pltpu.VMEM((chans, rows), jnp.float32),
            pltpu.VMEM((chans, rows), jnp.float32),
            pltpu.VMEM((width, chans), jnp.bfloat16),
        ],
        compiler_params=PARAMS,
        cost_estimate=pl.CostEstimate(
            flops=4 * rows * cols * chans * width, bytes_accessed=6 * rows * cols * chans, transcendentals=rows * cols * width
        ),
        name="left_front" if side == 0 else "right_front",
    )(tile_mask, pair, gain, bias, proj_weight)


def tail_kernel(mask, pair, gain, bias, weight, *refs):
    lefts, refs = refs[:CHUNKS], refs[CHUNKS:]
    rights, refs = refs[: 3 * CHUNKS], refs[3 * CHUNKS :]
    out, flipped, turned, normed, inverses, grads, right_flat, left_flat, gain_col, bias_col, weight_t = refs
    rows, keys, _ = pair.shape
    hidden = weight.shape[1] // 4
    part = hidden // CHUNKS
    set_columns(gain, bias, weight, gain_col, bias_col, weight_t)
    valid = unit_mask(mask, rows, pl.num_programs(0) * keys)
    for chunk in range(CHUNKS):
        own, up, down = (rights[i * CHUNKS + chunk][...].astype(jnp.float32) for i in range(3))
        place = slice(chunk * part * keys, (chunk + 1) * part * keys)
        right_flat[place, :] = (own + up + down).reshape(part * keys, rows)
        left_flat[place, :] = lefts[chunk][...].reshape(part * keys, rows)
    turn(pair, flipped, turned)
    scaled, inverse = normalize(turned[...])
    turned[...] = scaled
    inverses[...] = inverse
    normed[...] = (scaled * gain_col[...] + bias_col[...]).astype(jnp.bfloat16)
    for key in range(keys):
        projected = jnp.dot(weight_t[...], normed[key], preferred_element_type=jnp.float32)
        for side, source in enumerate((left_flat, right_flat)):
            lin = projected[2 * side * hidden : (2 * side + 1) * hidden]
            sig = jax.nn.sigmoid(projected[(2 * side + 1) * hidden : (2 * side + 2) * hidden])
            through = source[pl.ds(key, hidden, stride=keys), :] * valid * sig
            grads[key, 2 * side * hidden : (2 * side + 1) * hidden, :] = through.astype(jnp.bfloat16)
            grads[key, (2 * side + 1) * hidden : (2 * side + 2) * hidden, :] = (through * lin * (1.0 - sig)).astype(
                jnp.bfloat16
            )
    for key in range(keys):
        scaled = turned[key]
        scaled_grad = jnp.dot(weight[...], grads[key], preferred_element_type=jnp.float32) * gain_col[...]
        result = inverses[key] * (
            scaled_grad
            - jnp.mean(scaled_grad, axis=0, keepdims=True)
            - scaled * jnp.mean(scaled_grad * scaled, axis=0, keepdims=True)
        )
        normed[key] = result.astype(jnp.bfloat16)
    eye = identity(rows)
    for key in range(keys):
        flipped[key] = lax.dot_general(eye, normed[key], BY_LAST, preferred_element_type=jnp.float32).astype(jnp.bfloat16)
    out[...] = jnp.transpose(flipped[...], (1, 0, 2))


def tail(pair, gain, bias, proj_weight, tile_mask, lefts, rights):
    rows, cols, chans = pair.shape
    width = proj_weight.shape[1]
    part = width // 4 // CHUNKS
    whole = lambda shape: pl.BlockSpec(shape, lambda g: (0, 0))
    cells = pl.BlockSpec((rows, KEYS, chans), lambda g: (0, g, 0))
    small = pl.BlockSpec((part, KEYS, rows), lambda g: (0, g, 0))
    return pl.pallas_call(
        tail_kernel,
        out_shape=jax.ShapeDtypeStruct(pair.shape, jnp.bfloat16),
        grid=(cols // KEYS,),
        in_specs=[
            pl.BlockSpec(memory_space=pltpu.SMEM),
            cells,
            whole((1, chans)),
            whole((1, chans)),
            whole((chans, width)),
        ]
        + [small] * (4 * CHUNKS),
        out_specs=cells,
        scratch_shapes=[
            pltpu.VMEM((KEYS, rows, chans), jnp.bfloat16),
            pltpu.VMEM((KEYS, chans, rows), jnp.float32),
            pltpu.VMEM((KEYS, chans, rows), jnp.bfloat16),
            pltpu.VMEM((KEYS, 1, rows), jnp.float32),
            pltpu.VMEM((KEYS, width, rows), jnp.bfloat16),
            pltpu.VMEM((width // 4 * KEYS, rows), jnp.float32),
            pltpu.VMEM((width // 4 * KEYS, rows), jnp.float32),
            pltpu.VMEM((chans, rows), jnp.float32),
            pltpu.VMEM((chans, rows), jnp.float32),
            pltpu.VMEM((width, chans), jnp.bfloat16),
        ],
        compiler_params=PARAMS,
        cost_estimate=pl.CostEstimate(
            flops=8 * rows * cols * chans * width, bytes_accessed=10 * rows * cols * chans, transcendentals=rows * cols * width
        ),
        name="tail",
    )(tile_mask, pair, gain, bias, proj_weight, *lefts, *rights)


def column_devices(n_col):
    return [m for m in range(0, n_col, 2)] + [m for m in range(1, n_col, 2)]


def exchange(value, mask, n_col):
    return lax.ppermute(value, "col", [(d, d ^ mask) for d in range(n_col)])


def gather_columns(block, n_col):
    return [block] + [exchange(block, m, n_col) for m in range(2, n_col, 2)]


def load_panel(blocks, panel, sems, first, chans, masks):
    col = lax.axis_index("col")
    cols = blocks[0].shape[1]
    copies = []
    for p, m in enumerate(masks):
        place = pl.multiple_of(jnp.bitwise_xor(col, m) * cols, cols)
        copies.append(
            pltpu.make_async_copy(
                blocks[p].at[pl.ds(first, chans)], panel.at[pl.ds(first, chans), pl.ds(place, cols), :], sems.at[p]
            )
        )
    return copies


def fill_panel(blocks, panel, sems, masks):
    step = pl.program_id(0)
    total = panel.shape[0] // STEP

    @pl.when(step == 0)
    def _():
        for g in range(total):
            for c in load_panel(blocks, panel, sems.at[g], g * STEP, STEP, masks):
                c.start()

    for c in load_panel(blocks, panel, sems.at[step], pl.multiple_of(step * STEP, STEP), STEP, masks):
        c.wait()


def partial_kernel(n, masks, left, *refs):
    blocks, refs = refs[: len(masks)], refs[len(masks) :]
    outs, (panel, sems) = refs[:n], refs[n:]
    fill_panel(blocks, panel, sems, masks)
    row = lax.axis_index("row")
    rows = left.shape[2]
    first = pl.program_id(0) * STEP
    for c in range(STEP):
        lhs = left[c]
        for s in range(n):
            b = lax.rem(row + s, n)
            rhs = panel[first + c, pl.ds(pl.multiple_of(b * rows, rows), rows), :]
            outs[s][c] = lax.dot_general(lhs, rhs, BY_LAST, preferred_element_type=jnp.float32).astype(jnp.bfloat16)


def partial_products(left, blocks, n):
    chans, ks, rows = left.shape
    masks = column_devices(len(blocks))
    total = len(blocks) * blocks[0].shape[1]
    small = pl.BlockSpec((STEP, ks, rows), lambda g: (g, 0, 0))
    return pl.pallas_call(
        functools.partial(partial_kernel, n, masks),
        out_shape=[jax.ShapeDtypeStruct((chans, ks, rows), jnp.bfloat16)] * n,
        grid=(chans // STEP,),
        in_specs=[small] + [pl.BlockSpec(memory_space=pl.ANY)] * len(masks),
        out_specs=[small] * n,
        scratch_shapes=[
            pltpu.VMEM((chans, total, rows), jnp.bfloat16),
            pltpu.SemaphoreType.DMA((chans // STEP, len(masks))),
        ],
        compiler_params=PARAMS,
        cost_estimate=pl.CostEstimate(
            flops=2 * chans * ks * rows * total, bytes_accessed=2 * chans * rows * (total + ks * (n + 1)), transcendentals=0
        ),
        name="right_partials",
    )(left, *blocks)


def left_kernel(n, masks, own, *refs):
    ups, downs, refs = refs[: n - 1], refs[n - 1 : 2 * n - 2], refs[2 * n - 2 :]
    blocks, (out, panel, sems) = refs[: len(masks)], refs[len(masks) :]
    fill_panel(blocks, panel, sems, masks)
    row = lax.axis_index("row")
    rows = own.shape[2]
    first = pl.program_id(0) * STEP
    for c in range(STEP):
        acts, grads = [], []
        for s in range(n):
            b = lax.rem(row + s, n)
            grads.append(panel[first + c, pl.ds(pl.multiple_of(b * rows, rows), rows), :])
            acts.append(own[c] if s == 0 else jnp.where(row + s < n, downs[s - 1][c], ups[n - s - 1][c]))
        out[c] = jnp.dot(
            jnp.concatenate(acts, axis=1), jnp.concatenate(grads, axis=0), preferred_element_type=jnp.float32
        )


def left_products(own, ups, downs, blocks, n):
    chans, ks, rows = own.shape
    masks = column_devices(len(blocks))
    total = len(blocks) * blocks[0].shape[1]
    small = pl.BlockSpec((STEP, ks, rows), lambda g: (g, 0, 0))
    return pl.pallas_call(
        functools.partial(left_kernel, n, masks),
        out_shape=jax.ShapeDtypeStruct((chans, ks, rows), jnp.float32),
        grid=(chans // STEP,),
        in_specs=[small] * (2 * n - 1) + [pl.BlockSpec(memory_space=pl.ANY)] * len(masks),
        out_specs=small,
        scratch_shapes=[
            pltpu.VMEM((chans, total, rows), jnp.bfloat16),
            pltpu.SemaphoreType.DMA((chans // STEP, len(masks))),
        ],
        compiler_params=PARAMS,
        cost_estimate=pl.CostEstimate(
            flops=2 * chans * ks * rows * total, bytes_accessed=2 * chans * rows * (total + ks * (n + 2)), transcendentals=0
        ),
        name="left_products",
    )(own, *ups, *downs, *blocks)


def shards(pair, grad_x, norm_gain, norm_bias, proj_weight, tile_mask):
    hidden = grad_x.shape[2]
    n, n_col = lax.axis_size("row"), lax.axis_size("col")
    part = hidden // CHUNKS
    gain, bias = norm_gain[None, :], norm_bias[None, :]

    grad_t = jnp.transpose(grad_x, (2, 1, 0))
    same_core = [gather_columns(grad_t[chunk * part : (chunk + 1) * part], n_col) for chunk in range(CHUNKS)]
    owns = front(pair, gain, bias, proj_weight, tile_mask, 1)
    left_acts = front(pair, gain, bias, proj_weight, tile_mask, 0)
    blocks = []
    for same in same_core:
        same, _, _ = lax.optimization_barrier((same, owns, left_acts))
        blocks.append(same + [exchange(value, 1, n_col) for value in same])

    ups, downs = [], []
    for own in owns:
        up_list, down_list = [], []
        up, down = own, own
        for h in range(1, n):
            up = lax.ppermute(up, "row", [(r, r + 1) for r in range(h - 1, n - 1)])
            down = lax.ppermute(down, "row", [(r, r - 1) for r in range(1, n - h + 1)])
            up_list.append(up)
            down_list.append(down)
        ups.append(up_list)
        downs.append(down_list)

    partials, up_sums, down_sums, firsts = [], [], [], []
    for chunk in range(CHUNKS):
        left_act, _ = lax.optimization_barrier((left_acts[chunk], (ups[chunk][0], downs[chunk][0])))
        sums = partial_products(left_act, blocks[chunk], n)
        up = down = None
        for step in range(1, n):
            away = n - step
            up_sum, down_sum = sums[away], sums[n - away]
            if up is not None:
                up_sum = (up_sum.astype(jnp.float32) + up.astype(jnp.float32)).astype(jnp.bfloat16)
                down_sum = (down_sum.astype(jnp.float32) + down.astype(jnp.float32)).astype(jnp.bfloat16)
            up = lax.ppermute(up_sum, "row", [(r, r + 1) for r in range(step)])
            down = lax.ppermute(down_sum, "row", [(r, r - 1) for r in range(n - step, n)])
            if step == 1:
                firsts.append(up)
        partials.append(sums[0])
        up_sums.append(up)
        down_sums.append(down)

    lefts = []
    for chunk in range(CHUNKS):
        own, _ = lax.optimization_barrier((owns[chunk], firsts[chunk]))
        lefts.append(left_products(own, ups[chunk], downs[chunk], blocks[chunk], n))

    return tail(pair, gain, bias, proj_weight, tile_mask, lefts, partials + up_sums + down_sums)


def solution(mesh):
    placed = (P("row", "col", None), P("row", "col", None), P(), P(), P(), P())
    return jax.shard_map(
        shards, mesh=mesh, in_specs=placed, out_specs=P("row", "col", None), check_vma=False
    )
```

```python
import functools

import jax
import jax.numpy as jnp
from jax import lax
from jax.experimental import pallas as pl
from jax.experimental.pallas import tpu as pltpu
from jax.sharding import PartitionSpec as P

BLK = 128
CHUNKS = 2
STEP = 8
KEYS = 16
CORES = 2
VMEM_LIMIT = 48 * 1024 * 1024
PARAMS = pltpu.CompilerParams(vmem_limit_bytes=VMEM_LIMIT)
BY_LAST = (((1,), (1,)), ((), ()))


def identity(size):
    return (
        lax.broadcasted_iota(jnp.int32, (size, size), 0) == lax.broadcasted_iota(jnp.int32, (size, size), 1)
    ).astype(jnp.bfloat16)


def column(vector_ref, rows):
    return jnp.broadcast_to(vector_ref[...], (rows, vector_ref.shape[1])).T


def unit_mask(mask_ref, rows, cols):
    row, col = lax.axis_index("row"), lax.axis_index("col")
    return mask_ref[(row * rows) // BLK, (col * cols) // BLK].astype(jnp.float32)


def this_core():
    return lax.rem(lax.axis_index("col"), CORES)


def turn(pair, flipped, turned):
    flipped[...] = jnp.transpose(pair[...], (1, 0, 2))
    eye = identity(pair.shape[2])
    for key in range(pair.shape[1]):
        turned[key] = lax.dot_general(eye, flipped[key], BY_LAST, preferred_element_type=jnp.float32)


def normalize(values):
    centred = values - jnp.mean(values, axis=1, keepdims=True)
    inverse = lax.rsqrt(jnp.mean(centred * centred, axis=1, keepdims=True) + 1e-05)
    return centred * inverse, inverse


def set_columns(gain, bias, weight, gain_col, bias_col, weight_t):
    @pl.when(pl.program_id(0) == 0)
    def _():
        gain_col[...] = column(gain, gain_col.shape[1])
        bias_col[...] = column(bias, bias_col.shape[1])
        weight_t[...] = weight[...].astype(jnp.float32).T.astype(jnp.bfloat16)


def front_kernel(mask, pair, gain, bias, weight, mine, theirs, flipped, turned, normed, acts, whole, gain_col, bias_col, weight_t):
    rows, keys, _ = pair.shape
    hidden = weight.shape[1] // 2
    half = hidden // CORES
    set_columns(gain, bias, weight, gain_col, bias_col, weight_t)
    valid = unit_mask(mask, rows, pl.num_programs(0) * keys)
    turn(pair, flipped, turned)
    scaled, _ = normalize(turned[...])
    normed[...] = (scaled * gain_col[...] + bias_col[...]).astype(jnp.bfloat16)
    for key in range(keys):
        projected = jnp.dot(weight_t[...], normed[key], preferred_element_type=jnp.float32)
        acts[key] = (valid * jax.nn.sigmoid(projected[hidden:]) * projected[:hidden]).astype(jnp.bfloat16)
    whole[...] = jnp.transpose(acts[...], (1, 0, 2))
    core = this_core()
    mine[...] = whole[pl.ds(core * half, half)]
    theirs[...] = whole[pl.ds((1 - core) * half, half)]


def front(pair, gain, bias, proj_weight, tile_mask, side):
    rows, cols, chans = pair.shape
    width = proj_weight.shape[1] // 2
    half = width // 2 // CORES
    vector = pl.BlockSpec((1, chans), lambda g: (0, 0))
    return pl.pallas_call(
        front_kernel,
        out_shape=[jax.ShapeDtypeStruct((half, cols, rows), jnp.bfloat16)] * 2,
        grid=(cols // KEYS,),
        in_specs=[
            pl.BlockSpec(memory_space=pltpu.SMEM),
            pl.BlockSpec((rows, KEYS, chans), lambda g: (0, g, 0)),
            vector,
            vector,
            pl.BlockSpec((chans, width), lambda g: (0, side)),
        ],
        out_specs=[pl.BlockSpec((half, KEYS, rows), lambda g: (0, g, 0))] * 2,
        scratch_shapes=[
            pltpu.VMEM((KEYS, rows, chans), jnp.bfloat16),
            pltpu.VMEM((KEYS, chans, rows), jnp.float32),
            pltpu.VMEM((KEYS, chans, rows), jnp.bfloat16),
            pltpu.VMEM((KEYS, width // 2, rows), jnp.bfloat16),
            pltpu.VMEM((width // 2, KEYS, rows), jnp.bfloat16),
            pltpu.VMEM((chans, rows), jnp.float32),
            pltpu.VMEM((chans, rows), jnp.float32),
            pltpu.VMEM((width, chans), jnp.bfloat16),
        ],
        compiler_params=PARAMS,
        cost_estimate=pl.CostEstimate(
            flops=4 * rows * cols * chans * width, bytes_accessed=6 * rows * cols * chans, transcendentals=rows * cols * width
        ),
        name="left_front" if side == 0 else "right_front",
    )(tile_mask, pair, gain, bias, proj_weight)


def pack_kernel(own, other, *outs):
    cols, half, _ = other.shape
    part = half // len(outs)
    core = this_core()
    for block, place in ((own[:, pl.ds(pl.multiple_of(core * half, half), half), :], core), (other[...], 1 - core)):
        block = jnp.transpose(block, (1, 0, 2))
        for chunk, out in enumerate(outs):
            out[:, pl.ds(pl.multiple_of(place * cols, cols), cols), :] = block[chunk * part : (chunk + 1) * part]


def pack(own, other):
    cols, half, rows = other.shape
    return pl.pallas_call(
        pack_kernel,
        out_shape=[jax.ShapeDtypeStruct((half // CHUNKS, CORES * cols, rows), jnp.bfloat16)] * CHUNKS,
        compiler_params=PARAMS,
        cost_estimate=pl.CostEstimate(flops=0, bytes_accessed=10 * cols * half * rows, transcendentals=0),
        name="pack",
    )(own, other)


def partial_kernel(left_mine, left_other, *refs):
    blocks, out = refs[:-1], refs[-1]
    n = out.shape[0]
    row, chip = lax.axis_index("row"), lax.axis_index("col") // CORES
    for c in range(STEP):
        lhs = jnp.concatenate((left_mine[c], left_other[c]), axis=0)
        for m, block in enumerate(blocks):
            away = lax.rem(jnp.bitwise_xor(chip, m) - row + n, n)
            out[away, c] = lax.dot_general(lhs, block[c], BY_LAST, preferred_element_type=jnp.float32).astype(jnp.bfloat16)


def partial_products(left_mine, left_other, blocks, chunk):
    chans, rows, _ = blocks[0].shape
    ks = left_mine.shape[1]
    n = len(blocks)
    first = chunk * chans // STEP
    left = pl.BlockSpec((STEP, ks, rows), lambda g: (first + g, 0, 0))
    return pl.pallas_call(
        partial_kernel,
        out_shape=jax.ShapeDtypeStruct((n, chans, CORES * ks, rows), jnp.bfloat16),
        grid=(chans // STEP,),
        in_specs=[left, left] + [pl.BlockSpec((STEP, rows, rows), lambda g: (g, 0, 0))] * n,
        out_specs=pl.BlockSpec((n, STEP, CORES * ks, rows), lambda g: (0, g, 0, 0)),
        compiler_params=PARAMS,
        cost_estimate=pl.CostEstimate(
            flops=4 * chans * ks * rows * n * rows, bytes_accessed=2 * chans * rows * (n * rows + 2 * ks * (n + 1)), transcendentals=0
        ),
        name="right_partials",
    )(left_mine, left_other, *blocks)


def left_kernel(n, own, *refs):
    ups, downs, refs = refs[: n - 1], refs[n - 1 : 2 * n - 2], refs[2 * n - 2 :]
    blocks, (mine, theirs, panel) = refs[:n], refs[n:]
    row, chip = lax.axis_index("row"), lax.axis_index("col") // CORES
    ks = mine.shape[1]
    for c in range(STEP):
        for m, block in enumerate(blocks):
            panel[c, jnp.bitwise_xor(chip, m)] = block[c]
        acts, grads = [], []
        for s in range(n):
            grads.append(panel[c, lax.rem(row + s, n)])
            acts.append(own[c] if s == 0 else jnp.where(row + s < n, downs[s - 1][c], ups[n - s - 1][c]))
        out = jnp.dot(
            jnp.concatenate(acts, axis=1), jnp.concatenate(grads, axis=0), preferred_element_type=jnp.float32
        )
        mine[c] = out[:ks]
        theirs[c] = out[ks:].astype(jnp.bfloat16)


def left_products(own, ups, downs, blocks):
    chans, ks, rows = own.shape
    n = len(blocks)
    act = pl.BlockSpec((STEP, ks, rows), lambda g: (g, 0, 0))
    out = pl.BlockSpec((STEP, ks // CORES, rows), lambda g: (g, 0, 0))
    return pl.pallas_call(
        functools.partial(left_kernel, n),
        out_shape=[
            jax.ShapeDtypeStruct((chans, ks // CORES, rows), jnp.float32),
            jax.ShapeDtypeStruct((chans, ks // CORES, rows), jnp.bfloat16),
        ],
        grid=(chans // STEP,),
        in_specs=[act] * (2 * n - 1) + [pl.BlockSpec((STEP, rows, rows), lambda g: (g, 0, 0))] * n,
        out_specs=[out] * 2,
        scratch_shapes=[pltpu.VMEM((STEP, n, rows, rows), jnp.bfloat16)],
        compiler_params=PARAMS,
        cost_estimate=pl.CostEstimate(
            flops=2 * chans * ks * rows * n * rows, bytes_accessed=2 * chans * rows * (n * rows + ks * (2 * n + 1)), transcendentals=0
        ),
        name="left_products",
    )(own, *ups, *downs, *blocks)


def tail_kernel(mask, pair, gain, bias, weight, *refs):
    groups = [refs[i * CHUNKS : (i + 1) * CHUNKS] for i in range(6)]
    left_mine, left_other, partials, ups, downs, right_other = groups
    out, flipped, turned, normed, inverses, grads, right_flat, left_flat, gain_col, bias_col, weight_t = refs[6 * CHUNKS :]
    rows, keys, _ = pair.shape
    hidden = weight.shape[1] // 4
    half = hidden // CORES
    part = half // CHUNKS
    core = this_core()
    set_columns(gain, bias, weight, gain_col, bias_col, weight_t)
    valid = unit_mask(mask, rows, pl.num_programs(0) * keys)

    def put(flat, owner, chunk, value):
        first = pl.multiple_of((owner * half + chunk * part) * keys, part * keys)
        flat[pl.ds(first, part * keys), :] = value.astype(jnp.float32).reshape(part * keys, rows)

    for chunk in range(CHUNKS):
        own, up, down = (ref[chunk][...].astype(jnp.float32) for ref in (partials, ups, downs))
        put(right_flat, core, chunk, own[0] + up + down)
        put(right_flat, 1 - core, chunk, right_other[chunk][...])
        put(left_flat, core, chunk, left_mine[chunk][...])
        put(left_flat, 1 - core, chunk, left_other[chunk][...])
    turn(pair, flipped, turned)
    scaled, inverse = normalize(turned[...])
    turned[...] = scaled
    inverses[...] = inverse
    normed[...] = (scaled * gain_col[...] + bias_col[...]).astype(jnp.bfloat16)
    for key in range(keys):
        projected = jnp.dot(weight_t[...], normed[key], preferred_element_type=jnp.float32)
        for side, source in enumerate((left_flat, right_flat)):
            lin = projected[2 * side * hidden : (2 * side + 1) * hidden]
            sig = jax.nn.sigmoid(projected[(2 * side + 1) * hidden : (2 * side + 2) * hidden])
            through = source[pl.ds(key, hidden, stride=keys), :] * valid * sig
            grads[key, 2 * side * hidden : (2 * side + 1) * hidden, :] = through.astype(jnp.bfloat16)
            grads[key, (2 * side + 1) * hidden : (2 * side + 2) * hidden, :] = (through * lin * (1.0 - sig)).astype(
                jnp.bfloat16
            )
    for key in range(keys):
        scaled = turned[key]
        scaled_grad = jnp.dot(weight[...], grads[key], preferred_element_type=jnp.float32) * gain_col[...]
        result = inverses[key] * (
            scaled_grad
            - jnp.mean(scaled_grad, axis=0, keepdims=True)
            - scaled * jnp.mean(scaled_grad * scaled, axis=0, keepdims=True)
        )
        normed[key] = result.astype(jnp.bfloat16)
    eye = identity(rows)
    for key in range(keys):
        flipped[key] = lax.dot_general(eye, normed[key], BY_LAST, preferred_element_type=jnp.float32).astype(jnp.bfloat16)
    out[...] = jnp.transpose(flipped[...], (1, 0, 2))


def tail(pair, gain, bias, proj_weight, tile_mask, left_mine, left_other, partials, ups, downs, right_other):
    rows, cols, chans = pair.shape
    width = proj_weight.shape[1]
    part = width // 4 // CORES // CHUNKS
    vector = pl.BlockSpec((1, chans), lambda g: (0, 0))
    cells = pl.BlockSpec((rows, KEYS, chans), lambda g: (0, g, 0))
    small = [pl.BlockSpec((part, KEYS, rows), lambda g: (0, g, 0))] * CHUNKS
    first = [pl.BlockSpec((1, part, KEYS, rows), lambda g: (0, 0, g, 0))] * CHUNKS
    return pl.pallas_call(
        tail_kernel,
        out_shape=jax.ShapeDtypeStruct(pair.shape, jnp.bfloat16),
        grid=(cols // KEYS,),
        in_specs=[
            pl.BlockSpec(memory_space=pltpu.SMEM),
            cells,
            vector,
            vector,
            pl.BlockSpec((chans, width), lambda g: (0, 0)),
        ]
        + small * 2
        + first
        + small * 3,
        out_specs=cells,
        scratch_shapes=[
            pltpu.VMEM((KEYS, rows, chans), jnp.bfloat16),
            pltpu.VMEM((KEYS, chans, rows), jnp.float32),
            pltpu.VMEM((KEYS, chans, rows), jnp.bfloat16),
            pltpu.VMEM((KEYS, 1, rows), jnp.float32),
            pltpu.VMEM((KEYS, width, rows), jnp.bfloat16),
            pltpu.VMEM((width // 4 * KEYS, rows), jnp.float32),
            pltpu.VMEM((width // 4 * KEYS, rows), jnp.float32),
            pltpu.VMEM((chans, rows), jnp.float32),
            pltpu.VMEM((chans, rows), jnp.float32),
            pltpu.VMEM((width, chans), jnp.bfloat16),
        ],
        compiler_params=PARAMS,
        cost_estimate=pl.CostEstimate(
            flops=8 * rows * cols * chans * width, bytes_accessed=10 * rows * cols * chans, transcendentals=rows * cols * width
        ),
        name="tail",
    )(tile_mask, pair, gain, bias, proj_weight, *left_mine, *left_other, *partials, *ups, *downs, *right_other)


def after(value, *others):
    return lax.optimization_barrier((value, others))[0]


def shards(pair, grad_x, norm_gain, norm_bias, proj_weight, tile_mask):
    n, n_col = lax.axis_size("row"), lax.axis_size("col")
    row = lax.axis_index("row")
    half = grad_x.shape[2] // CORES
    part = half // CHUNKS
    gain, bias = norm_gain[None, :], norm_bias[None, :]

    def exchange(value, mask):
        return lax.ppermute(value, "col", [(d, d ^ mask) for d in range(n_col)])

    def step_up(value):
        return lax.ppermute(value, "row", [(r, r + 1) for r in range(n - 1)])

    def step_down(value):
        return lax.ppermute(value, "row", [(r + 1, r) for r in range(n - 1)])

    raw = jnp.transpose(grad_x, (1, 2, 0))
    other = exchange(lax.dynamic_slice_in_dim(raw, (1 - this_core()) * half, half, 1), 1)
    right_mine, right_theirs = front(pair, gain, bias, proj_weight, tile_mask, 1)
    packed = pack(raw, after(other, right_mine))
    right_other = exchange(right_theirs, 1)
    owns = [
        jnp.concatenate((right_mine[c * part : (c + 1) * part], right_other[c * part : (c + 1) * part]), axis=1)
        for c in range(CHUNKS)
    ]
    left_mine, left_theirs = front(after(pair, owns), gain, bias, proj_weight, tile_mask, 0)
    left_other = exchange(left_theirs, 1)

    bits = [1 << b for b in range(n_col.bit_length() - 2)]
    panels = []
    for c, own in enumerate(packed):
        slots = {0: own}
        order = bits[c % len(bits) :] + bits[: c % len(bits)]
        for bit in order:
            for m in list(slots):
                value = slots[m]
                if c == 0 and m > 0:
                    value = after(value, left_mine)
                if c > 0 and m == 0:
                    value = after(value, panels[-1][bit] if bit != order[0] else panels[-1][1:])
                slots[m | bit] = exchange(value, CORES * bit)
        panels.append([slots[m] for m in range(len(slots))])

    ups, downs, partials = [], [], []
    for c in range(CHUNKS):
        own = owns[c] if c == 0 else after(owns[c], ups[0][0], downs[0][0])
        ups.append([step_up(own)])
        downs.append([step_down(own)])
    for c in range(CHUNKS):
        partials.append(partial_products(left_mine, left_other, panels[c], c))

    def plus(arrived, sums, use):
        return (arrived.astype(jnp.float32) + jnp.where(use, sums.astype(jnp.float32), 0.0)).astype(jnp.bfloat16)

    for t in range(1, n):
        for c in range(CHUNKS):
            ups[c].append(step_up(plus(ups[c][-1], partials[c][n - t], row < t)))
            downs[c].append(step_down(plus(downs[c][-1], partials[c][t], row >= n - t)))

    left_grads = []
    for c in range(CHUNKS):
        own = after(owns[c], ups[-1][n - 2], downs[-1][n - 2])
        left_grads.append(left_products(own, ups[c][: n - 1], downs[c][: n - 1], panels[c]))
    left_grad_other = [exchange(theirs, 1) for _, theirs in left_grads]
    ks = left_mine.shape[1]
    right_grad_other = []
    for c in range(CHUNKS):
        total = sum(v[:, ks:].astype(jnp.float32) for v in (partials[c][0], ups[c][-1], downs[c][-1]))
        right_grad_other.append(exchange(total.astype(jnp.bfloat16), 1))

    return tail(
        pair,
        gain,
        bias,
        proj_weight,
        tile_mask,
        [mine for mine, _ in left_grads],
        left_grad_other,
        partials,
        [u[-1] for u in ups],
        [d[-1] for d in downs],
        right_grad_other,
    )


def solution(mesh):
    placed = (P("row", "col", None), P("row", "col", None), P(), P(), P(), P())
    return jax.shard_map(
        shards, mesh=mesh, in_specs=placed, out_specs=P("row", "col", None), check_vma=False
    )
```

```python
import functools

import jax
import jax.numpy as jnp
from jax import lax
from jax.experimental import pallas as pl
from jax.experimental.pallas import tpu as pltpu
from jax.sharding import PartitionSpec as P

BLK = 128
CHUNKS = 2
STEP = 8
KEYS = 16
CORES = 2
VMEM_LIMIT = 12 * 1024 * 1024
PARAMS = pltpu.CompilerParams(vmem_limit_bytes=VMEM_LIMIT)
FRONT_COST = pl.CostEstimate(flops=1, bytes_accessed=18_000_000, transcendentals=0)
COST = pl.CostEstimate(flops=1, bytes_accessed=8_000_000, transcendentals=0)
BY_LAST = (((1,), (1,)), ((), ()))


def identity(size):
    return (
        lax.broadcasted_iota(jnp.int32, (size, size), 0) == lax.broadcasted_iota(jnp.int32, (size, size), 1)
    ).astype(jnp.bfloat16)


def column(vector_ref, rows):
    return jnp.broadcast_to(vector_ref[...], (rows, vector_ref.shape[1])).T


def unit_mask(mask_ref, rows, cols):
    row, col = lax.axis_index("row"), lax.axis_index("col")
    return mask_ref[(row * rows) // BLK, (col * cols) // BLK].astype(jnp.float32)


def this_core():
    return lax.rem(lax.axis_index("col"), CORES)


def turn(pair, flipped, turned):
    flipped[...] = jnp.transpose(pair[...], (1, 0, 2))
    eye = identity(pair.shape[2])
    for key in range(pair.shape[1]):
        turned[key] = lax.dot_general(eye, flipped[key], BY_LAST, preferred_element_type=jnp.float32)


def normalize(values):
    centred = values - jnp.mean(values, axis=1, keepdims=True)
    inverse = lax.rsqrt(jnp.mean(centred * centred, axis=1, keepdims=True) + 1e-05)
    return centred * inverse, inverse


def set_columns(gain, bias, weight, gain_col, bias_col, weight_t):
    @pl.when(pl.program_id(0) == 0)
    def _():
        gain_col[...] = column(gain, gain_col.shape[1])
        bias_col[...] = column(bias, bias_col.shape[1])
        weight_t[...] = weight[...].astype(jnp.float32).T.astype(jnp.bfloat16)


def front_kernel(mask, pair, gain, bias, weight, mine, theirs, flipped, turned, normed, acts, whole, gain_col, bias_col, weight_t):
    rows, keys, _ = pair.shape
    hidden = weight.shape[1] // 2
    half = hidden // CORES
    set_columns(gain, bias, weight, gain_col, bias_col, weight_t)
    valid = unit_mask(mask, rows, pl.num_programs(0) * keys)
    turn(pair, flipped, turned)
    scaled, _ = normalize(turned[...])
    normed[...] = (scaled * gain_col[...] + bias_col[...]).astype(jnp.bfloat16)
    for key in range(keys):
        projected = jnp.dot(weight_t[...], normed[key], preferred_element_type=jnp.float32)
        acts[key] = (valid * jax.nn.sigmoid(projected[hidden:]) * projected[:hidden]).astype(jnp.bfloat16)
    whole[...] = jnp.transpose(acts[...], (1, 0, 2))
    core = this_core()
    mine[...] = whole[pl.ds(core * half, half)]
    theirs[...] = whole[pl.ds((1 - core) * half, half)]


def front(pair, gain, bias, proj_weight, tile_mask, side):
    rows, cols, chans = pair.shape
    width = proj_weight.shape[1] // 2
    half = width // 2 // CORES
    vector = pl.BlockSpec((1, chans), lambda g: (0, 0))
    return pl.pallas_call(
        front_kernel,
        out_shape=[jax.ShapeDtypeStruct((half, cols, rows), jnp.bfloat16)] * 2,
        grid=(cols // KEYS,),
        in_specs=[
            pl.BlockSpec(memory_space=pltpu.SMEM),
            pl.BlockSpec((rows, KEYS, chans), lambda g: (0, g, 0)),
            vector,
            vector,
            pl.BlockSpec((chans, width), lambda g: (0, side)),
        ],
        out_specs=[pl.BlockSpec((half, KEYS, rows), lambda g: (0, g, 0))] * 2,
        scratch_shapes=[
            pltpu.VMEM((KEYS, rows, chans), jnp.bfloat16),
            pltpu.VMEM((KEYS, chans, rows), jnp.float32),
            pltpu.VMEM((KEYS, chans, rows), jnp.bfloat16),
            pltpu.VMEM((KEYS, width // 2, rows), jnp.bfloat16),
            pltpu.VMEM((width // 2, KEYS, rows), jnp.bfloat16),
            pltpu.VMEM((chans, rows), jnp.float32),
            pltpu.VMEM((chans, rows), jnp.float32),
            pltpu.VMEM((width, chans), jnp.bfloat16),
        ],
        compiler_params=PARAMS,
        cost_estimate=FRONT_COST,
        name="left_front" if side == 0 else "right_front",
    )(tile_mask, *(pltpu.with_memory_space_constraint(v, pltpu.HBM) for v in (pair, gain, bias, proj_weight)))


def pack_kernel(own, other, out):
    cols, half, _ = other.shape
    core = this_core()
    for block, place in ((own[:, pl.ds(pl.multiple_of(core * half, half), half), :], core), (other[...], 1 - core)):
        out[:, pl.ds(pl.multiple_of(place * cols, cols), cols), :] = jnp.transpose(block, (1, 0, 2))


def pack(own, other):
    cols, half, rows = other.shape
    return pl.pallas_call(
        pack_kernel,
        out_shape=jax.ShapeDtypeStruct((half, CORES * cols, rows), jnp.bfloat16),
        compiler_params=PARAMS,
        cost_estimate=COST,
        name="pack",
    )(own, other)


def chunk_spec(array, chans, chunk):
    first = chunk * chans // STEP if array.shape[0] > chans else 0
    return pl.BlockSpec((STEP,) + array.shape[1:], lambda g: (first + g, 0, 0))


def partial_kernel(n, left_mine, left_other, up, down, *refs):
    blocks, outs, (up_next, down_next, sums) = refs[:n], refs[n : 2 * n], refs[2 * n :]
    row, chip = lax.axis_index("row"), lax.axis_index("col") // CORES
    for c in range(STEP):
        lhs = jnp.concatenate((left_mine[c], left_other[c]), axis=0)
        for m, block in enumerate(blocks):
            away = lax.rem(jnp.bitwise_xor(chip, m) - row + n, n)
            sums[away, c] = lax.dot_general(lhs, block[c], BY_LAST, preferred_element_type=jnp.float32).astype(jnp.bfloat16)
    for s, out in enumerate(outs):
        out[...] = sums[s]
    up_next[...] = jnp.where(row < 1, sums[n - 1], up[...])
    down_next[...] = jnp.where(row >= n - 1, sums[1], down[...])


def partial_products(left_mine, left_other, up, down, blocks, chunk):
    rows = blocks[0].shape[1]
    ks, chans = left_mine.shape[1], left_mine.shape[0] // CHUNKS
    n = len(blocks)
    args = (left_mine, left_other, up, down, *blocks)
    return pl.pallas_call(
        functools.partial(partial_kernel, n),
        out_shape=[pltpu.HBM((chans, CORES * ks, rows), jnp.bfloat16)] * (n + 2),
        grid=(chans // STEP,),
        in_specs=[chunk_spec(v, chans, chunk) for v in args],
        out_specs=[pl.BlockSpec((STEP, CORES * ks, rows), lambda g: (g, 0, 0))] * (n + 2),
        scratch_shapes=[pltpu.VMEM((n, STEP, CORES * ks, rows), jnp.bfloat16)],
        compiler_params=PARAMS,
        cost_estimate=COST,
        name="right_partials",
    )(*args)


def left_kernel(n, own, *refs):
    ups, downs, refs = refs[: n - 1], refs[n - 1 : 2 * n - 2], refs[2 * n - 2 :]
    blocks, (mine, theirs, panel) = refs[:n], refs[n:]
    row, chip = lax.axis_index("row"), lax.axis_index("col") // CORES
    ks = mine.shape[1]
    for c in range(STEP):
        for m, block in enumerate(blocks):
            panel[c, jnp.bitwise_xor(chip, m)] = block[c]
        acts, grads = [], []
        for s in range(n):
            grads.append(panel[c, lax.rem(row + s, n)])
            acts.append(own[c] if s == 0 else jnp.where(row + s < n, downs[s - 1][c], ups[n - s - 1][c]))
        out = jnp.dot(
            jnp.concatenate(acts, axis=1), jnp.concatenate(grads, axis=0), preferred_element_type=jnp.float32
        )
        mine[c] = out[:ks]
        theirs[c] = out[ks:].astype(jnp.bfloat16)


def left_products(own, ups, downs, blocks, chunk):
    chans, ks, rows = ups[-1].shape
    n = len(blocks)
    out = pl.BlockSpec((STEP, ks // CORES, rows), lambda g: (g, 0, 0))
    args = (own, *ups, *downs, *blocks)
    return pl.pallas_call(
        functools.partial(left_kernel, n),
        out_shape=[
            jax.ShapeDtypeStruct((chans, ks // CORES, rows), jnp.float32),
            jax.ShapeDtypeStruct((chans, ks // CORES, rows), jnp.bfloat16),
        ],
        grid=(chans // STEP,),
        in_specs=[chunk_spec(v, chans, chunk) for v in args],
        out_specs=[out] * 2,
        scratch_shapes=[pltpu.VMEM((STEP, n, rows, rows), jnp.bfloat16)],
        compiler_params=PARAMS,
        cost_estimate=COST,
        name="left_products",
    )(*args)


def tail_kernel(mask, pair, gain, bias, weight, *refs):
    groups = [refs[i * CHUNKS : (i + 1) * CHUNKS] for i in range(6)]
    left_mine, left_other, partials, ups, downs, right_other = groups
    out, flipped, turned, normed, inverses, grads, right_flat, left_flat, gain_col, bias_col, weight_t = refs[6 * CHUNKS :]
    rows, keys, _ = pair.shape
    hidden = weight.shape[1] // 4
    half = hidden // CORES
    part = half // CHUNKS
    core = this_core()
    set_columns(gain, bias, weight, gain_col, bias_col, weight_t)
    valid = unit_mask(mask, rows, pl.num_programs(0) * keys)

    def put(flat, owner, chunk, value):
        first = pl.multiple_of((owner * half + chunk * part) * keys, part * keys)
        flat[pl.ds(first, part * keys), :] = value.astype(jnp.float32).reshape(part * keys, rows)

    for chunk in range(CHUNKS):
        own, up, down = (ref[chunk][...].astype(jnp.float32) for ref in (partials, ups, downs))
        put(right_flat, core, chunk, own + up + down)
        put(right_flat, 1 - core, chunk, right_other[chunk][...])
        put(left_flat, core, chunk, left_mine[chunk][...])
        put(left_flat, 1 - core, chunk, left_other[chunk][...])
    turn(pair, flipped, turned)
    scaled, inverse = normalize(turned[...])
    turned[...] = scaled
    inverses[...] = inverse
    normed[...] = (scaled * gain_col[...] + bias_col[...]).astype(jnp.bfloat16)
    for key in range(keys):
        projected = jnp.dot(weight_t[...], normed[key], preferred_element_type=jnp.float32)
        for side, source in enumerate((left_flat, right_flat)):
            lin = projected[2 * side * hidden : (2 * side + 1) * hidden]
            sig = jax.nn.sigmoid(projected[(2 * side + 1) * hidden : (2 * side + 2) * hidden])
            through = source[pl.ds(key, hidden, stride=keys), :] * valid * sig
            grads[key, 2 * side * hidden : (2 * side + 1) * hidden, :] = through.astype(jnp.bfloat16)
            grads[key, (2 * side + 1) * hidden : (2 * side + 2) * hidden, :] = (through * lin * (1.0 - sig)).astype(
                jnp.bfloat16
            )
    for key in range(keys):
        scaled = turned[key]
        scaled_grad = jnp.dot(weight[...], grads[key], preferred_element_type=jnp.float32) * gain_col[...]
        result = inverses[key] * (
            scaled_grad
            - jnp.mean(scaled_grad, axis=0, keepdims=True)
            - scaled * jnp.mean(scaled_grad * scaled, axis=0, keepdims=True)
        )
        normed[key] = result.astype(jnp.bfloat16)
    eye = identity(rows)
    for key in range(keys):
        flipped[key] = lax.dot_general(eye, normed[key], BY_LAST, preferred_element_type=jnp.float32).astype(jnp.bfloat16)
    out[...] = jnp.transpose(flipped[...], (1, 0, 2))


def tail(pair, gain, bias, proj_weight, tile_mask, left_mine, left_other, partials, ups, downs, right_other):
    rows, cols, chans = pair.shape
    width = proj_weight.shape[1]
    part = width // 4 // CORES // CHUNKS
    vector = pl.BlockSpec((1, chans), lambda g: (0, 0))
    cells = pl.BlockSpec((rows, KEYS, chans), lambda g: (0, g, 0))
    small = [pl.BlockSpec((part, KEYS, rows), lambda g: (0, g, 0))] * CHUNKS
    return pl.pallas_call(
        tail_kernel,
        out_shape=jax.ShapeDtypeStruct(pair.shape, jnp.bfloat16),
        grid=(cols // KEYS,),
        in_specs=[
            pl.BlockSpec(memory_space=pltpu.SMEM),
            cells,
            vector,
            vector,
            pl.BlockSpec((chans, width), lambda g: (0, 0)),
        ]
        + small * 6,
        out_specs=cells,
        scratch_shapes=[
            pltpu.VMEM((KEYS, rows, chans), jnp.bfloat16),
            pltpu.VMEM((KEYS, chans, rows), jnp.float32),
            pltpu.VMEM((KEYS, chans, rows), jnp.bfloat16),
            pltpu.VMEM((KEYS, 1, rows), jnp.float32),
            pltpu.VMEM((KEYS, width, rows), jnp.bfloat16),
            pltpu.VMEM((width // 4 * KEYS, rows), jnp.float32),
            pltpu.VMEM((width // 4 * KEYS, rows), jnp.float32),
            pltpu.VMEM((chans, rows), jnp.float32),
            pltpu.VMEM((chans, rows), jnp.float32),
            pltpu.VMEM((width, chans), jnp.bfloat16),
        ],
        compiler_params=PARAMS,
        cost_estimate=COST,
        name="tail",
    )(tile_mask, pair, gain, bias, proj_weight, *left_mine, *left_other, *partials, *ups, *downs, *right_other)


def after(value, *others):
    return lax.optimization_barrier((value, others))[0]


def shards(pair, grad_x, norm_gain, norm_bias, proj_weight, tile_mask):
    n, n_col = lax.axis_size("row"), lax.axis_size("col")
    row = lax.axis_index("row")
    half = grad_x.shape[2] // CORES
    part = half // CHUNKS
    gain, bias = norm_gain[None, :], norm_bias[None, :]

    def exchange(value, mask):
        return lax.ppermute(value, "col", [(d, d ^ mask) for d in range(n_col)])

    def step_up(value):
        return lax.ppermute(value, "row", [(r, r + 1) for r in range(n - 1)])

    def step_down(value):
        return lax.ppermute(value, "row", [(r + 1, r) for r in range(n - 1)])

    raw = jnp.transpose(grad_x, (1, 2, 0))
    packed = pack(raw, exchange(lax.dynamic_slice_in_dim(raw, (1 - this_core()) * half, half, 1), 1))

    slots = [[packed] * CHUNKS]
    for m in range(1, n_col // CORES):
        axes = [1 << b for b in range(m.bit_length()) if m >> b & 1]
        if len(axes) == 1:
            slots.append([exchange(packed, CORES * m)] * CHUNKS)
            continue
        slots.append([])
        for c in range(CHUNKS):
            bit = axes[(c + 1) % len(axes)]
            value = slots[m ^ bit][c]
            value = value if value.shape[0] == part else value[c * part : (c + 1) * part]
            slots[m].append(exchange(value, CORES * bit))
    panels = [[slot[c] for slot in slots] for c in range(CHUNKS)]

    right_mine, right_theirs = front(after(pair, packed), gain, bias, proj_weight, tile_mask, 1)
    own = jnp.concatenate((right_mine, exchange(right_theirs, 1)), axis=1)
    first_up, first_down = step_up(own), step_down(own)
    left_mine, left_theirs = front(after(pair, own), gain, bias, proj_weight, tile_mask, 0)
    left_other = exchange(left_theirs, 1)

    ups, downs, partials = [], [], []
    for c in range(CHUNKS):
        *sums, up, down = partial_products(left_mine, left_other, first_up, first_down, panels[c], c)
        partials.append(sums)
        ups.append([first_up, step_up(up)])
        downs.append([first_down, step_down(down)])

    def plus(arrived, sums, use):
        return (arrived.astype(jnp.float32) + jnp.where(use, sums.astype(jnp.float32), 0.0)).astype(jnp.bfloat16)

    left_grads = []
    for t in range(2, n):
        for c in range(CHUNKS):
            up, down = ups[c][-1], downs[c][-1]
            if t == n - 1 and c > 0:
                up = after(up, left_grads[c - 1])
            ups[c].append(step_up(plus(up, partials[c][n - t], row < t)))
            downs[c].append(step_down(plus(down, partials[c][t], row >= n - t)))
            if t == n - 1:
                left_grads.append(left_products(own, ups[c][: n - 1], downs[c][: n - 1], panels[c], c))
    left_grad_other = [exchange(theirs, 1) for _, theirs in left_grads]
    ks = left_mine.shape[1]
    right_grad_other = []
    for c in range(CHUNKS):
        total = sum(v[:, ks:].astype(jnp.float32) for v in (partials[c][0], ups[c][-1], downs[c][-1]))
        right_grad_other.append(exchange(total.astype(jnp.bfloat16), 1))

    return tail(
        pair,
        gain,
        bias,
        proj_weight,
        tile_mask,
        [mine for mine, _ in left_grads],
        left_grad_other,
        [sums[0] for sums in partials],
        [u[-1] for u in ups],
        [d[-1] for d in downs],
        right_grad_other,
    )


def solution(mesh):
    placed = (P("row", "col", None), P("row", "col", None), P(), P(), P(), P())
    return jax.shard_map(
        shards, mesh=mesh, in_specs=placed, out_specs=P("row", "col", None), check_vma=False
    )
```

```python
import functools

import jax
import jax.numpy as jnp
from jax import lax
from jax.experimental import pallas as pl
from jax.experimental.pallas import tpu as pltpu
from jax.sharding import PartitionSpec as P

BLK = 128
CHUNKS = 2
STEP = 8
KEYS = 16
CORES = 2
VMEM_LIMIT = 18 * 1024 * 1024
PARAMS = pltpu.CompilerParams(vmem_limit_bytes=VMEM_LIMIT)
FRONT_COST = pl.CostEstimate(flops=1, bytes_accessed=18_000_000, transcendentals=0)
COST = pl.CostEstimate(flops=1, bytes_accessed=8_000_000, transcendentals=0)
BY_LAST = (((1,), (1,)), ((), ()))


def identity(size):
    return (
        lax.broadcasted_iota(jnp.int32, (size, size), 0) == lax.broadcasted_iota(jnp.int32, (size, size), 1)
    ).astype(jnp.bfloat16)


def column(vector_ref, rows):
    return jnp.broadcast_to(vector_ref[...], (rows, vector_ref.shape[1])).T


def unit_mask(mask_ref, rows, cols):
    row, col = lax.axis_index("row"), lax.axis_index("col")
    return mask_ref[(row * rows) // BLK, (col * cols) // BLK].astype(jnp.float32)


def this_core():
    return lax.rem(lax.axis_index("col"), CORES)


def turn(pair, flipped, turned):
    flipped[...] = jnp.transpose(pair[...], (1, 0, 2))
    eye = identity(pair.shape[2])
    for key in range(pair.shape[1]):
        turned[key] = lax.dot_general(eye, flipped[key], BY_LAST, preferred_element_type=jnp.float32)


def normalize(values):
    centred = values - jnp.mean(values, axis=1, keepdims=True)
    inverse = lax.rsqrt(jnp.mean(centred * centred, axis=1, keepdims=True) + 1e-05)
    return centred * inverse, inverse


def set_columns(gain, bias, weight, gain_col, bias_col, weight_t):
    @pl.when(pl.program_id(0) == 0)
    def _():
        gain_col[...] = column(gain, gain_col.shape[1])
        bias_col[...] = column(bias, bias_col.shape[1])
        weight_t[...] = weight[...].astype(jnp.float32).T.astype(jnp.bfloat16)


def front_kernel(mask, pair, gain, bias, weight, mine, theirs, flipped, turned, normed, acts, whole, gain_col, bias_col, weight_t):
    rows, keys, _ = pair.shape
    hidden = weight.shape[1] // 2
    half = hidden // CORES
    set_columns(gain, bias, weight, gain_col, bias_col, weight_t)
    valid = unit_mask(mask, rows, pl.num_programs(0) * keys)
    turn(pair, flipped, turned)
    scaled, _ = normalize(turned[...])
    normed[...] = (scaled * gain_col[...] + bias_col[...]).astype(jnp.bfloat16)
    for key in range(keys):
        projected = jnp.dot(weight_t[...], normed[key], preferred_element_type=jnp.float32)
        acts[key] = (valid * jax.nn.sigmoid(projected[hidden:]) * projected[:hidden]).astype(jnp.bfloat16)
    whole[...] = jnp.transpose(acts[...], (1, 0, 2))
    core = this_core()
    mine[...] = whole[pl.ds(core * half, half)]
    theirs[...] = whole[pl.ds((1 - core) * half, half)]


def front(pair, gain, bias, proj_weight, tile_mask, side):
    rows, cols, chans = pair.shape
    width = proj_weight.shape[1] // 2
    half = width // 2 // CORES
    vector = pl.BlockSpec((1, chans), lambda g: (0, 0))
    return pl.pallas_call(
        front_kernel,
        out_shape=[jax.ShapeDtypeStruct((half, cols, rows), jnp.bfloat16)] * 2,
        grid=(cols // KEYS,),
        in_specs=[
            pl.BlockSpec(memory_space=pltpu.SMEM),
            pl.BlockSpec((rows, KEYS, chans), lambda g: (0, g, 0)),
            vector,
            vector,
            pl.BlockSpec((chans, width), lambda g: (0, side)),
        ],
        out_specs=[pl.BlockSpec((half, KEYS, rows), lambda g: (0, g, 0))] * 2,
        scratch_shapes=[
            pltpu.VMEM((KEYS, rows, chans), jnp.bfloat16),
            pltpu.VMEM((KEYS, chans, rows), jnp.float32),
            pltpu.VMEM((KEYS, chans, rows), jnp.bfloat16),
            pltpu.VMEM((KEYS, width // 2, rows), jnp.bfloat16),
            pltpu.VMEM((width // 2, KEYS, rows), jnp.bfloat16),
            pltpu.VMEM((chans, rows), jnp.float32),
            pltpu.VMEM((chans, rows), jnp.float32),
            pltpu.VMEM((width, chans), jnp.bfloat16),
        ],
        compiler_params=PARAMS,
        cost_estimate=FRONT_COST,
        name="left_front" if side == 0 else "right_front",
    )(tile_mask, *(pltpu.with_memory_space_constraint(v, pltpu.HBM) for v in (pair, gain, bias, proj_weight)))


def pack_kernel(own, other, out):
    cols, half, _ = other.shape
    core = this_core()
    for block, place in ((own[:, pl.ds(pl.multiple_of(core * half, half), half), :], core), (other[...], 1 - core)):
        out[:, pl.ds(pl.multiple_of(place * cols, cols), cols), :] = jnp.transpose(block, (1, 0, 2))


def pack(own, other):
    cols, half, rows = other.shape
    return pl.pallas_call(
        pack_kernel,
        out_shape=jax.ShapeDtypeStruct((half, CORES * cols, rows), jnp.bfloat16),
        compiler_params=PARAMS,
        cost_estimate=COST,
        name="pack",
    )(own, other)


def chunk_spec(array, chans, chunk):
    first = chunk * chans // STEP if array.shape[0] > chans else 0
    return pl.BlockSpec((STEP,) + array.shape[1:], lambda g: (first + g, 0, 0))


def lanes(n):
    row = lax.axis_index("row")
    even = lax.rem(row, 2) == 0
    return even, jnp.where(even, row + 1 < n, True), jnp.where(even, row > 0, row + 1 < n)


def onward(by_a, by_b, up_sums, down_sums, t, n):
    row = lax.axis_index("row")
    even, use_a, use_b = lanes(n)
    up = jnp.where(row < t, up_sums.astype(jnp.float32), 0.0)
    down = jnp.where(row >= n - t, down_sums.astype(jnp.float32), 0.0)
    out_a = jnp.where(use_b, by_b.astype(jnp.float32), 0.0) + jnp.where(even, up, down)
    out_b = jnp.where(use_a, by_a.astype(jnp.float32), 0.0) + jnp.where(even, down, up)
    return out_a.astype(jnp.bfloat16), out_b.astype(jnp.bfloat16)


def partial_kernel(n, left_mine, left_other, by_a, by_b, *refs):
    blocks, outs, (next_a, next_b, sums) = refs[:n], refs[n : 2 * n], refs[2 * n :]
    row, chip = lax.axis_index("row"), lax.axis_index("col") // CORES
    for c in range(STEP):
        lhs = jnp.concatenate((left_mine[c], left_other[c]), axis=0)
        for m, block in enumerate(blocks):
            away = lax.rem(jnp.bitwise_xor(chip, m) - row + n, n)
            sums[away, c] = lax.dot_general(lhs, block[c], BY_LAST, preferred_element_type=jnp.float32).astype(jnp.bfloat16)
    for s, out in enumerate(outs):
        out[...] = sums[s]
    next_a[...], next_b[...] = onward(by_a[...], by_b[...], sums[n - 1], sums[1], 1, n)


def in_hbm(*values):
    return [pltpu.with_memory_space_constraint(v, pltpu.HBM) for v in values]


def partial_products(left_mine, left_other, by_a, by_b, blocks, chunk):
    rows = blocks[0].shape[1]
    ks, chans = left_mine.shape[1], left_mine.shape[0] // CHUNKS
    n = len(blocks)
    args = (left_mine, left_other, by_a, by_b, *blocks)
    return pl.pallas_call(
        functools.partial(partial_kernel, n),
        out_shape=[pltpu.HBM((chans, CORES * ks, rows), jnp.bfloat16)] * n
        + [jax.ShapeDtypeStruct((chans, CORES * ks, rows), jnp.bfloat16)] * 2,
        grid=(chans // STEP,),
        in_specs=[chunk_spec(v, chans, chunk) for v in args],
        out_specs=[pl.BlockSpec((STEP, CORES * ks, rows), lambda g: (g, 0, 0))] * (n + 2),
        scratch_shapes=[pltpu.VMEM((n, STEP, CORES * ks, rows), jnp.bfloat16)],
        compiler_params=PARAMS,
        cost_estimate=COST,
        name="right_partials",
    )(*args)


def left_kernel(n, own, *refs):
    by_a, by_b, refs = refs[: n - 1], refs[n - 1 : 2 * n - 2], refs[2 * n - 2 :]
    blocks, (mine, theirs, panel) = refs[:n], refs[n:]
    row, chip = lax.axis_index("row"), lax.axis_index("col") // CORES
    even = lanes(n)[0]
    ks = mine.shape[1]
    for c in range(STEP):
        for m, block in enumerate(blocks):
            panel[c, jnp.bitwise_xor(chip, m)] = block[c]
        acts, grads = [own[c]], [panel[c, row]]
        for s in range(1, n):
            from_above = jnp.where(even, by_a[s - 1][c], by_b[s - 1][c])
            from_below = jnp.where(even, by_b[n - s - 1][c], by_a[n - s - 1][c])
            acts.append(jnp.where(row + s < n, from_above, from_below))
            grads.append(panel[c, lax.rem(row + s, n)])
        out = jnp.dot(
            jnp.concatenate(acts, axis=1), jnp.concatenate(grads, axis=0), preferred_element_type=jnp.float32
        )
        mine[c] = out[:ks]
        theirs[c] = out[ks:].astype(jnp.bfloat16)


def left_products(own, by_a, by_b, blocks, chunk):
    chans, ks, rows = by_a[-1].shape
    n = len(blocks)
    out = pl.BlockSpec((STEP, ks // CORES, rows), lambda g: (g, 0, 0))
    args = (own, *by_a, *by_b, *blocks)
    return pl.pallas_call(
        functools.partial(left_kernel, n),
        out_shape=[
            jax.ShapeDtypeStruct((chans, ks // CORES, rows), jnp.float32),
            jax.ShapeDtypeStruct((chans, ks // CORES, rows), jnp.bfloat16),
        ],
        grid=(chans // STEP,),
        in_specs=[chunk_spec(v, chans, chunk) for v in args],
        out_specs=[out] * 2,
        scratch_shapes=[pltpu.VMEM((STEP, n, rows, rows), jnp.bfloat16)],
        compiler_params=PARAMS,
        cost_estimate=COST,
        name="left_products",
    )(*args)


def arrived_total(own, by_a, by_b, n):
    _, use_a, use_b = lanes(n)
    total = own.astype(jnp.float32) + jnp.where(use_a, by_a.astype(jnp.float32), 0.0)
    return total + jnp.where(use_b, by_b.astype(jnp.float32), 0.0)


def tail_kernel(n, mask, pair, gain, bias, weight, *refs):
    groups = [refs[i * CHUNKS : (i + 1) * CHUNKS] for i in range(6)]
    left_mine, left_other, partials, by_a, by_b, right_other = groups
    out, flipped, turned, normed, inverses, grads, right_flat, left_flat, gain_col, bias_col, weight_t = refs[6 * CHUNKS :]
    rows, keys, _ = pair.shape
    hidden = weight.shape[1] // 4
    half = hidden // CORES
    part = half // CHUNKS
    core = this_core()
    set_columns(gain, bias, weight, gain_col, bias_col, weight_t)
    valid = unit_mask(mask, rows, pl.num_programs(0) * keys)

    def put(flat, owner, chunk, value):
        first = pl.multiple_of((owner * half + chunk * part) * keys, part * keys)
        flat[pl.ds(first, part * keys), :] = value.astype(jnp.float32).reshape(part * keys, rows)

    for chunk in range(CHUNKS):
        total = arrived_total(partials[chunk][...], by_a[chunk][...], by_b[chunk][...], n)
        put(right_flat, core, chunk, total)
        put(right_flat, 1 - core, chunk, right_other[chunk][...])
        put(left_flat, core, chunk, left_mine[chunk][...])
        put(left_flat, 1 - core, chunk, left_other[chunk][...])
    turn(pair, flipped, turned)
    scaled, inverse = normalize(turned[...])
    turned[...] = scaled
    inverses[...] = inverse
    normed[...] = (scaled * gain_col[...] + bias_col[...]).astype(jnp.bfloat16)
    for key in range(keys):
        projected = jnp.dot(weight_t[...], normed[key], preferred_element_type=jnp.float32)
        for side, source in enumerate((left_flat, right_flat)):
            lin = projected[2 * side * hidden : (2 * side + 1) * hidden]
            sig = jax.nn.sigmoid(projected[(2 * side + 1) * hidden : (2 * side + 2) * hidden])
            through = source[pl.ds(key, hidden, stride=keys), :] * valid * sig
            grads[key, 2 * side * hidden : (2 * side + 1) * hidden, :] = through.astype(jnp.bfloat16)
            grads[key, (2 * side + 1) * hidden : (2 * side + 2) * hidden, :] = (through * lin * (1.0 - sig)).astype(
                jnp.bfloat16
            )
    for key in range(keys):
        scaled = turned[key]
        scaled_grad = jnp.dot(weight[...], grads[key], preferred_element_type=jnp.float32) * gain_col[...]
        result = inverses[key] * (
            scaled_grad
            - jnp.mean(scaled_grad, axis=0, keepdims=True)
            - scaled * jnp.mean(scaled_grad * scaled, axis=0, keepdims=True)
        )
        normed[key] = result.astype(jnp.bfloat16)
    eye = identity(rows)
    for key in range(keys):
        flipped[key] = lax.dot_general(eye, normed[key], BY_LAST, preferred_element_type=jnp.float32).astype(jnp.bfloat16)
    out[...] = jnp.transpose(flipped[...], (1, 0, 2))


def tail(pair, gain, bias, proj_weight, tile_mask, left_mine, left_other, partials, by_a, by_b, right_other):
    rows, cols, chans = pair.shape
    width = proj_weight.shape[1]
    part = width // 4 // CORES // CHUNKS
    vector = pl.BlockSpec((1, chans), lambda g: (0, 0))
    cells = pl.BlockSpec((rows, KEYS, chans), lambda g: (0, g, 0))
    small = [pl.BlockSpec((part, KEYS, rows), lambda g: (0, g, 0))] * CHUNKS
    return pl.pallas_call(
        functools.partial(tail_kernel, lax.axis_size("row")),
        out_shape=jax.ShapeDtypeStruct(pair.shape, jnp.bfloat16),
        grid=(cols // KEYS,),
        in_specs=[
            pl.BlockSpec(memory_space=pltpu.SMEM),
            cells,
            vector,
            vector,
            pl.BlockSpec((chans, width), lambda g: (0, 0)),
        ]
        + small * 6,
        out_specs=cells,
        scratch_shapes=[
            pltpu.VMEM((KEYS, rows, chans), jnp.bfloat16),
            pltpu.VMEM((KEYS, chans, rows), jnp.float32),
            pltpu.VMEM((KEYS, chans, rows), jnp.bfloat16),
            pltpu.VMEM((KEYS, 1, rows), jnp.float32),
            pltpu.VMEM((KEYS, width, rows), jnp.bfloat16),
            pltpu.VMEM((width // 4 * KEYS, rows), jnp.float32),
            pltpu.VMEM((width // 4 * KEYS, rows), jnp.float32),
            pltpu.VMEM((chans, rows), jnp.float32),
            pltpu.VMEM((chans, rows), jnp.float32),
            pltpu.VMEM((width, chans), jnp.bfloat16),
        ],
        compiler_params=PARAMS,
        cost_estimate=COST,
        name="tail",
    )(tile_mask, pair, gain, bias, proj_weight, *left_mine, *left_other, *partials, *by_a, *by_b, *right_other)


def after(value, *others):
    return lax.optimization_barrier((value, others))[0]


def shards(pair, grad_x, norm_gain, norm_bias, proj_weight, tile_mask):
    n, n_col = lax.axis_size("row"), lax.axis_size("col")
    half = grad_x.shape[2] // CORES
    part = half // CHUNKS
    gain, bias = norm_gain[None, :], norm_bias[None, :]

    def exchange(value, mask):
        return lax.ppermute(value, "col", [(d, d ^ mask) for d in range(n_col)])

    def hop(value, first):
        pairs = {r: r + 1 for r in range(first, n - 1, 2)}
        pairs.update({above: r for r, above in pairs.items()})
        perm = [
            (r * n_col + d, pairs[r] * n_col + d if r in pairs else r * n_col + (d ^ 1)) for r in range(n) for d in range(n_col)
        ]
        return lax.ppermute(value, ("row", "col"), perm)

    raw = jnp.transpose(grad_x, (1, 2, 0))
    other = exchange(lax.dynamic_slice_in_dim(raw, (1 - this_core()) * half, half, 1), 1)
    right_mine, right_theirs = front(pair, gain, bias, proj_weight, tile_mask, 1)
    packed = pack(raw, after(other, right_mine))

    slots = [[packed] * CHUNKS]
    for m in range(1, n_col // CORES):
        axes = [1 << b for b in range(m.bit_length()) if m >> b & 1]
        if len(axes) == 1:
            slots.append([exchange(packed, CORES * m)] * CHUNKS)
            continue
        slots.append([])
        for c in range(CHUNKS):
            bit = axes[(c + 1) % len(axes)]
            value = slots[m ^ bit][c]
            value = value if value.shape[0] == part else value[c * part : (c + 1) * part]
            slots[m].append(exchange(value, CORES * bit))
    panels = [[slot[c] for slot in slots] for c in range(CHUNKS)]

    own = jnp.concatenate((right_mine, exchange(right_theirs, 1)), axis=1)
    first_a, first_b = hop(own, 0), hop(own, 1)
    left_mine, left_theirs = front(after(pair, own), gain, bias, proj_weight, tile_mask, 0)
    left_other = exchange(left_theirs, 1)

    by_a, by_b, partials = [], [], []
    for c in range(CHUNKS):
        *sums, next_a, next_b = partial_products(left_mine, left_other, first_a, first_b, panels[c], c)
        partials.append(sums)
        by_a.append([first_a, hop(next_a, 0)])
        by_b.append([first_b, hop(next_b, 1)])

    left_grads = []
    for t in range(2, n):
        for c in range(CHUNKS):
            value = by_a[c][-1]
            if t == n - 1 and c > 0:
                value = after(value, left_grads[c - 1])
            next_a, next_b = onward(value, by_b[c][-1], partials[c][n - t], partials[c][t], t, n)
            by_a[c].append(hop(next_a, 0))
            by_b[c].append(hop(next_b, 1))
            if t == n - 1:
                left_grads.append(left_products(own, by_a[c][: n - 1], by_b[c][: n - 1], panels[c], c))
    left_grad_other = [exchange(theirs, 1) for _, theirs in left_grads]
    ks = left_mine.shape[1]
    right_grad_other = []
    for c in range(CHUNKS):
        total = arrived_total(partials[c][0][:, ks:], by_a[c][-1][:, ks:], by_b[c][-1][:, ks:], n)
        right_grad_other.append(exchange(total.astype(jnp.bfloat16), 1))

    return tail(
        pair,
        gain,
        bias,
        proj_weight,
        tile_mask,
        [mine for mine, _ in left_grads],
        left_grad_other,
        [sums[0] for sums in partials],
        [v[-1] for v in by_a],
        [v[-1] for v in by_b],
        right_grad_other,
    )


def solution(mesh):
    placed = (P("row", "col", None), P("row", "col", None), P(), P(), P(), P())
    return jax.shard_map(
        shards, mesh=mesh, in_specs=placed, out_specs=P("row", "col", None), check_vma=False
    )
```

```python
import functools

import jax
import jax.numpy as jnp
from jax import lax
from jax.experimental import pallas as pl
from jax.experimental.pallas import tpu as pltpu
from jax.sharding import PartitionSpec as P

BLK = 128
CHUNKS = 2
STEP = 8
KEYS = 16
CORES = 2
VMEM_LIMIT = 18 * 1024 * 1024
PARAMS = pltpu.CompilerParams(vmem_limit_bytes=VMEM_LIMIT)
FRONT_COST = pl.CostEstimate(flops=1, bytes_accessed=18_000_000, transcendentals=0)
COST = pl.CostEstimate(flops=1, bytes_accessed=8_000_000, transcendentals=0)
BY_LAST = (((1,), (1,)), ((), ()))


def identity(size):
    return (
        lax.broadcasted_iota(jnp.int32, (size, size), 0) == lax.broadcasted_iota(jnp.int32, (size, size), 1)
    ).astype(jnp.bfloat16)


def column(vector_ref, rows):
    return jnp.broadcast_to(vector_ref[...], (rows, vector_ref.shape[1])).T


def unit_mask(mask_ref, rows, cols):
    row, col = lax.axis_index("row"), lax.axis_index("col")
    return mask_ref[(row * rows) // BLK, (col * cols) // BLK].astype(jnp.float32)


def in_hbm(*values):
    return [pltpu.with_memory_space_constraint(v, pltpu.HBM) for v in values]


def this_core():
    return lax.rem(lax.axis_index("col"), CORES)


def turn(pair, flipped, turned):
    flipped[...] = jnp.transpose(pair[...], (1, 0, 2))
    eye = identity(pair.shape[2])
    for key in range(pair.shape[1]):
        turned[key] = lax.dot_general(eye, flipped[key], BY_LAST, preferred_element_type=jnp.float32)


def normalize(values):
    centred = values - jnp.mean(values, axis=1, keepdims=True)
    inverse = lax.rsqrt(jnp.mean(centred * centred, axis=1, keepdims=True) + 1e-05)
    return centred * inverse, inverse


def set_columns(gain, bias, weight, gain_col, bias_col, weight_t):
    @pl.when(pl.program_id(0) == 0)
    def _():
        gain_col[...] = column(gain, gain_col.shape[1])
        bias_col[...] = column(bias, bias_col.shape[1])
        weight_t[...] = weight[...].astype(jnp.float32).T.astype(jnp.bfloat16)


def normalized(pair, gain_col, bias_col, flipped, turned, normed):
    turn(pair, flipped, turned)
    scaled, inverse = normalize(turned[...])
    normed[...] = (scaled * gain_col[...] + bias_col[...]).astype(jnp.bfloat16)
    return scaled, inverse


def split_channels(acts, whole, mine, theirs):
    half = mine.shape[0]
    whole[...] = jnp.transpose(acts[...], (1, 0, 2))
    core = this_core()
    mine[...] = whole[pl.ds(core * half, half)]
    theirs[...] = whole[pl.ds((1 - core) * half, half)]


def right_kernel(mask, pair, gain, bias, weight, mine, theirs, flipped, turned, normed, acts, whole, gain_col, bias_col, weight_t):
    rows, keys, _ = pair.shape
    hidden = acts.shape[1]
    set_columns(gain, bias, weight, gain_col, bias_col, weight_t)
    valid = unit_mask(mask, rows, pl.num_programs(0) * keys)
    normalized(pair, gain_col, bias_col, flipped, turned, normed)
    for key in range(keys):
        projected = jnp.dot(weight_t[...], normed[key], preferred_element_type=jnp.float32)
        acts[key] = (valid * jax.nn.sigmoid(projected[hidden:]) * projected[:hidden]).astype(jnp.bfloat16)
    split_channels(acts, whole, mine, theirs)


def left_forward_kernel(
    mask, pair, gain, bias, weight, mine, theirs, scaled_out, inverse_out, factors,
    flipped, turned, normed, acts, whole, gain_col, bias_col, weight_t,
):
    rows, keys, _ = pair.shape
    hidden = acts.shape[1]
    set_columns(gain, bias, weight, gain_col, bias_col, weight_t)
    valid = unit_mask(mask, rows, pl.num_programs(0) * keys)
    scaled, inverse = normalized(pair, gain_col, bias_col, flipped, turned, normed)
    scaled_out[...] = scaled.astype(jnp.bfloat16)
    inverse_out[...] = inverse
    for key in range(keys):
        projected = jnp.dot(weight_t[...], normed[key], preferred_element_type=jnp.float32)
        for side in range(2):
            first = 2 * side * hidden
            lin = projected[first : first + hidden]
            sig = jax.nn.sigmoid(projected[first + hidden : first + 2 * hidden])
            masked = valid * sig
            act = masked * lin
            if side == 0:
                acts[key] = act.astype(jnp.bfloat16)
            factors[key, first : first + hidden, :] = masked.astype(jnp.bfloat16)
            factors[key, first + hidden : first + 2 * hidden, :] = (act * (1.0 - sig)).astype(jnp.bfloat16)
    split_channels(acts, whole, mine, theirs)


def front(pair, gain, bias, proj_weight, tile_mask, right):
    rows, cols, chans = pair.shape
    width = proj_weight.shape[1]
    hidden = width // 4
    half = hidden // CORES
    used = width // 2 if right else width
    vector = pl.BlockSpec((1, chans), lambda g: (0, 0))
    by_key = lambda *shape: pl.BlockSpec((KEYS,) + shape, lambda g: (g, 0, 0))
    out_shape = [jax.ShapeDtypeStruct((half, cols, rows), jnp.bfloat16)] * 2
    out_specs = [pl.BlockSpec((half, KEYS, rows), lambda g: (0, g, 0))] * 2
    if not right:
        out_shape += [
            jax.ShapeDtypeStruct((cols, chans, rows), jnp.bfloat16),
            jax.ShapeDtypeStruct((cols, 1, rows), jnp.float32),
            jax.ShapeDtypeStruct((cols, width, rows), jnp.bfloat16),
        ]
        out_specs += [by_key(chans, rows), by_key(1, rows), by_key(width, rows)]
    return pl.pallas_call(
        right_kernel if right else left_forward_kernel,
        out_shape=out_shape,
        grid=(cols // KEYS,),
        in_specs=[
            pl.BlockSpec(memory_space=pltpu.SMEM),
            pl.BlockSpec((rows, KEYS, chans), lambda g: (0, g, 0)),
            vector,
            vector,
            pl.BlockSpec((chans, used), lambda g: (0, 1 if right else 0)),
        ],
        out_specs=out_specs,
        scratch_shapes=[
            pltpu.VMEM((KEYS, rows, chans), jnp.bfloat16),
            pltpu.VMEM((KEYS, chans, rows), jnp.float32),
            pltpu.VMEM((KEYS, chans, rows), jnp.bfloat16),
            pltpu.VMEM((KEYS, hidden, rows), jnp.bfloat16),
            pltpu.VMEM((hidden, KEYS, rows), jnp.bfloat16),
            pltpu.VMEM((chans, rows), jnp.float32),
            pltpu.VMEM((chans, rows), jnp.float32),
            pltpu.VMEM((used, chans), jnp.bfloat16),
        ],
        compiler_params=PARAMS,
        cost_estimate=FRONT_COST,
        name="right_front" if right else "left_front",
    )(tile_mask, *in_hbm(pair, gain, bias, proj_weight))


def pack_kernel(own, other, out):
    cols, half, _ = other.shape
    core = this_core()
    for block, place in ((own[:, pl.ds(pl.multiple_of(core * half, half), half), :], core), (other[...], 1 - core)):
        out[:, pl.ds(pl.multiple_of(place * cols, cols), cols), :] = jnp.transpose(block, (1, 0, 2))


def pack(own, other):
    cols, half, rows = other.shape
    return pl.pallas_call(
        pack_kernel,
        out_shape=jax.ShapeDtypeStruct((half, CORES * cols, rows), jnp.bfloat16),
        compiler_params=PARAMS,
        cost_estimate=COST,
        name="pack",
    )(own, other)


def chunk_spec(array, chans, chunk):
    first = chunk * chans // STEP if array.shape[0] > chans else 0
    return pl.BlockSpec((STEP,) + array.shape[1:], lambda g: (first + g, 0, 0))


def cut_kernel(*refs):
    count = len(refs) // 2
    for source, out in zip(refs[:count], refs[count:]):
        out[...] = source[...]


def cut(arrays, chunks):
    chans = arrays[0].shape[0] // CHUNKS
    shape = (chans,) + arrays[0].shape[1:]
    return pl.pallas_call(
        cut_kernel,
        out_shape=[jax.ShapeDtypeStruct(shape, jnp.bfloat16)] * len(arrays),
        grid=(chans // STEP,),
        in_specs=[chunk_spec(v, chans, c) for v, c in zip(arrays, chunks)],
        out_specs=[pl.BlockSpec((STEP,) + shape[1:], lambda g: (g, 0, 0))] * len(arrays),
        compiler_params=PARAMS,
        cost_estimate=FRONT_COST,
        name="cut",
    )(*arrays)


def lanes(n):
    row = lax.axis_index("row")
    even = lax.rem(row, 2) == 0
    return even, jnp.where(even, row + 1 < n, True), jnp.where(even, row > 0, row + 1 < n)


def onward(by_a, by_b, up_sums, down_sums, t, n):
    row = lax.axis_index("row")
    even, use_a, use_b = lanes(n)
    up = jnp.where(row < t, up_sums.astype(jnp.float32), 0.0)
    down = jnp.where(row >= n - t, down_sums.astype(jnp.float32), 0.0)
    out_a = jnp.where(use_b, by_b.astype(jnp.float32), 0.0) + jnp.where(even, up, down)
    out_b = jnp.where(use_a, by_a.astype(jnp.float32), 0.0) + jnp.where(even, down, up)
    return out_a.astype(jnp.bfloat16), out_b.astype(jnp.bfloat16)


def partial_kernel(n, left_mine, left_other, by_a, by_b, *refs):
    blocks, outs, (next_a, next_b, sums) = refs[:n], refs[n : 2 * n], refs[2 * n :]
    row, chip = lax.axis_index("row"), lax.axis_index("col") // CORES
    for c in range(STEP):
        lhs = jnp.concatenate((left_mine[c], left_other[c]), axis=0)
        for m, block in enumerate(blocks):
            away = lax.rem(jnp.bitwise_xor(chip, m) - row + n, n)
            sums[away, c] = lax.dot_general(lhs, block[c], BY_LAST, preferred_element_type=jnp.float32).astype(jnp.bfloat16)
    for s, out in enumerate(outs):
        out[...] = sums[s]
    next_a[...], next_b[...] = onward(by_a[...], by_b[...], sums[n - 1], sums[1], 1, n)


def partial_products(left_mine, left_other, by_a, by_b, blocks, chunk):
    rows = blocks[0].shape[1]
    ks, chans = left_mine.shape[1], left_mine.shape[0] // CHUNKS
    n = len(blocks)
    args = (left_mine, left_other, by_a, by_b, *blocks)
    return pl.pallas_call(
        functools.partial(partial_kernel, n),
        out_shape=[pltpu.HBM((chans, CORES * ks, rows), jnp.bfloat16)] * n
        + [jax.ShapeDtypeStruct((chans, CORES * ks, rows), jnp.bfloat16)] * 2,
        grid=(chans // STEP,),
        in_specs=[chunk_spec(v, chans, chunk) for v in args],
        out_specs=[pl.BlockSpec((STEP, CORES * ks, rows), lambda g: (g, 0, 0))] * (n + 2),
        scratch_shapes=[pltpu.VMEM((n, STEP, CORES * ks, rows), jnp.bfloat16)],
        compiler_params=PARAMS,
        cost_estimate=COST,
        name="right_partials",
    )(*args)


def left_kernel(n, own, *refs):
    by_a, by_b, refs = refs[: n - 1], refs[n - 1 : 2 * n - 2], refs[2 * n - 2 :]
    blocks, (mine, theirs, panel) = refs[:n], refs[n:]
    row, chip = lax.axis_index("row"), lax.axis_index("col") // CORES
    even = lanes(n)[0]
    ks = mine.shape[1]
    for c in range(STEP):
        for m, block in enumerate(blocks):
            panel[c, jnp.bitwise_xor(chip, m)] = block[c]
        acts, grads = [own[c]], [panel[c, row]]
        for s in range(1, n):
            from_above = jnp.where(even, by_a[s - 1][c], by_b[s - 1][c])
            from_below = jnp.where(even, by_b[n - s - 1][c], by_a[n - s - 1][c])
            acts.append(jnp.where(row + s < n, from_above, from_below))
            grads.append(panel[c, lax.rem(row + s, n)])
        out = jnp.dot(
            jnp.concatenate(acts, axis=1), jnp.concatenate(grads, axis=0), preferred_element_type=jnp.float32
        )
        mine[c] = out[:ks]
        theirs[c] = out[ks:].astype(jnp.bfloat16)


def left_products(own, by_a, by_b, blocks, chunk):
    chans, ks, rows = by_a[-1].shape
    n = len(blocks)
    out = pl.BlockSpec((STEP, ks // CORES, rows), lambda g: (g, 0, 0))
    args = (own, *by_a, *by_b, *blocks)
    return pl.pallas_call(
        functools.partial(left_kernel, n),
        out_shape=[
            jax.ShapeDtypeStruct((chans, ks // CORES, rows), jnp.float32),
            jax.ShapeDtypeStruct((chans, ks // CORES, rows), jnp.bfloat16),
        ],
        grid=(chans // STEP,),
        in_specs=[chunk_spec(v, chans, chunk) for v in args],
        out_specs=[out] * 2,
        scratch_shapes=[pltpu.VMEM((STEP, n, rows, rows), jnp.bfloat16)],
        compiler_params=PARAMS,
        cost_estimate=COST,
        name="left_products",
    )(*args)


def arrived_total(own, by_a, by_b, n):
    _, use_a, use_b = lanes(n)
    total = own.astype(jnp.float32) + jnp.where(use_a, by_a.astype(jnp.float32), 0.0)
    return total + jnp.where(use_b, by_b.astype(jnp.float32), 0.0)


def tail_kernel(n, scaled, inverse, factors, gain, weight, *refs):
    groups = [refs[i * CHUNKS : (i + 1) * CHUNKS] for i in range(6)]
    left_mine, left_other, partials, by_a, by_b, right_other = groups
    out, results, flipped, grads, right_flat, left_flat, gain_col = refs[6 * CHUNKS :]
    keys, chans, rows = scaled.shape
    hidden = weight.shape[1] // 4
    half = hidden // CORES
    part = half // CHUNKS
    core = this_core()

    @pl.when(pl.program_id(0) == 0)
    def _():
        gain_col[...] = column(gain, rows)

    def put(flat, owner, chunk, value):
        first = pl.multiple_of((owner * half + chunk * part) * keys, part * keys)
        flat[pl.ds(first, part * keys), :] = value.astype(jnp.float32).reshape(part * keys, rows)

    for chunk in range(CHUNKS):
        total = arrived_total(partials[chunk][...], by_a[chunk][...], by_b[chunk][...], n)
        put(right_flat, core, chunk, total)
        put(right_flat, 1 - core, chunk, right_other[chunk][...])
        put(left_flat, core, chunk, left_mine[chunk][...])
        put(left_flat, 1 - core, chunk, left_other[chunk][...])
    for key in range(keys):
        for side, source in enumerate((left_flat, right_flat)):
            grad = source[pl.ds(key, hidden, stride=keys), :]
            for i in (2 * side, 2 * side + 1):
                place = slice(i * hidden, (i + 1) * hidden)
                grads[key, place, :] = (grad * factors[key, place, :].astype(jnp.float32)).astype(jnp.bfloat16)
    for key in range(keys):
        scaled_key = scaled[key].astype(jnp.float32)
        scaled_grad = jnp.dot(weight[...], grads[key], preferred_element_type=jnp.float32) * gain_col[...]
        result = inverse[key] * (
            scaled_grad
            - jnp.mean(scaled_grad, axis=0, keepdims=True)
            - scaled_key * jnp.mean(scaled_grad * scaled_key, axis=0, keepdims=True)
        )
        results[key] = result.astype(jnp.bfloat16)
    eye = identity(rows)
    for key in range(keys):
        flipped[key] = lax.dot_general(eye, results[key], BY_LAST, preferred_element_type=jnp.float32).astype(jnp.bfloat16)
    out[...] = jnp.transpose(flipped[...], (1, 0, 2))


def tail(scaled, inverse, factors, gain, proj_weight, left_mine, left_other, partials, by_a, by_b, right_other):
    cols, chans, rows = scaled.shape
    width = proj_weight.shape[1]
    hidden = width // 4
    part = hidden // CORES // CHUNKS
    by_key = lambda *shape: pl.BlockSpec((KEYS,) + shape, lambda g: (g, 0, 0))
    return pl.pallas_call(
        functools.partial(tail_kernel, lax.axis_size("row")),
        out_shape=jax.ShapeDtypeStruct((rows, cols, chans), jnp.bfloat16),
        grid=(cols // KEYS,),
        in_specs=[
            by_key(chans, rows),
            by_key(1, rows),
            by_key(width, rows),
            pl.BlockSpec((1, chans), lambda g: (0, 0)),
            pl.BlockSpec((chans, width), lambda g: (0, 0)),
        ]
        + [pl.BlockSpec((part, KEYS, rows), lambda g: (0, g, 0))] * (6 * CHUNKS),
        out_specs=pl.BlockSpec((rows, KEYS, chans), lambda g: (0, g, 0)),
        scratch_shapes=[
            pltpu.VMEM((KEYS, chans, rows), jnp.bfloat16),
            pltpu.VMEM((KEYS, rows, chans), jnp.bfloat16),
            pltpu.VMEM((KEYS, width, rows), jnp.bfloat16),
            pltpu.VMEM((hidden * KEYS, rows), jnp.float32),
            pltpu.VMEM((hidden * KEYS, rows), jnp.float32),
            pltpu.VMEM((chans, rows), jnp.float32),
        ],
        compiler_params=PARAMS,
        cost_estimate=COST,
        name="tail",
    )(scaled, inverse, factors, gain, proj_weight, *left_mine, *left_other, *partials, *by_a, *by_b, *right_other)


def after(value, *others):
    return lax.optimization_barrier((value, others))[0]


def shards(pair, grad_x, norm_gain, norm_bias, proj_weight, tile_mask):
    n, n_col = lax.axis_size("row"), lax.axis_size("col")
    half = grad_x.shape[2] // CORES
    part = half // CHUNKS
    gain, bias = norm_gain[None, :], norm_bias[None, :]

    def exchange(value, mask):
        return lax.ppermute(value, "col", [(d, d ^ mask) for d in range(n_col)])

    def hop(value, first):
        pairs = {r: r + 1 for r in range(first, n - 1, 2)}
        pairs.update({above: r for r, above in pairs.items()})
        perm = [
            (r * n_col + d, pairs[r] * n_col + d if r in pairs else r * n_col + (d ^ 1)) for r in range(n) for d in range(n_col)
        ]
        return lax.ppermute(value, ("row", "col"), perm)

    raw = jnp.transpose(grad_x, (1, 2, 0))
    other = exchange(lax.dynamic_slice_in_dim(raw, (1 - this_core()) * half, half, 1), 1)
    packed = pack(raw, other)

    axes = {m: [1 << b for b in range(m.bit_length()) if m >> b & 1] for m in range(n_col // CORES)}
    whole = {m: exchange(packed, CORES * m) for m in axes if len(axes[m]) == 1}
    turns = [(m, c, axes[m][(c + 1) % 2]) for m in axes if len(axes[m]) == 2 for c in range(CHUNKS)]
    cuts = cut([whole[m ^ bit] for m, _, bit in turns], [c for _, c, _ in turns])
    relayed = {(m, c): exchange(value, CORES * bit) for (m, c, bit), value in zip(turns, cuts)}
    for m in axes:
        for c in range(CHUNKS if len(axes[m]) > 2 else 0):
            bit = axes[m][c % len(axes[m])]
            relayed[m, c] = exchange(relayed[m ^ bit, c], CORES * bit)
    whole[0] = packed
    panels = [[whole[m] if m in whole else relayed[m, c] for m in axes] for c in range(CHUNKS)]

    right_mine, right_theirs = front(after(pair, packed), gain, bias, proj_weight, tile_mask, True)
    right_other = [exchange(right_theirs[c * part : (c + 1) * part], 1) for c in range(CHUNKS)]
    own = jnp.concatenate((right_mine, jnp.concatenate(right_other)), axis=1)
    first_a, first_b = hop(own, 0), hop(own, 1)
    left_mine, left_theirs, *forward = front(after(pair, own), gain, bias, proj_weight, tile_mask, False)
    left_other = exchange(left_theirs, 1)

    by_a, by_b, partials = [], [], []
    for c in range(CHUNKS):
        *sums, next_a, next_b = partial_products(left_mine, left_other, first_a, first_b, panels[c], c)
        partials.append(sums)
        by_a.append([first_a, hop(next_a, 0)])
        by_b.append([first_b, hop(next_b, 1)])

    left_grads = []
    for t in range(2, n):
        for c in range(CHUNKS):
            value = by_a[c][-1]
            if t == n - 1 and c > 0:
                value = after(value, left_grads[c - 1])
            next_a, next_b = onward(value, by_b[c][-1], partials[c][n - t], partials[c][t], t, n)
            by_a[c].append(hop(next_a, 0))
            by_b[c].append(hop(next_b, 1))
            if t == n - 1:
                left_grads.append(left_products(own, by_a[c][: n - 1], by_b[c][: n - 1], panels[c], c))
    left_grad_other = [exchange(theirs, 1) for _, theirs in left_grads]
    ks = left_mine.shape[1]
    right_grad_other = []
    for c in range(CHUNKS):
        total = arrived_total(partials[c][0][:, ks:], by_a[c][-1][:, ks:], by_b[c][-1][:, ks:], n)
        right_grad_other.append(exchange(total.astype(jnp.bfloat16), 1))

    return tail(
        *forward,
        gain,
        proj_weight,
        [mine for mine, _ in left_grads],
        left_grad_other,
        [sums[0] for sums in partials],
        [v[-1] for v in by_a],
        [v[-1] for v in by_b],
        right_grad_other,
    )


def solution(mesh):
    placed = (P("row", "col", None), P("row", "col", None), P(), P(), P(), P())
    return jax.shard_map(
        shards, mesh=mesh, in_specs=placed, out_specs=P("row", "col", None), check_vma=False
    )
```

```python
import functools

import jax
import jax.numpy as jnp
from jax import lax
from jax.experimental import pallas as pl
from jax.experimental.pallas import tpu as pltpu
from jax.sharding import PartitionSpec as P

BLK = 128
CHUNKS = 2
STEP = 8
KEYS = 16
CORES = 2
VMEM_LIMIT = 18 * 1024 * 1024
PARAMS = pltpu.CompilerParams(vmem_limit_bytes=VMEM_LIMIT)
FRONT_COST = pl.CostEstimate(flops=1, bytes_accessed=18_000_000, transcendentals=0)
COST = pl.CostEstimate(flops=1, bytes_accessed=8_000_000, transcendentals=0)
BY_LAST = (((1,), (1,)), ((), ()))


def identity(size):
    return (
        lax.broadcasted_iota(jnp.int32, (size, size), 0) == lax.broadcasted_iota(jnp.int32, (size, size), 1)
    ).astype(jnp.bfloat16)


def column(vector_ref, rows):
    return jnp.broadcast_to(vector_ref[...], (rows, vector_ref.shape[1])).T


def unit_mask(mask_ref, rows, cols):
    row, col = lax.axis_index("row"), lax.axis_index("col")
    return mask_ref[(row * rows) // BLK, (col * cols) // BLK].astype(jnp.float32)


def in_hbm(*values):
    return [pltpu.with_memory_space_constraint(v, pltpu.HBM) for v in values]


def this_core():
    return lax.rem(lax.axis_index("col"), CORES)


def turn(pair, flipped, turned):
    flipped[...] = jnp.transpose(pair[...], (1, 0, 2))
    eye = identity(pair.shape[2])
    for key in range(pair.shape[1]):
        turned[key] = lax.dot_general(eye, flipped[key], BY_LAST, preferred_element_type=jnp.float32)


def normalize(values):
    centred = values - jnp.mean(values, axis=1, keepdims=True)
    inverse = lax.rsqrt(jnp.mean(centred * centred, axis=1, keepdims=True) + 1e-05)
    return centred * inverse, inverse


def set_columns(gain, bias, weight, gain_col, bias_col, weight_t):
    @pl.when(pl.program_id(0) == 0)
    def _():
        gain_col[...] = column(gain, gain_col.shape[1])
        bias_col[...] = column(bias, bias_col.shape[1])
        weight_t[...] = weight[...].astype(jnp.float32).T.astype(jnp.bfloat16)


def normalized(pair, gain_col, bias_col, flipped, turned, normed):
    turn(pair, flipped, turned)
    scaled, inverse = normalize(turned[...])
    normed[...] = (scaled * gain_col[...] + bias_col[...]).astype(jnp.bfloat16)
    return scaled, inverse


def split_channels(acts, whole, mine, theirs):
    half = mine.shape[0]
    whole[...] = jnp.transpose(acts[...], (1, 0, 2))
    core = this_core()
    mine[...] = whole[pl.ds(core * half, half)]
    theirs[...] = whole[pl.ds((1 - core) * half, half)]


def right_kernel(mask, pair, gain, bias, weight, mine, theirs, flipped, turned, normed, acts, whole, gain_col, bias_col, weight_t):
    rows, keys, _ = pair.shape
    hidden = acts.shape[1]
    set_columns(gain, bias, weight, gain_col, bias_col, weight_t)
    valid = unit_mask(mask, rows, pl.num_programs(0) * keys)
    normalized(pair, gain_col, bias_col, flipped, turned, normed)
    for key in range(keys):
        projected = jnp.dot(weight_t[...], normed[key], preferred_element_type=jnp.float32)
        acts[key] = (valid * jax.nn.sigmoid(projected[hidden:]) * projected[:hidden]).astype(jnp.bfloat16)
    split_channels(acts, whole, mine, theirs)


def last_rows(hidden):
    part = hidden // CORES // CHUNKS
    return [((2 + kind) * hidden + (core * CHUNKS + CHUNKS - 1) * part, part) for kind in range(2) for core in range(CORES)]


def left_forward_kernel(
    mask, pair, gain, bias, weight, mine, theirs, scaled_out, inverse_out, factors, last,
    flipped, turned, normed, acts, whole, gain_col, bias_col, weight_t,
):
    rows, keys, _ = pair.shape
    hidden = acts.shape[1]
    set_columns(gain, bias, weight, gain_col, bias_col, weight_t)
    valid = unit_mask(mask, rows, pl.num_programs(0) * keys)
    scaled, inverse = normalized(pair, gain_col, bias_col, flipped, turned, normed)
    scaled_out[...] = scaled.astype(jnp.bfloat16)
    inverse_out[...] = inverse
    for key in range(keys):
        projected = jnp.dot(weight_t[...], normed[key], preferred_element_type=jnp.float32)
        for side in range(2):
            first = 2 * side * hidden
            lin = projected[first : first + hidden]
            sig = jax.nn.sigmoid(projected[first + hidden : first + 2 * hidden])
            masked = valid * sig
            act = masked * lin
            if side == 0:
                acts[key] = act.astype(jnp.bfloat16)
            factors[key, first : first + hidden, :] = masked.astype(jnp.bfloat16)
            factors[key, first + hidden : first + 2 * hidden, :] = (act * (1.0 - sig)).astype(jnp.bfloat16)
    for i, (first, size) in enumerate(last_rows(hidden)):
        last[:, i * size : (i + 1) * size, :] = factors[:, first : first + size, :]
    split_channels(acts, whole, mine, theirs)


def front(pair, gain, bias, proj_weight, tile_mask, right):
    rows, cols, chans = pair.shape
    width = proj_weight.shape[1]
    hidden = width // 4
    half = hidden // CORES
    used = width // 2 if right else width
    vector = pl.BlockSpec((1, chans), lambda g: (0, 0))
    by_key = lambda *shape: pl.BlockSpec((KEYS,) + shape, lambda g: (g, 0, 0))
    out_shape = [jax.ShapeDtypeStruct((half, cols, rows), jnp.bfloat16)] * 2
    out_specs = [pl.BlockSpec((half, KEYS, rows), lambda g: (0, g, 0))] * 2
    if not right:
        out_shape += [
            jax.ShapeDtypeStruct((cols, chans, rows), jnp.bfloat16),
            jax.ShapeDtypeStruct((cols, 1, rows), jnp.float32),
            jax.ShapeDtypeStruct((cols, width, rows), jnp.bfloat16),
            jax.ShapeDtypeStruct((cols, 2 * hidden // CHUNKS, rows), jnp.bfloat16),
        ]
        out_specs += [by_key(chans, rows), by_key(1, rows), by_key(width, rows), by_key(2 * hidden // CHUNKS, rows)]
    return pl.pallas_call(
        right_kernel if right else left_forward_kernel,
        out_shape=out_shape,
        grid=(cols // KEYS,),
        in_specs=[
            pl.BlockSpec(memory_space=pltpu.SMEM),
            pl.BlockSpec((rows, KEYS, chans), lambda g: (0, g, 0)),
            vector,
            vector,
            pl.BlockSpec((chans, used), lambda g: (0, 1 if right else 0)),
        ],
        out_specs=out_specs,
        scratch_shapes=[
            pltpu.VMEM((KEYS, rows, chans), jnp.bfloat16),
            pltpu.VMEM((KEYS, chans, rows), jnp.float32),
            pltpu.VMEM((KEYS, chans, rows), jnp.bfloat16),
            pltpu.VMEM((KEYS, hidden, rows), jnp.bfloat16),
            pltpu.VMEM((hidden, KEYS, rows), jnp.bfloat16),
            pltpu.VMEM((chans, rows), jnp.float32),
            pltpu.VMEM((chans, rows), jnp.float32),
            pltpu.VMEM((used, chans), jnp.bfloat16),
        ],
        compiler_params=PARAMS,
        cost_estimate=FRONT_COST,
        name="right_front" if right else "left_front",
    )(tile_mask, *in_hbm(pair, gain, bias, proj_weight))


def pack_kernel(own, other, out, mine, sem):
    cols, half, _ = other.shape
    core = this_core()
    copy = pltpu.make_async_copy(own.at[:, pl.ds(pl.multiple_of(core * half, half), half), :], mine, sem)
    copy.start()
    out[:, pl.ds(pl.multiple_of((1 - core) * cols, cols), cols), :] = jnp.transpose(other[...], (1, 0, 2))
    copy.wait()
    out[:, pl.ds(pl.multiple_of(core * cols, cols), cols), :] = jnp.transpose(mine[...], (1, 0, 2))


def pack(own, other):
    cols, half, rows = other.shape
    return pl.pallas_call(
        pack_kernel,
        out_shape=jax.ShapeDtypeStruct((half, CORES * cols, rows), jnp.bfloat16),
        in_specs=[pl.BlockSpec(memory_space=pl.ANY), pl.BlockSpec(memory_space=pltpu.VMEM)],
        scratch_shapes=[pltpu.VMEM((cols, half, rows), jnp.bfloat16), pltpu.SemaphoreType.DMA],
        compiler_params=PARAMS,
        cost_estimate=COST,
        name="pack",
    )(*in_hbm(own), other)


def chunk_spec(array, chans, chunk):
    first = chunk * chans // STEP if array.shape[0] > chans else 0
    return pl.BlockSpec((STEP,) + array.shape[1:], lambda g: (first + g, 0, 0))


def cut_kernel(*refs):
    count = len(refs) // 2
    for source, out in zip(refs[:count], refs[count:]):
        out[...] = source[...]


def cut(arrays, chunks):
    chans = arrays[0].shape[0] // CHUNKS
    shape = (chans,) + arrays[0].shape[1:]
    return pl.pallas_call(
        cut_kernel,
        out_shape=[jax.ShapeDtypeStruct(shape, jnp.bfloat16)] * len(arrays),
        grid=(chans // STEP,),
        in_specs=[chunk_spec(v, chans, c) for v, c in zip(arrays, chunks)],
        out_specs=[pl.BlockSpec((STEP,) + shape[1:], lambda g: (g, 0, 0))] * len(arrays),
        compiler_params=PARAMS,
        cost_estimate=FRONT_COST,
        name="cut",
    )(*arrays)


def lanes(n):
    row = lax.axis_index("row")
    even = lax.rem(row, 2) == 0
    return even, jnp.where(even, row + 1 < n, True), jnp.where(even, row > 0, row + 1 < n)


def onward(by_a, by_b, up_sums, down_sums, t, n):
    row = lax.axis_index("row")
    even, use_a, use_b = lanes(n)
    up = jnp.where(row < t, up_sums.astype(jnp.float32), 0.0)
    down = jnp.where(row >= n - t, down_sums.astype(jnp.float32), 0.0)
    out_a = jnp.where(use_b, by_b.astype(jnp.float32), 0.0) + jnp.where(even, up, down)
    out_b = jnp.where(use_a, by_a.astype(jnp.float32), 0.0) + jnp.where(even, down, up)
    return out_a.astype(jnp.bfloat16), out_b.astype(jnp.bfloat16)


def partial_kernel(n, left_mine, left_other, by_a, by_b, *refs):
    blocks, outs, (next_a, next_b, sums) = refs[:n], refs[n : 2 * n], refs[2 * n :]
    row, chip = lax.axis_index("row"), lax.axis_index("col") // CORES
    for c in range(STEP):
        lhs = jnp.concatenate((left_mine[c], left_other[c]), axis=0)
        for m, block in enumerate(blocks):
            away = lax.rem(jnp.bitwise_xor(chip, m) - row + n, n)
            sums[away, c] = lax.dot_general(lhs, block[c], BY_LAST, preferred_element_type=jnp.float32).astype(jnp.bfloat16)
    for s, out in enumerate(outs):
        out[...] = sums[s]
    next_a[...], next_b[...] = onward(by_a[...], by_b[...], sums[n - 1], sums[1], 1, n)


def partial_products(left_mine, left_other, by_a, by_b, blocks, chunk):
    rows = blocks[0].shape[1]
    ks, chans = left_mine.shape[1], left_mine.shape[0] // CHUNKS
    n = len(blocks)
    args = (left_mine, left_other, by_a, by_b, *blocks)
    return pl.pallas_call(
        functools.partial(partial_kernel, n),
        out_shape=[pltpu.HBM((chans, CORES * ks, rows), jnp.bfloat16)] * n
        + [jax.ShapeDtypeStruct((chans, CORES * ks, rows), jnp.bfloat16)] * 2,
        grid=(chans // STEP,),
        in_specs=[chunk_spec(v, chans, chunk) for v in args],
        out_specs=[pl.BlockSpec((STEP, CORES * ks, rows), lambda g: (g, 0, 0))] * (n + 2),
        scratch_shapes=[pltpu.VMEM((n, STEP, CORES * ks, rows), jnp.bfloat16)],
        compiler_params=PARAMS,
        cost_estimate=COST,
        name="right_partials",
    )(*args)


def left_kernel(n, own, *refs):
    by_a, by_b, refs = refs[: n - 1], refs[n - 1 : 2 * n - 2], refs[2 * n - 2 :]
    blocks, (mine, theirs, panel) = refs[:n], refs[n:]
    row, chip = lax.axis_index("row"), lax.axis_index("col") // CORES
    even = lanes(n)[0]
    ks = mine.shape[1]
    for c in range(STEP):
        for m, block in enumerate(blocks):
            panel[c, jnp.bitwise_xor(chip, m)] = block[c]
        acts, grads = [own[c]], [panel[c, row]]
        for s in range(1, n):
            from_above = jnp.where(even, by_a[s - 1][c], by_b[s - 1][c])
            from_below = jnp.where(even, by_b[n - s - 1][c], by_a[n - s - 1][c])
            acts.append(jnp.where(row + s < n, from_above, from_below))
            grads.append(panel[c, lax.rem(row + s, n)])
        out = jnp.dot(
            jnp.concatenate(acts, axis=1), jnp.concatenate(grads, axis=0), preferred_element_type=jnp.float32
        )
        mine[c] = out[:ks]
        theirs[c] = out[ks:].astype(jnp.bfloat16)


def left_products(own, by_a, by_b, blocks, chunk):
    chans, ks, rows = by_a[-1].shape
    n = len(blocks)
    out = pl.BlockSpec((STEP, ks // CORES, rows), lambda g: (g, 0, 0))
    args = (own, *by_a, *by_b, *blocks)
    return pl.pallas_call(
        functools.partial(left_kernel, n),
        out_shape=[
            jax.ShapeDtypeStruct((chans, ks // CORES, rows), jnp.float32),
            jax.ShapeDtypeStruct((chans, ks // CORES, rows), jnp.bfloat16),
        ],
        grid=(chans // STEP,),
        in_specs=[chunk_spec(v, chans, chunk) for v in args],
        out_specs=[out] * 2,
        scratch_shapes=[pltpu.VMEM((STEP, n, rows, rows), jnp.bfloat16)],
        compiler_params=PARAMS,
        cost_estimate=COST,
        name="left_products",
    )(*args)


def arrived_total(own, by_a, by_b, n):
    _, use_a, use_b = lanes(n)
    total = own.astype(jnp.float32) + jnp.where(use_a, by_a.astype(jnp.float32), 0.0)
    return total + jnp.where(use_b, by_b.astype(jnp.float32), 0.0)


def put(flat, owner, value):
    size = value.shape[0] * value.shape[1]
    flat[pl.ds(pl.multiple_of(owner * size, size), size), :] = value.astype(jnp.float32).reshape(size, value.shape[2])


def known_kernel(n, factors, weight, *refs):
    known = CHUNKS - 1
    left_mine, left_other = refs[:CHUNKS], refs[CHUNKS : 2 * CHUNKS]
    partials, by_a, by_b, right_other = (refs[2 * CHUNKS + i * known : 2 * CHUNKS + (i + 1) * known] for i in range(4))
    out, grads, *flats = refs[2 * CHUNKS + 4 * known :]
    keys, width, _ = factors.shape
    hidden = width // 4
    part = hidden // CORES // CHUNKS
    core = this_core()

    @pl.when(pl.program_id(0) == 0)
    def _():
        grads[...] = jnp.zeros_like(grads)

    for chunk in range(CHUNKS):
        put(flats[chunk], core, left_mine[chunk][...])
        put(flats[chunk], 1 - core, left_other[chunk][...])
    for chunk in range(known):
        put(flats[CHUNKS + chunk], core, arrived_total(partials[chunk][...], by_a[chunk][...], by_b[chunk][...], n))
        put(flats[CHUNKS + chunk], 1 - core, right_other[chunk][...])
    for key in range(keys):
        for i, flat in enumerate(flats):
            side, chunk = divmod(i, CHUNKS)
            grad = flat[pl.ds(key, CORES * part, stride=keys), :]
            for owner in range(CORES):
                for kind in range(2):
                    first = (2 * side + kind) * hidden + (owner * CHUNKS + chunk) * part
                    place = slice(first, first + part)
                    factor = factors[key, place, :].astype(jnp.float32)
                    grads[key, place, :] = (grad[owner * part : (owner + 1) * part] * factor).astype(jnp.bfloat16)
    for key in range(keys):
        out[key] = jnp.dot(weight[...], grads[key], preferred_element_type=jnp.float32)


def known(factors, proj_weight, left_mine, left_other, partials, by_a, by_b, right_other):
    cols, width, rows = factors.shape
    chans, hidden = proj_weight.shape[0], width // 4
    part = hidden // CORES // CHUNKS
    by_key = lambda *shape: pl.BlockSpec((KEYS,) + shape, lambda g: (g, 0, 0))
    args = (*left_mine, *left_other, *partials, *by_a, *by_b, *right_other)
    return pl.pallas_call(
        functools.partial(known_kernel, lax.axis_size("row")),
        out_shape=jax.ShapeDtypeStruct((cols, chans, rows), jnp.float32),
        grid=(cols // KEYS,),
        in_specs=[by_key(width, rows), pl.BlockSpec((chans, width), lambda g: (0, 0))]
        + [pl.BlockSpec((part, KEYS, rows), lambda g: (0, g, 0))] * len(args),
        out_specs=by_key(chans, rows),
        scratch_shapes=[pltpu.VMEM((KEYS, width, rows), jnp.bfloat16)]
        + [pltpu.VMEM((CORES * part * KEYS, rows), jnp.float32)] * (2 * CHUNKS - 1),
        compiler_params=PARAMS,
        cost_estimate=COST,
        name="known",
    )(factors, proj_weight, *args)


def tail_kernel(n, base, scaled, inverse, last, gain, weight, partials, by_a, by_b, right_other, out, results, flipped, grads, flat, gain_col):
    keys, chans, rows = scaled.shape
    hidden = weight.shape[1] // 4
    core = this_core()

    @pl.when(pl.program_id(0) == 0)
    def _():
        gain_col[...] = column(gain, rows)
        grads[...] = jnp.zeros_like(grads)

    put(flat, core, arrived_total(partials[...], by_a[...], by_b[...], n))
    put(flat, 1 - core, right_other[...])
    places = last_rows(hidden)
    for key in range(keys):
        grad = flat[pl.ds(key, 2 * hidden // len(places) // CHUNKS * CORES, stride=keys), :]
        for i, (first, size) in enumerate(places):
            factor = last[key, i * size : (i + 1) * size, :].astype(jnp.float32)
            owner = i % CORES
            grads[key, first : first + size, :] = (grad[owner * size : (owner + 1) * size] * factor).astype(jnp.bfloat16)
    for key in range(keys):
        scaled_key = scaled[key].astype(jnp.float32)
        added = jnp.dot(weight[...], grads[key], preferred_element_type=jnp.float32)
        scaled_grad = (base[key] + added) * gain_col[...]
        result = inverse[key] * (
            scaled_grad
            - jnp.mean(scaled_grad, axis=0, keepdims=True)
            - scaled_key * jnp.mean(scaled_grad * scaled_key, axis=0, keepdims=True)
        )
        results[key] = result.astype(jnp.bfloat16)
    eye = identity(rows)
    for key in range(keys):
        flipped[key] = lax.dot_general(eye, results[key], BY_LAST, preferred_element_type=jnp.float32).astype(jnp.bfloat16)
    out[...] = jnp.transpose(flipped[...], (1, 0, 2))


def tail(base, scaled, inverse, last, gain, proj_weight, partials, by_a, by_b, right_other):
    cols, chans, rows = scaled.shape
    width = proj_weight.shape[1]
    part = width // 4 // CORES // CHUNKS
    by_key = lambda *shape: pl.BlockSpec((KEYS,) + shape, lambda g: (g, 0, 0))
    return pl.pallas_call(
        functools.partial(tail_kernel, lax.axis_size("row")),
        out_shape=jax.ShapeDtypeStruct((rows, cols, chans), jnp.bfloat16),
        grid=(cols // KEYS,),
        in_specs=[
            by_key(chans, rows),
            by_key(chans, rows),
            by_key(1, rows),
            by_key(last.shape[1], rows),
            pl.BlockSpec((1, chans), lambda g: (0, 0)),
            pl.BlockSpec((chans, width), lambda g: (0, 0)),
        ]
        + [pl.BlockSpec((part, KEYS, rows), lambda g: (0, g, 0))] * 4,
        out_specs=pl.BlockSpec((rows, KEYS, chans), lambda g: (0, g, 0)),
        scratch_shapes=[
            pltpu.VMEM((KEYS, chans, rows), jnp.bfloat16),
            pltpu.VMEM((KEYS, rows, chans), jnp.bfloat16),
            pltpu.VMEM((KEYS, width, rows), jnp.bfloat16),
            pltpu.VMEM((CORES * part * KEYS, rows), jnp.float32),
            pltpu.VMEM((chans, rows), jnp.float32),
        ],
        compiler_params=PARAMS,
        cost_estimate=COST,
        name="tail",
    )(base, scaled, inverse, last, gain, proj_weight, partials, by_a, by_b, right_other)


def after(value, *others):
    return lax.optimization_barrier((value, others))[0]


def shards(pair, grad_x, norm_gain, norm_bias, proj_weight, tile_mask):
    n, n_col = lax.axis_size("row"), lax.axis_size("col")
    half = grad_x.shape[2] // CORES
    part = half // CHUNKS
    gain, bias = norm_gain[None, :], norm_bias[None, :]

    def exchange(value, mask):
        return lax.ppermute(value, "col", [(d, d ^ mask) for d in range(n_col)])

    def hop(value, first):
        pairs = {r: r + 1 for r in range(first, n - 1, 2)}
        pairs.update({above: r for r, above in pairs.items()})
        perm = [
            (r * n_col + d, pairs[r] * n_col + d if r in pairs else r * n_col + (d ^ 1)) for r in range(n) for d in range(n_col)
        ]
        return lax.ppermute(value, ("row", "col"), perm)

    raw = jnp.transpose(grad_x, (1, 2, 0))
    other = exchange(lax.dynamic_slice_in_dim(raw, (1 - this_core()) * half, half, 1), 1)
    packed = pack(raw, other)

    axes = {m: [1 << b for b in range(m.bit_length()) if m >> b & 1] for m in range(n_col // CORES)}
    whole = {m: exchange(packed, CORES * m) for m in axes if len(axes[m]) == 1}
    turns = [(m, c, axes[m][(c + 1) % 2]) for m in axes if len(axes[m]) == 2 for c in range(CHUNKS)]
    cuts = cut([whole[m ^ bit] for m, _, bit in turns], [c for _, c, _ in turns])
    relayed = {(m, c): exchange(value, CORES * bit) for (m, c, bit), value in zip(turns, cuts)}
    for m in axes:
        for c in range(CHUNKS if len(axes[m]) > 2 else 0):
            bit = axes[m][c % len(axes[m])]
            relayed[m, c] = exchange(relayed[m ^ bit, c], CORES * bit)
    whole[0] = packed
    panels = [[whole[m] if m in whole else relayed[m, c] for m in axes] for c in range(CHUNKS)]

    right_mine, right_theirs = front(after(pair, packed), gain, bias, proj_weight, tile_mask, True)
    right_other = [exchange(right_theirs[c * part : (c + 1) * part], 1) for c in range(CHUNKS)]
    own = jnp.concatenate((right_mine, jnp.concatenate(right_other)), axis=1)
    first_a, first_b = hop(own, 0), hop(own, 1)
    left_mine, left_theirs, *forward = front(after(pair, own), gain, bias, proj_weight, tile_mask, False)
    left_other = exchange(left_theirs, 1)

    by_a, by_b, partials = [], [], []
    for c in range(CHUNKS):
        *sums, next_a, next_b = partial_products(left_mine, left_other, first_a, first_b, panels[c], c)
        partials.append(sums)
        by_a.append([first_a, hop(next_a, 0)])
        by_b.append([first_b, hop(next_b, 1)])

    left_grads = []
    for t in range(2, n):
        for c in range(CHUNKS):
            value = by_a[c][-1]
            if t == n - 1 and c > 0:
                value = after(value, left_grads[c - 1])
            next_a, next_b = onward(value, by_b[c][-1], partials[c][n - t], partials[c][t], t, n)
            by_a[c].append(hop(next_a, 0))
            by_b[c].append(hop(next_b, 1))
            if t == n - 1:
                left_grads.append(left_products(own, by_a[c][: n - 1], by_b[c][: n - 1], panels[c], c))
    left_grad_other = [exchange(theirs, 1) for _, theirs in left_grads]
    ks = left_mine.shape[1]
    scaled, inverse, factors, last = forward
    own_sums, last_a, last_b = [sums[0] for sums in partials], [v[-1] for v in by_a], [v[-1] for v in by_b]
    right_grad_other = []
    for c in range(CHUNKS):
        value = own_sums[c]
        if c == CHUNKS - 1:
            base = known(
                factors,
                proj_weight,
                [mine for mine, _ in left_grads],
                left_grad_other,
                own_sums[:c],
                last_a[:c],
                last_b[:c],
                right_grad_other,
            )
            value = after(value, base)
        total = arrived_total(value[:, ks:], last_a[c][:, ks:], last_b[c][:, ks:], n)
        right_grad_other.append(exchange(total.astype(jnp.bfloat16), 1))
    return tail(
        base, scaled, inverse, last, gain, proj_weight, own_sums[-1], last_a[-1], last_b[-1], right_grad_other[-1]
    )


def solution(mesh):
    placed = (P("row", "col", None), P("row", "col", None), P(), P(), P(), P())
    return jax.shard_map(
        shards, mesh=mesh, in_specs=placed, out_specs=P("row", "col", None), check_vma=False
    )
```

```python
import functools

import jax
import jax.numpy as jnp
from jax import lax
from jax.experimental import pallas as pl
from jax.experimental.pallas import tpu as pltpu
from jax.sharding import PartitionSpec as P

BLK = 128
CHUNKS = 2
STEP = 8
KEYS = 16
CORES = 2
VMEM_LIMIT = 18 * 1024 * 1024
PARAMS = pltpu.CompilerParams(vmem_limit_bytes=VMEM_LIMIT)
FRONT_COST = pl.CostEstimate(flops=1, bytes_accessed=18_000_000, transcendentals=0)
COST = pl.CostEstimate(flops=1, bytes_accessed=8_000_000, transcendentals=0)
WHOLE = pl.BlockSpec(memory_space=pltpu.VMEM)
BY_LAST = (((1,), (1,)), ((), ()))


def identity(size):
    return (
        lax.broadcasted_iota(jnp.int32, (size, size), 0) == lax.broadcasted_iota(jnp.int32, (size, size), 1)
    ).astype(jnp.bfloat16)


def column(vector_ref, rows):
    return jnp.broadcast_to(vector_ref[...], (rows, vector_ref.shape[1])).T


def unit_mask(mask_ref, rows, cols):
    row, col = lax.axis_index("row"), lax.axis_index("col")
    return mask_ref[(row * rows) // BLK, (col * cols) // BLK].astype(jnp.float32)


def in_hbm(*values):
    return [pltpu.with_memory_space_constraint(v, pltpu.HBM) for v in values]


def this_core():
    return lax.rem(lax.axis_index("col"), CORES)


def turn(pair, flipped, turned):
    flipped[...] = jnp.transpose(pair[...], (1, 0, 2))
    eye = identity(pair.shape[2])
    for key in range(pair.shape[1]):
        turned[key] = lax.dot_general(eye, flipped[key], BY_LAST, preferred_element_type=jnp.float32)


def normalize(values):
    centred = values - jnp.mean(values, axis=1, keepdims=True)
    inverse = lax.rsqrt(jnp.mean(centred * centred, axis=1, keepdims=True) + 1e-05)
    return centred * inverse, inverse


def set_columns(gain, bias, weight, gain_col, bias_col, weight_t):
    @pl.when(pl.program_id(0) == 0)
    def _():
        gain_col[...] = column(gain, gain_col.shape[1])
        bias_col[...] = column(bias, bias_col.shape[1])
        weight_t[...] = weight[...].astype(jnp.float32).T.astype(jnp.bfloat16)


def normalized(pair, gain_col, bias_col, flipped, turned, normed):
    turn(pair, flipped, turned)
    scaled, inverse = normalize(turned[...])
    normed[...] = (scaled * gain_col[...] + bias_col[...]).astype(jnp.bfloat16)
    return scaled, inverse


def split_channels(acts, whole, mine, theirs):
    half = mine.shape[0]
    whole[...] = jnp.transpose(acts[...], (1, 0, 2))
    core = this_core()
    mine[...] = whole[pl.ds(core * half, half)]
    theirs[...] = whole[pl.ds((1 - core) * half, half)]


def right_kernel(mask, pair, gain, bias, weight, mine, theirs, flipped, turned, normed, acts, whole, gain_col, bias_col, weight_t):
    rows, keys, _ = pair.shape
    hidden = acts.shape[1]
    set_columns(gain, bias, weight, gain_col, bias_col, weight_t)
    valid = unit_mask(mask, rows, pl.num_programs(0) * keys)
    normalized(pair, gain_col, bias_col, flipped, turned, normed)
    for key in range(keys):
        projected = jnp.dot(weight_t[...], normed[key], preferred_element_type=jnp.float32)
        acts[key] = (valid * jax.nn.sigmoid(projected[hidden:]) * projected[:hidden]).astype(jnp.bfloat16)
    split_channels(acts, whole, mine, theirs)


def last_rows(hidden):
    part = hidden // CORES // CHUNKS
    return [((2 + kind) * hidden + (core * CHUNKS + CHUNKS - 1) * part, part) for kind in range(2) for core in range(CORES)]


def left_forward_kernel(
    mask, pair, gain, bias, weight, mine, theirs, scaled_out, inverse_out, factors, last,
    flipped, turned, normed, acts, whole, gain_col, bias_col, weight_t,
):
    rows, keys, _ = pair.shape
    hidden = acts.shape[1]
    set_columns(gain, bias, weight, gain_col, bias_col, weight_t)
    valid = unit_mask(mask, rows, pl.num_programs(0) * keys)
    scaled, inverse = normalized(pair, gain_col, bias_col, flipped, turned, normed)
    scaled_out[...] = scaled.astype(jnp.bfloat16)
    inverse_out[...] = inverse
    for key in range(keys):
        projected = jnp.dot(weight_t[...], normed[key], preferred_element_type=jnp.float32)
        for side in range(2):
            first = 2 * side * hidden
            lin = projected[first : first + hidden]
            sig = jax.nn.sigmoid(projected[first + hidden : first + 2 * hidden])
            masked = valid * sig
            act = masked * lin
            if side == 0:
                acts[key] = act.astype(jnp.bfloat16)
            factors[key, first : first + hidden, :] = masked.astype(jnp.bfloat16)
            factors[key, first + hidden : first + 2 * hidden, :] = (act * (1.0 - sig)).astype(jnp.bfloat16)
    for i, (first, size) in enumerate(last_rows(hidden)):
        last[:, i * size : (i + 1) * size, :] = factors[:, first : first + size, :]
    split_channels(acts, whole, mine, theirs)


def front(pair, gain, bias, proj_weight, tile_mask, right):
    rows, cols, chans = pair.shape
    width = proj_weight.shape[1]
    hidden = width // 4
    half = hidden // CORES
    used = width // 2 if right else width
    vector = pl.BlockSpec((1, chans), lambda g: (0, 0))
    by_key = lambda *shape: pl.BlockSpec((KEYS,) + shape, lambda g: (g, 0, 0))
    out_shape = [jax.ShapeDtypeStruct((half, cols, rows), jnp.bfloat16)] * 2
    out_specs = [pl.BlockSpec((half, KEYS, rows), lambda g: (0, g, 0))] * 2
    if not right:
        out_shape += [
            jax.ShapeDtypeStruct((cols, chans, rows), jnp.bfloat16),
            jax.ShapeDtypeStruct((cols, 1, rows), jnp.float32),
            jax.ShapeDtypeStruct((cols, width, rows), jnp.bfloat16),
            jax.ShapeDtypeStruct((cols, 2 * hidden // CHUNKS, rows), jnp.bfloat16),
        ]
        out_specs += [by_key(chans, rows), by_key(1, rows), by_key(width, rows), by_key(2 * hidden // CHUNKS, rows)]
    return pl.pallas_call(
        right_kernel if right else left_forward_kernel,
        out_shape=out_shape,
        grid=(cols // KEYS,),
        in_specs=[
            pl.BlockSpec(memory_space=pltpu.SMEM),
            pl.BlockSpec((rows, KEYS, chans), lambda g: (0, g, 0)),
            vector,
            vector,
            pl.BlockSpec((chans, used), lambda g: (0, 1 if right else 0)),
        ],
        out_specs=out_specs,
        scratch_shapes=[
            pltpu.VMEM((KEYS, rows, chans), jnp.bfloat16),
            pltpu.VMEM((KEYS, chans, rows), jnp.float32),
            pltpu.VMEM((KEYS, chans, rows), jnp.bfloat16),
            pltpu.VMEM((KEYS, hidden, rows), jnp.bfloat16),
            pltpu.VMEM((hidden, KEYS, rows), jnp.bfloat16),
            pltpu.VMEM((chans, rows), jnp.float32),
            pltpu.VMEM((chans, rows), jnp.float32),
            pltpu.VMEM((used, chans), jnp.bfloat16),
        ],
        compiler_params=PARAMS,
        cost_estimate=FRONT_COST,
        name="right_front" if right else "left_front",
    )(tile_mask, *in_hbm(pair, gain, bias, proj_weight))


def half_kernel(theirs, raw, out, sem):
    half = out.shape[1]
    core = this_core()
    first = pl.multiple_of((1 - core if theirs else core) * half, half)
    copy = pltpu.make_async_copy(raw.at[:, pl.ds(first, half), :], out, sem)
    copy.start()
    copy.wait()


def take_half(raw, theirs):
    cols, hidden, rows = raw.shape
    return pl.pallas_call(
        functools.partial(half_kernel, theirs),
        out_shape=jax.ShapeDtypeStruct((cols, hidden // CORES, rows), raw.dtype),
        in_specs=[pl.BlockSpec(memory_space=pl.ANY)],
        out_specs=WHOLE,
        scratch_shapes=[pltpu.SemaphoreType.DMA],
        compiler_params=PARAMS,
        cost_estimate=COST,
        name="theirs" if theirs else "mine",
    )(*in_hbm(raw))


def pack_kernel(own, other, out):
    cols = other.shape[0]
    core = this_core()
    for block, place in ((own, core), (other, 1 - core)):
        out[:, pl.ds(pl.multiple_of(place * cols, cols), cols), :] = jnp.transpose(block[...], (1, 0, 2))


def pack(own, other):
    cols, half, rows = other.shape
    return pl.pallas_call(
        pack_kernel,
        out_shape=jax.ShapeDtypeStruct((half, CORES * cols, rows), jnp.bfloat16),
        in_specs=[WHOLE] * 2,
        out_specs=WHOLE,
        compiler_params=PARAMS,
        cost_estimate=COST,
        name="pack",
    )(own, other)


def chunk_spec(array, chans, chunk):
    first = chunk * chans // STEP if array.shape[0] > chans else 0
    return pl.BlockSpec((STEP,) + array.shape[1:], lambda g: (first + g, 0, 0))


def cut_kernel(chunks, *refs):
    for source, out, chunk in zip(refs, refs[len(chunks) :], chunks):
        chans = out.shape[0]
        out[...] = source[chunk * chans : (chunk + 1) * chans]


def cut(arrays, chunks):
    shape = (arrays[0].shape[0] // CHUNKS,) + arrays[0].shape[1:]
    return pl.pallas_call(
        functools.partial(cut_kernel, chunks),
        out_shape=[jax.ShapeDtypeStruct(shape, jnp.bfloat16)] * len(arrays),
        in_specs=[WHOLE] * len(arrays),
        out_specs=[WHOLE] * len(arrays),
        compiler_params=PARAMS,
        cost_estimate=FRONT_COST,
        name="cut",
    )(*arrays)


def lanes(n):
    row = lax.axis_index("row")
    even = lax.rem(row, 2) == 0
    return even, jnp.where(even, row + 1 < n, True), jnp.where(even, row > 0, row + 1 < n)


def onward(by_a, by_b, up_sums, down_sums, t, n):
    row = lax.axis_index("row")
    even, use_a, use_b = lanes(n)
    up = jnp.where(row < t, up_sums.astype(jnp.float32), 0.0)
    down = jnp.where(row >= n - t, down_sums.astype(jnp.float32), 0.0)
    out_a = jnp.where(use_b, by_b.astype(jnp.float32), 0.0) + jnp.where(even, up, down)
    out_b = jnp.where(use_a, by_a.astype(jnp.float32), 0.0) + jnp.where(even, down, up)
    return out_a.astype(jnp.bfloat16), out_b.astype(jnp.bfloat16)


def first_kernel(chunk, left_mine, left_other, by_a, by_b, *refs):
    *blocks, next_a, next_b = refs
    n = len(blocks)
    chip, target = lax.axis_index("col") // CORES, jnp.where(lax.axis_index("row") == 0, n - 1, 0)
    slot = jnp.bitwise_xor(chip, target)
    chans = next_a.shape[0]
    for c in range(chans):
        at = chunk * chans + c
        lhs = jnp.concatenate((left_mine[at], left_other[at]), axis=0)
        rhs = blocks[0][at]
        for m in range(1, n):
            rhs = jnp.where(slot == m, blocks[m][at if blocks[m].shape[0] > chans else c], rhs)
        sums = lax.dot_general(lhs, rhs, BY_LAST, preferred_element_type=jnp.float32).astype(jnp.bfloat16)
        next_a[c], next_b[c] = onward(by_a[at], by_b[at], sums, sums, 1, n)


def first_step(left_mine, left_other, by_a, by_b, blocks, chunk):
    shape = (left_mine.shape[0] // CHUNKS,) + by_a.shape[1:]
    args = (left_mine, left_other, by_a, by_b, *blocks)
    return pl.pallas_call(
        functools.partial(first_kernel, chunk),
        out_shape=[jax.ShapeDtypeStruct(shape, jnp.bfloat16)] * 2,
        in_specs=[WHOLE] * len(args),
        out_specs=[WHOLE] * 2,
        compiler_params=PARAMS,
        cost_estimate=COST,
        name="first_step",
    )(*args)


def partial_kernel(n, chunk, left_mine, left_other, *refs):
    blocks, outs, sums = refs[:n], refs[n : 2 * n], refs[2 * n]
    row, chip = lax.axis_index("row"), lax.axis_index("col") // CORES
    chans = left_mine.shape[0] // CHUNKS
    step = pl.program_id(0) * STEP
    first = chunk * chans + step
    for c in range(STEP):
        lhs = jnp.concatenate((left_mine[first + c], left_other[first + c]), axis=0)
        for m, block in enumerate(blocks):
            away = lax.rem(jnp.bitwise_xor(chip, m) - row + n, n)
            rhs = block[(first if block.shape[0] > chans else step) + c]
            sums[away, c] = lax.dot_general(lhs, rhs, BY_LAST, preferred_element_type=jnp.float32).astype(jnp.bfloat16)
    for s, out in enumerate(outs):
        out[...] = sums[s]


def partial_products(left_mine, left_other, blocks, chunk):
    rows = blocks[0].shape[1]
    ks, chans = left_mine.shape[1], left_mine.shape[0] // CHUNKS
    n = len(blocks)
    args = (left_mine, left_other, *blocks)
    return pl.pallas_call(
        functools.partial(partial_kernel, n, chunk),
        out_shape=[pltpu.HBM((chans, CORES * ks, rows), jnp.bfloat16)] * n,
        grid=(chans // STEP,),
        in_specs=[WHOLE] * len(args),
        out_specs=[pl.BlockSpec((STEP, CORES * ks, rows), lambda g: (g, 0, 0))] * n,
        scratch_shapes=[pltpu.VMEM((n, STEP, CORES * ks, rows), jnp.bfloat16)],
        compiler_params=PARAMS,
        cost_estimate=COST,
        name="right_partials",
    )(*args)


def left_kernel(n, own, *refs):
    by_a, by_b, refs = refs[: n - 1], refs[n - 1 : 2 * n - 2], refs[2 * n - 2 :]
    blocks, (mine, theirs, panel) = refs[:n], refs[n:]
    row, chip = lax.axis_index("row"), lax.axis_index("col") // CORES
    even = lanes(n)[0]
    ks = mine.shape[1]
    for c in range(STEP):
        for m, block in enumerate(blocks):
            panel[c, jnp.bitwise_xor(chip, m)] = block[c]
        acts, grads = [own[c]], [panel[c, row]]
        for s in range(1, n):
            from_above = jnp.where(even, by_a[s - 1][c], by_b[s - 1][c])
            from_below = jnp.where(even, by_b[n - s - 1][c], by_a[n - s - 1][c])
            acts.append(jnp.where(row + s < n, from_above, from_below))
            grads.append(panel[c, lax.rem(row + s, n)])
        out = jnp.dot(
            jnp.concatenate(acts, axis=1), jnp.concatenate(grads, axis=0), preferred_element_type=jnp.float32
        )
        mine[c] = out[:ks]
        theirs[c] = out[ks:].astype(jnp.bfloat16)


def left_products(own, by_a, by_b, blocks, chunk):
    chans, ks, rows = by_a[-1].shape
    n = len(blocks)
    out = pl.BlockSpec((STEP, ks // CORES, rows), lambda g: (g, 0, 0))
    args = (own, *by_a, *by_b, *blocks)
    return pl.pallas_call(
        functools.partial(left_kernel, n),
        out_shape=[
            jax.ShapeDtypeStruct((chans, ks // CORES, rows), jnp.float32),
            jax.ShapeDtypeStruct((chans, ks // CORES, rows), jnp.bfloat16),
        ],
        grid=(chans // STEP,),
        in_specs=[chunk_spec(v, chans, chunk) for v in args],
        out_specs=[out] * 2,
        scratch_shapes=[pltpu.VMEM((STEP, n, rows, rows), jnp.bfloat16)],
        compiler_params=PARAMS,
        cost_estimate=COST,
        name="left_products",
    )(*args)


def arrived_total(own, by_a, by_b, n):
    _, use_a, use_b = lanes(n)
    total = own.astype(jnp.float32) + jnp.where(use_a, by_a.astype(jnp.float32), 0.0)
    return total + jnp.where(use_b, by_b.astype(jnp.float32), 0.0)


def put(flat, owner, value):
    size = value.shape[0] * value.shape[1]
    flat[pl.ds(pl.multiple_of(owner * size, size), size), :] = value.astype(jnp.float32).reshape(size, value.shape[2])


def known_kernel(n, factors, weight, *refs):
    known = CHUNKS - 1
    left_mine, left_other = refs[:CHUNKS], refs[CHUNKS : 2 * CHUNKS]
    partials, by_a, by_b, right_other = (refs[2 * CHUNKS + i * known : 2 * CHUNKS + (i + 1) * known] for i in range(4))
    out, grads, *flats = refs[2 * CHUNKS + 4 * known :]
    keys, width, _ = factors.shape
    hidden = width // 4
    part = hidden // CORES // CHUNKS
    core = this_core()

    @pl.when(pl.program_id(0) == 0)
    def _():
        grads[...] = jnp.zeros_like(grads)

    for chunk in range(CHUNKS):
        put(flats[chunk], core, left_mine[chunk][...])
        put(flats[chunk], 1 - core, left_other[chunk][...])
    for chunk in range(known):
        put(flats[CHUNKS + chunk], core, arrived_total(partials[chunk][...], by_a[chunk][...], by_b[chunk][...], n))
        put(flats[CHUNKS + chunk], 1 - core, right_other[chunk][...])
    for key in range(keys):
        for i, flat in enumerate(flats):
            side, chunk = divmod(i, CHUNKS)
            grad = flat[pl.ds(key, CORES * part, stride=keys), :]
            for owner in range(CORES):
                for kind in range(2):
                    first = (2 * side + kind) * hidden + (owner * CHUNKS + chunk) * part
                    place = slice(first, first + part)
                    factor = factors[key, place, :].astype(jnp.float32)
                    grads[key, place, :] = (grad[owner * part : (owner + 1) * part] * factor).astype(jnp.bfloat16)
    for key in range(keys):
        out[key] = jnp.dot(weight[...], grads[key], preferred_element_type=jnp.float32)


def known(factors, proj_weight, left_mine, left_other, partials, by_a, by_b, right_other):
    cols, width, rows = factors.shape
    chans, hidden = proj_weight.shape[0], width // 4
    part = hidden // CORES // CHUNKS
    by_key = lambda *shape: pl.BlockSpec((KEYS,) + shape, lambda g: (g, 0, 0))
    args = (*left_mine, *left_other, *partials, *by_a, *by_b, *right_other)
    return pl.pallas_call(
        functools.partial(known_kernel, lax.axis_size("row")),
        out_shape=jax.ShapeDtypeStruct((cols, chans, rows), jnp.float32),
        grid=(cols // KEYS,),
        in_specs=[by_key(width, rows), pl.BlockSpec((chans, width), lambda g: (0, 0))]
        + [pl.BlockSpec((part, KEYS, rows), lambda g: (0, g, 0))] * len(args),
        out_specs=by_key(chans, rows),
        scratch_shapes=[pltpu.VMEM((KEYS, width, rows), jnp.bfloat16)]
        + [pltpu.VMEM((CORES * part * KEYS, rows), jnp.float32)] * (2 * CHUNKS - 1),
        compiler_params=PARAMS,
        cost_estimate=COST,
        name="known",
    )(factors, proj_weight, *args)


def tail_kernel(n, base, scaled, inverse, last, gain, weight, partials, by_a, by_b, right_other, out, results, flipped, grads, flat, gain_col):
    _, keys, chans = out.shape
    rows = scaled.shape[2]
    core = this_core()

    @pl.when(pl.program_id(0) == 0)
    def _():
        gain_col[...] = column(gain, rows)

    first_key = pl.program_id(0) * keys
    here = pl.ds(pl.multiple_of(first_key, keys), keys)
    put(flat, core, arrived_total(partials[:, here, :], by_a[:, here, :], by_b[:, here, :], n))
    put(flat, 1 - core, right_other[:, here, :])
    count = last.shape[1] // 2
    for key in range(keys):
        grad = flat[pl.ds(key, count, stride=keys), :]
        for kind in range(2):
            place = slice(kind * count, (kind + 1) * count)
            grads[key, place, :] = (grad * last[first_key + key, place, :].astype(jnp.float32)).astype(jnp.bfloat16)
    for key in range(keys):
        scaled_key = scaled[first_key + key].astype(jnp.float32)
        added = jnp.dot(weight[...], grads[key], preferred_element_type=jnp.float32)
        scaled_grad = (base[first_key + key] + added) * gain_col[...]
        result = inverse[first_key + key] * (
            scaled_grad
            - jnp.mean(scaled_grad, axis=0, keepdims=True)
            - scaled_key * jnp.mean(scaled_grad * scaled_key, axis=0, keepdims=True)
        )
        results[key] = result.astype(jnp.bfloat16)
    eye = identity(rows)
    for key in range(keys):
        flipped[key] = lax.dot_general(eye, results[key], BY_LAST, preferred_element_type=jnp.float32).astype(jnp.bfloat16)
    out[...] = jnp.transpose(flipped[...], (1, 0, 2))


def tail(base, scaled, inverse, last, gain, proj_weight, partials, by_a, by_b, right_other):
    cols, chans, rows = scaled.shape
    hidden, part = proj_weight.shape[1] // 4, partials.shape[0]
    weight = jnp.concatenate([proj_weight[:, first : first + size] for first, size in last_rows(hidden)], axis=1)
    return pl.pallas_call(
        functools.partial(tail_kernel, lax.axis_size("row")),
        out_shape=jax.ShapeDtypeStruct((rows, cols, chans), jnp.bfloat16),
        grid=(cols // KEYS,),
        in_specs=[WHOLE] * 10,
        out_specs=pl.BlockSpec((rows, KEYS, chans), lambda g: (0, g, 0)),
        scratch_shapes=[
            pltpu.VMEM((KEYS, chans, rows), jnp.bfloat16),
            pltpu.VMEM((KEYS, rows, chans), jnp.bfloat16),
            pltpu.VMEM((KEYS, last.shape[1], rows), jnp.bfloat16),
            pltpu.VMEM((CORES * part * KEYS, rows), jnp.float32),
            pltpu.VMEM((chans, rows), jnp.float32),
        ],
        compiler_params=PARAMS,
        cost_estimate=COST,
        name="tail",
    )(base, scaled, inverse, last, gain, weight, partials, by_a, by_b, right_other)


def after(value, *others):
    return lax.optimization_barrier((value, others))[0]


def shards(pair, grad_x, norm_gain, norm_bias, proj_weight, tile_mask):
    n, n_col = lax.axis_size("row"), lax.axis_size("col")
    half = grad_x.shape[2] // CORES
    part = half // CHUNKS
    gain, bias = norm_gain[None, :], norm_bias[None, :]

    def exchange(value, mask):
        return lax.ppermute(value, "col", [(d, d ^ mask) for d in range(n_col)])

    def hop(value, first):
        pairs = {r: r + 1 for r in range(first, n - 1, 2)}
        pairs.update({above: r for r, above in pairs.items()})
        perm = [
            (r * n_col + d, pairs[r] * n_col + d if r in pairs else r * n_col + (d ^ 1)) for r in range(n) for d in range(n_col)
        ]
        return lax.ppermute(value, ("row", "col"), perm)

    raw = jnp.transpose(grad_x, (1, 2, 0))
    other = exchange(take_half(raw, True), 1)
    packed = pack(take_half(raw, False), other)

    axes = {m: [1 << b for b in range(m.bit_length()) if m >> b & 1] for m in range(n_col // CORES)}
    whole = {m: exchange(packed, CORES * m) for m in axes if len(axes[m]) == 1}
    turns = [(m, c, axes[m][(c + 1) % 2]) for m in axes if len(axes[m]) == 2 for c in range(CHUNKS)]
    cuts = cut([whole[m ^ bit] for m, _, bit in turns], [c for _, c, _ in turns])
    relayed = {(m, c): exchange(value, CORES * bit) for (m, c, bit), value in zip(turns, cuts)}
    for m in axes:
        for c in range(CHUNKS if len(axes[m]) > 2 else 0):
            bit = axes[m][c % len(axes[m])]
            relayed[m, c] = exchange(relayed[m ^ bit, c], CORES * bit)
    whole[0] = packed
    panels = [[whole[m] if m in whole else relayed[m, c] for m in axes] for c in range(CHUNKS)]

    right_mine, right_theirs = front(after(pair, packed), gain, bias, proj_weight, tile_mask, True)
    right_other = [exchange(right_theirs[c * part : (c + 1) * part], 1) for c in range(CHUNKS)]
    own = jnp.concatenate((right_mine, jnp.concatenate(right_other)), axis=1)
    first_a, first_b = hop(own, 0), hop(own, 1)
    left_mine, left_theirs, *forward = front(after(pair, own), gain, bias, proj_weight, tile_mask, False)
    left_other = exchange(left_theirs, 1)

    by_a, by_b, partials = [], [], []
    for c in range(CHUNKS):
        next_a, next_b = first_step(left_mine, left_other, first_a, first_b, panels[c], c)
        partials.append(partial_products(left_mine, left_other, panels[c], c))
        by_a.append([first_a, hop(next_a, 0)])
        by_b.append([first_b, hop(next_b, 1)])

    left_grads = []
    for t in range(2, n):
        for c in range(CHUNKS):
            value = by_a[c][-1]
            if t == n - 1 and c > 0:
                value = after(value, left_grads[c - 1])
            next_a, next_b = onward(value, by_b[c][-1], partials[c][n - t], partials[c][t], t, n)
            by_a[c].append(hop(next_a, 0))
            by_b[c].append(hop(next_b, 1))
            if t == n - 1:
                left_grads.append(left_products(own, by_a[c][: n - 1], by_b[c][: n - 1], panels[c], c))
    left_grad_other = [exchange(theirs, 1) for _, theirs in left_grads]
    ks = left_mine.shape[1]
    scaled, inverse, factors, last = forward
    own_sums, last_a, last_b = [sums[0] for sums in partials], [v[-1] for v in by_a], [v[-1] for v in by_b]
    right_grad_other = []
    for c in range(CHUNKS):
        value = own_sums[c]
        if c == CHUNKS - 1:
            base = known(
                factors,
                proj_weight,
                [mine for mine, _ in left_grads],
                left_grad_other,
                own_sums[:c],
                last_a[:c],
                last_b[:c],
                right_grad_other,
            )
            value = after(value, base)
        total = arrived_total(value[:, ks:], last_a[c][:, ks:], last_b[c][:, ks:], n)
        right_grad_other.append(exchange(total.astype(jnp.bfloat16), 1))
    return tail(
        base, scaled, inverse, last, gain, proj_weight, own_sums[-1], last_a[-1], last_b[-1], right_grad_other[-1]
    )


def solution(mesh):
    placed = (P("row", "col", None), P("row", "col", None), P(), P(), P(), P())
    return jax.shard_map(
        shards, mesh=mesh, in_specs=placed, out_specs=P("row", "col", None), check_vma=False
    )
```

```python
import functools

import jax
import jax.numpy as jnp
from jax import lax
from jax.experimental import pallas as pl
from jax.experimental.pallas import tpu as pltpu
from jax.sharding import PartitionSpec as P

BLK = 128
CHUNKS = 2
STEP = 8
KEYS = 16
CORES = 2
VMEM_LIMIT = 18 * 1024 * 1024
PARAMS = pltpu.CompilerParams(vmem_limit_bytes=VMEM_LIMIT)
FRONT_COST = pl.CostEstimate(flops=1, bytes_accessed=18_000_000, transcendentals=0)
COST = pl.CostEstimate(flops=1, bytes_accessed=8_000_000, transcendentals=0)
WHOLE = pl.BlockSpec(memory_space=pltpu.VMEM)
BY_LAST = (((1,), (1,)), ((), ()))


def identity(size):
    return (
        lax.broadcasted_iota(jnp.int32, (size, size), 0) == lax.broadcasted_iota(jnp.int32, (size, size), 1)
    ).astype(jnp.bfloat16)


def column(vector_ref, rows):
    return jnp.broadcast_to(vector_ref[...], (rows, vector_ref.shape[1])).T


def unit_mask(mask_ref, rows, cols):
    row, col = lax.axis_index("row"), lax.axis_index("col")
    return mask_ref[(row * rows) // BLK, (col * cols) // BLK].astype(jnp.float32)


def in_hbm(*values):
    return [pltpu.with_memory_space_constraint(v, pltpu.HBM) for v in values]


def this_core():
    return lax.rem(lax.axis_index("col"), CORES)


def turn(pair, flipped, turned):
    flipped[...] = jnp.transpose(pair[...], (1, 0, 2))
    eye = identity(pair.shape[2])
    for key in range(pair.shape[1]):
        turned[key] = lax.dot_general(eye, flipped[key], BY_LAST, preferred_element_type=jnp.float32)


def normalize(values):
    centred = values - jnp.mean(values, axis=1, keepdims=True)
    inverse = lax.rsqrt(jnp.mean(centred * centred, axis=1, keepdims=True) + 1e-05)
    return centred * inverse, inverse


def set_columns(gain, bias, weight, gain_col, bias_col, weight_t):
    @pl.when(pl.program_id(0) == 0)
    def _():
        gain_col[...] = column(gain, gain_col.shape[1])
        bias_col[...] = column(bias, bias_col.shape[1])
        weight_t[...] = weight[...].astype(jnp.float32).T.astype(jnp.bfloat16)


def normalized(pair, gain_col, bias_col, flipped, turned, normed):
    turn(pair, flipped, turned)
    scaled, inverse = normalize(turned[...])
    normed[...] = (scaled * gain_col[...] + bias_col[...]).astype(jnp.bfloat16)
    return scaled, inverse


def split_channels(acts, whole, mine, theirs):
    half = mine.shape[0]
    whole[...] = jnp.transpose(acts[...], (1, 0, 2))
    core = this_core()
    mine[...] = whole[pl.ds(core * half, half)]
    theirs[...] = whole[pl.ds((1 - core) * half, half)]


def right_kernel(mask, pair, gain, bias, weight, mine, theirs, flipped, turned, normed, acts, whole, gain_col, bias_col, weight_t):
    rows, keys, _ = pair.shape
    hidden = acts.shape[1]
    set_columns(gain, bias, weight, gain_col, bias_col, weight_t)
    valid = unit_mask(mask, rows, pl.num_programs(0) * keys)
    normalized(pair, gain_col, bias_col, flipped, turned, normed)
    for key in range(keys):
        projected = jnp.dot(weight_t[...], normed[key], preferred_element_type=jnp.float32)
        acts[key] = (valid * jax.nn.sigmoid(projected[hidden:]) * projected[:hidden]).astype(jnp.bfloat16)
    split_channels(acts, whole, mine, theirs)


def last_rows(hidden):
    part = hidden // CORES // CHUNKS
    return [((2 + kind) * hidden + (core * CHUNKS + CHUNKS - 1) * part, part) for kind in range(2) for core in range(CORES)]


def left_forward_kernel(
    mask, pair, gain, bias, weight, mine, theirs, scaled_out, inverse_out, factors, last,
    flipped, turned, normed, acts, whole, gain_col, bias_col, weight_t,
):
    rows, keys, _ = pair.shape
    hidden = acts.shape[1]
    set_columns(gain, bias, weight, gain_col, bias_col, weight_t)
    valid = unit_mask(mask, rows, pl.num_programs(0) * keys)
    scaled, inverse = normalized(pair, gain_col, bias_col, flipped, turned, normed)
    scaled_out[...] = scaled.astype(jnp.bfloat16)
    inverse_out[...] = inverse
    for key in range(keys):
        projected = jnp.dot(weight_t[...], normed[key], preferred_element_type=jnp.float32)
        for side in range(2):
            first = 2 * side * hidden
            lin = projected[first : first + hidden]
            sig = jax.nn.sigmoid(projected[first + hidden : first + 2 * hidden])
            masked = valid * sig
            act = masked * lin
            if side == 0:
                acts[key] = act.astype(jnp.bfloat16)
            factors[key, first : first + hidden, :] = masked.astype(jnp.bfloat16)
            factors[key, first + hidden : first + 2 * hidden, :] = (act * (1.0 - sig)).astype(jnp.bfloat16)
    for i, (first, size) in enumerate(last_rows(hidden)):
        last[:, i * size : (i + 1) * size, :] = factors[:, first : first + size, :]
    split_channels(acts, whole, mine, theirs)


def front(pair, gain, bias, proj_weight, tile_mask, right):
    rows, cols, chans = pair.shape
    width = proj_weight.shape[1]
    hidden = width // 4
    half = hidden // CORES
    used = width // 2 if right else width
    vector = pl.BlockSpec((1, chans), lambda g: (0, 0))
    by_key = lambda *shape: pl.BlockSpec((KEYS,) + shape, lambda g: (g, 0, 0))
    out_shape = [jax.ShapeDtypeStruct((half, cols, rows), jnp.bfloat16)] * 2
    out_specs = [pl.BlockSpec((half, KEYS, rows), lambda g: (0, g, 0))] * 2
    if not right:
        out_shape += [
            jax.ShapeDtypeStruct((cols, chans, rows), jnp.bfloat16),
            jax.ShapeDtypeStruct((cols, 1, rows), jnp.float32),
            jax.ShapeDtypeStruct((cols, width, rows), jnp.bfloat16),
            jax.ShapeDtypeStruct((cols, 2 * hidden // CHUNKS, rows), jnp.bfloat16),
        ]
        out_specs += [by_key(chans, rows), by_key(1, rows), by_key(width, rows), by_key(2 * hidden // CHUNKS, rows)]
    return pl.pallas_call(
        right_kernel if right else left_forward_kernel,
        out_shape=out_shape,
        grid=(cols // KEYS,),
        in_specs=[
            pl.BlockSpec(memory_space=pltpu.SMEM),
            pl.BlockSpec((rows, KEYS, chans), lambda g: (0, g, 0)),
            vector,
            vector,
            pl.BlockSpec((chans, used), lambda g: (0, 1 if right else 0)),
        ],
        out_specs=out_specs,
        scratch_shapes=[
            pltpu.VMEM((KEYS, rows, chans), jnp.bfloat16),
            pltpu.VMEM((KEYS, chans, rows), jnp.float32),
            pltpu.VMEM((KEYS, chans, rows), jnp.bfloat16),
            pltpu.VMEM((KEYS, hidden, rows), jnp.bfloat16),
            pltpu.VMEM((hidden, KEYS, rows), jnp.bfloat16),
            pltpu.VMEM((chans, rows), jnp.float32),
            pltpu.VMEM((chans, rows), jnp.float32),
            pltpu.VMEM((used, chans), jnp.bfloat16),
        ],
        compiler_params=PARAMS,
        cost_estimate=FRONT_COST,
        name="right_front" if right else "left_front",
    )(tile_mask, *in_hbm(pair, gain, bias, proj_weight))


def half_kernel(theirs, raw, out, sem):
    half = out.shape[1]
    core = this_core()
    first = pl.multiple_of((1 - core if theirs else core) * half, half)
    copy = pltpu.make_async_copy(raw.at[:, pl.ds(first, half), :], out, sem)
    copy.start()
    copy.wait()


def take_half(raw, theirs):
    cols, hidden, rows = raw.shape
    return pl.pallas_call(
        functools.partial(half_kernel, theirs),
        out_shape=jax.ShapeDtypeStruct((cols, hidden // CORES, rows), raw.dtype),
        in_specs=[pl.BlockSpec(memory_space=pl.ANY)],
        out_specs=WHOLE,
        scratch_shapes=[pltpu.SemaphoreType.DMA],
        compiler_params=PARAMS,
        cost_estimate=COST,
        name="theirs" if theirs else "mine",
    )(*in_hbm(raw))


def pack_kernel(own, other, *outs):
    cols = other.shape[0]
    core = this_core()
    for block, place in ((own, core), (other, 1 - core)):
        flipped = jnp.transpose(block[...], (1, 0, 2))
        for chunk, out in enumerate(outs):
            chans = out.shape[0]
            out[:, pl.ds(pl.multiple_of(place * cols, cols), cols), :] = flipped[chunk * chans : (chunk + 1) * chans]


def pack(own, other):
    cols, half, rows = other.shape
    return pl.pallas_call(
        pack_kernel,
        out_shape=[jax.ShapeDtypeStruct((half // CHUNKS, CORES * cols, rows), jnp.bfloat16)] * CHUNKS,
        in_specs=[WHOLE] * 2,
        out_specs=[WHOLE] * CHUNKS,
        compiler_params=PARAMS,
        cost_estimate=COST,
        name="pack",
    )(own, other)


def chunk_spec(array, chans, chunk):
    first = chunk * chans // STEP if array.shape[0] > chans else 0
    return pl.BlockSpec((STEP,) + array.shape[1:], lambda g: (first + g, 0, 0))


def slot_mask(m, core, chips):
    width = chips.bit_length() - 1
    return m if core == 0 else sum(1 << (width - 1 - b) for b in range(width) if m >> b & 1)


def slot_chips(chips):
    chip = lax.axis_index("col") // CORES
    return [
        jnp.bitwise_xor(chip, jnp.where(this_core() == 0, m, slot_mask(m, 1, chips))) for m in range(chips)
    ]


def lanes(n):
    row = lax.axis_index("row")
    even = lax.rem(row, 2) == 0
    return even, jnp.where(even, row + 1 < n, True), jnp.where(even, row > 0, row + 1 < n)


def onward(by_a, by_b, up_sums, down_sums, t, n):
    row = lax.axis_index("row")
    even, use_a, use_b = lanes(n)
    up = jnp.where(row < t, up_sums.astype(jnp.float32), 0.0)
    down = jnp.where(row >= n - t, down_sums.astype(jnp.float32), 0.0)
    out_a = jnp.where(use_b, by_b.astype(jnp.float32), 0.0) + jnp.where(even, up, down)
    out_b = jnp.where(use_a, by_a.astype(jnp.float32), 0.0) + jnp.where(even, down, up)
    return out_a.astype(jnp.bfloat16), out_b.astype(jnp.bfloat16)


def first_kernel(chunk, left_mine, left_other, by_a, by_b, *refs):
    *blocks, next_a, next_b = refs
    n = len(blocks)
    holders, target = slot_chips(n), jnp.where(lax.axis_index("row") == 0, n - 1, 0)
    chans = next_a.shape[0]
    for c in range(chans):
        at = chunk * chans + c
        lhs = jnp.concatenate((left_mine[at], left_other[at]), axis=0)
        rhs = blocks[0][c]
        for m in range(1, n):
            rhs = jnp.where(holders[m] == target, blocks[m][c], rhs)
        sums = lax.dot_general(lhs, rhs, BY_LAST, preferred_element_type=jnp.float32).astype(jnp.bfloat16)
        next_a[c], next_b[c] = onward(by_a[at], by_b[at], sums, sums, 1, n)


def first_step(left_mine, left_other, by_a, by_b, blocks, chunk):
    shape = (left_mine.shape[0] // CHUNKS,) + by_a.shape[1:]
    args = (left_mine, left_other, by_a, by_b, *blocks)
    return pl.pallas_call(
        functools.partial(first_kernel, chunk),
        out_shape=[jax.ShapeDtypeStruct(shape, jnp.bfloat16)] * 2,
        in_specs=[WHOLE] * len(args),
        out_specs=[WHOLE] * 2,
        compiler_params=PARAMS,
        cost_estimate=COST,
        name="first_step",
    )(*args)


def partial_kernel(n, left_mine, left_other, *refs):
    blocks, outs, sums = refs[:n], refs[n : 2 * n], refs[2 * n]
    row, holders = lax.axis_index("row"), slot_chips(n)
    for c in range(STEP):
        lhs = jnp.concatenate((left_mine[c], left_other[c]), axis=0)
        for holder, block in zip(holders, blocks):
            away = lax.rem(holder - row + n, n)
            sums[away, c] = lax.dot_general(lhs, block[c], BY_LAST, preferred_element_type=jnp.float32).astype(jnp.bfloat16)
    for s, out in enumerate(outs):
        out[...] = sums[s]


def partial_products(left_mine, left_other, blocks, chunk):
    chans, rows, _ = blocks[0].shape
    ks = left_mine.shape[1]
    n = len(blocks)
    args = (left_mine, left_other, *blocks)
    return pl.pallas_call(
        functools.partial(partial_kernel, n),
        out_shape=[pltpu.HBM((chans, CORES * ks, rows), jnp.bfloat16)] * n,
        grid=(chans // STEP,),
        in_specs=[chunk_spec(v, chans, chunk) for v in args],
        out_specs=[pl.BlockSpec((STEP, CORES * ks, rows), lambda g: (g, 0, 0))] * n,
        scratch_shapes=[pltpu.VMEM((n, STEP, CORES * ks, rows), jnp.bfloat16)],
        compiler_params=PARAMS,
        cost_estimate=COST,
        name="right_partials",
    )(*args)


def left_kernel(n, own, *refs):
    by_a, by_b, refs = refs[: n - 1], refs[n - 1 : 2 * n - 2], refs[2 * n - 2 :]
    blocks, (mine, theirs, panel) = refs[:n], refs[n:]
    row, holders = lax.axis_index("row"), slot_chips(n)
    even = lanes(n)[0]
    ks = mine.shape[1]
    for c in range(STEP):
        for holder, block in zip(holders, blocks):
            panel[c, holder] = block[c]
        acts, grads = [own[c]], [panel[c, row]]
        for s in range(1, n):
            from_above = jnp.where(even, by_a[s - 1][c], by_b[s - 1][c])
            from_below = jnp.where(even, by_b[n - s - 1][c], by_a[n - s - 1][c])
            acts.append(jnp.where(row + s < n, from_above, from_below))
            grads.append(panel[c, lax.rem(row + s, n)])
        out = jnp.dot(
            jnp.concatenate(acts, axis=1), jnp.concatenate(grads, axis=0), preferred_element_type=jnp.float32
        )
        mine[c] = out[:ks]
        theirs[c] = out[ks:].astype(jnp.bfloat16)


def left_products(own, by_a, by_b, blocks, chunk):
    chans, ks, rows = by_a[-1].shape
    n = len(blocks)
    out = pl.BlockSpec((STEP, ks // CORES, rows), lambda g: (g, 0, 0))
    args = (own, *by_a, *by_b, *blocks)
    return pl.pallas_call(
        functools.partial(left_kernel, n),
        out_shape=[
            jax.ShapeDtypeStruct((chans, ks // CORES, rows), jnp.float32),
            jax.ShapeDtypeStruct((chans, ks // CORES, rows), jnp.bfloat16),
        ],
        grid=(chans // STEP,),
        in_specs=[chunk_spec(v, chans, chunk) for v in args],
        out_specs=[out] * 2,
        scratch_shapes=[pltpu.VMEM((STEP, n, rows, rows), jnp.bfloat16)],
        compiler_params=PARAMS,
        cost_estimate=COST,
        name="left_products",
    )(*args)


def arrived_total(own, by_a, by_b, n):
    _, use_a, use_b = lanes(n)
    total = own.astype(jnp.float32) + jnp.where(use_a, by_a.astype(jnp.float32), 0.0)
    return total + jnp.where(use_b, by_b.astype(jnp.float32), 0.0)


def put(flat, owner, value):
    size = value.shape[0] * value.shape[1]
    flat[pl.ds(pl.multiple_of(owner * size, size), size), :] = value.astype(jnp.float32).reshape(size, value.shape[2])


def known_kernel(n, factors, weight, *refs):
    known = CHUNKS - 1
    left_mine, left_other = refs[:CHUNKS], refs[CHUNKS : 2 * CHUNKS]
    partials, by_a, by_b, right_other = (refs[2 * CHUNKS + i * known : 2 * CHUNKS + (i + 1) * known] for i in range(4))
    out, grads, *flats = refs[2 * CHUNKS + 4 * known :]
    keys, width, _ = factors.shape
    hidden = width // 4
    part = hidden // CORES // CHUNKS
    core = this_core()

    @pl.when(pl.program_id(0) == 0)
    def _():
        grads[...] = jnp.zeros_like(grads)

    for chunk in range(CHUNKS):
        put(flats[chunk], core, left_mine[chunk][...])
        put(flats[chunk], 1 - core, left_other[chunk][...])
    for chunk in range(known):
        put(flats[CHUNKS + chunk], core, arrived_total(partials[chunk][...], by_a[chunk][...], by_b[chunk][...], n))
        put(flats[CHUNKS + chunk], 1 - core, right_other[chunk][...])
    for key in range(keys):
        for i, flat in enumerate(flats):
            side, chunk = divmod(i, CHUNKS)
            grad = flat[pl.ds(key, CORES * part, stride=keys), :]
            for owner in range(CORES):
                for kind in range(2):
                    first = (2 * side + kind) * hidden + (owner * CHUNKS + chunk) * part
                    place = slice(first, first + part)
                    factor = factors[key, place, :].astype(jnp.float32)
                    grads[key, place, :] = (grad[owner * part : (owner + 1) * part] * factor).astype(jnp.bfloat16)
    for key in range(keys):
        out[key] = jnp.dot(weight[...], grads[key], preferred_element_type=jnp.float32)


def known(factors, proj_weight, left_mine, left_other, partials, by_a, by_b, right_other):
    cols, width, rows = factors.shape
    chans, hidden = proj_weight.shape[0], width // 4
    part = hidden // CORES // CHUNKS
    by_key = lambda *shape: pl.BlockSpec((KEYS,) + shape, lambda g: (g, 0, 0))
    args = (*left_mine, *left_other, *partials, *by_a, *by_b, *right_other)
    return pl.pallas_call(
        functools.partial(known_kernel, lax.axis_size("row")),
        out_shape=jax.ShapeDtypeStruct((cols, chans, rows), jnp.float32),
        grid=(cols // KEYS,),
        in_specs=[by_key(width, rows), pl.BlockSpec((chans, width), lambda g: (0, 0))]
        + [pl.BlockSpec((part, KEYS, rows), lambda g: (0, g, 0))] * len(args),
        out_specs=by_key(chans, rows),
        scratch_shapes=[pltpu.VMEM((KEYS, width, rows), jnp.bfloat16)]
        + [pltpu.VMEM((CORES * part * KEYS, rows), jnp.float32)] * (2 * CHUNKS - 1),
        compiler_params=PARAMS,
        cost_estimate=COST,
        name="known",
    )(factors, proj_weight, *args)


def tail_kernel(n, base, scaled, inverse, last, gain, weight, partials, by_a, by_b, right_other, out, results, flipped, grads, flat, gain_col):
    _, keys, chans = out.shape
    rows = scaled.shape[2]
    core = this_core()

    @pl.when(pl.program_id(0) == 0)
    def _():
        gain_col[...] = column(gain, rows)

    first_key = pl.program_id(0) * keys
    here = pl.ds(pl.multiple_of(first_key, keys), keys)
    put(flat, core, arrived_total(partials[:, here, :], by_a[:, here, :], by_b[:, here, :], n))
    put(flat, 1 - core, right_other[:, here, :])
    count = last.shape[1] // 2
    for key in range(keys):
        grad = flat[pl.ds(key, count, stride=keys), :]
        for kind in range(2):
            place = slice(kind * count, (kind + 1) * count)
            grads[key, place, :] = (grad * last[first_key + key, place, :].astype(jnp.float32)).astype(jnp.bfloat16)
    for key in range(keys):
        scaled_key = scaled[first_key + key].astype(jnp.float32)
        added = jnp.dot(weight[...], grads[key], preferred_element_type=jnp.float32)
        scaled_grad = (base[first_key + key] + added) * gain_col[...]
        result = inverse[first_key + key] * (
            scaled_grad
            - jnp.mean(scaled_grad, axis=0, keepdims=True)
            - scaled_key * jnp.mean(scaled_grad * scaled_key, axis=0, keepdims=True)
        )
        results[key] = result.astype(jnp.bfloat16)
    eye = identity(rows)
    for key in range(keys):
        flipped[key] = lax.dot_general(eye, results[key], BY_LAST, preferred_element_type=jnp.float32).astype(jnp.bfloat16)
    out[...] = jnp.transpose(flipped[...], (1, 0, 2))


def tail(base, scaled, inverse, last, gain, proj_weight, partials, by_a, by_b, right_other):
    cols, chans, rows = scaled.shape
    hidden, part = proj_weight.shape[1] // 4, partials.shape[0]
    weight = jnp.concatenate([proj_weight[:, first : first + size] for first, size in last_rows(hidden)], axis=1)
    return pl.pallas_call(
        functools.partial(tail_kernel, lax.axis_size("row")),
        out_shape=jax.ShapeDtypeStruct((rows, cols, chans), jnp.bfloat16),
        grid=(cols // KEYS,),
        in_specs=[WHOLE] * 10,
        out_specs=pl.BlockSpec((rows, KEYS, chans), lambda g: (0, g, 0)),
        scratch_shapes=[
            pltpu.VMEM((KEYS, chans, rows), jnp.bfloat16),
            pltpu.VMEM((KEYS, rows, chans), jnp.bfloat16),
            pltpu.VMEM((KEYS, last.shape[1], rows), jnp.bfloat16),
            pltpu.VMEM((CORES * part * KEYS, rows), jnp.float32),
            pltpu.VMEM((chans, rows), jnp.float32),
        ],
        compiler_params=PARAMS,
        cost_estimate=COST,
        name="tail",
    )(base, scaled, inverse, last, gain, weight, partials, by_a, by_b, right_other)


def after(value, *others):
    return lax.optimization_barrier((value, others))[0]


def shards(pair, grad_x, norm_gain, norm_bias, proj_weight, tile_mask):
    n, n_col = lax.axis_size("row"), lax.axis_size("col")
    half = grad_x.shape[2] // CORES
    part = half // CHUNKS
    gain, bias = norm_gain[None, :], norm_bias[None, :]

    def exchange(value, mask):
        return lax.ppermute(value, "col", [(d, d ^ mask) for d in range(n_col)])

    def hop(value, first):
        pairs = {r: r + 1 for r in range(first, n - 1, 2)}
        pairs.update({above: r for r, above in pairs.items()})
        perm = [
            (r * n_col + d, pairs[r] * n_col + d if r in pairs else r * n_col + (d ^ 1)) for r in range(n) for d in range(n_col)
        ]
        return lax.ppermute(value, ("row", "col"), perm)

    raw = jnp.transpose(grad_x, (1, 2, 0))
    other = exchange(take_half(raw, True), 1)
    packed = pack(take_half(raw, False), other)

    chips = n_col // CORES

    def along(value, bit):
        mask = [CORES * slot_mask(bit, core, chips) for core in range(CORES)]
        return lax.ppermute(value, "col", [(d, d ^ mask[d % CORES]) for d in range(n_col)])

    panels = []
    for block in packed:
        slots = [after(block, panels[-1][1:]) if panels else block]
        for m in range(1, chips):
            bit = 1 << (m.bit_length() - 1)
            slots.append(along(slots[m ^ bit], bit))
        panels.append(slots)

    right_mine, right_theirs = front(after(pair, packed), gain, bias, proj_weight, tile_mask, True)
    right_other = [exchange(right_theirs[c * part : (c + 1) * part], 1) for c in range(CHUNKS)]
    own = jnp.concatenate((right_mine, jnp.concatenate(right_other)), axis=1)
    first_a, first_b = hop(own, 0), hop(own, 1)
    left_mine, left_theirs, *forward = front(after(pair, own, panels[0][-2]), gain, bias, proj_weight, tile_mask, False)
    left_other = exchange(left_theirs, 1)

    by_a, by_b, partials = [], [], []
    for c in range(CHUNKS):
        ready = after(left_other, partials[-1]) if partials else left_other
        next_a, next_b = first_step(left_mine, ready, first_a, first_b, panels[c], c)
        partials.append(partial_products(left_mine, left_other, panels[c], c))
        by_a.append([first_a, hop(next_a, 0)])
        by_b.append([first_b, hop(next_b, 1)])

    left_grads = []
    for t in range(2, n):
        for c in range(CHUNKS):
            value = by_a[c][-1]
            if t == n - 1 and c > 0:
                value = after(value, left_grads[c - 1])
            next_a, next_b = onward(value, by_b[c][-1], partials[c][n - t], partials[c][t], t, n)
            by_a[c].append(hop(next_a, 0))
            by_b[c].append(hop(next_b, 1))
            if t == n - 1:
                left_grads.append(left_products(own, by_a[c][: n - 1], by_b[c][: n - 1], panels[c], c))
    left_grad_other = [exchange(theirs, 1) for _, theirs in left_grads]
    ks = left_mine.shape[1]
    scaled, inverse, factors, last = forward
    own_sums, last_a, last_b = [sums[0] for sums in partials], [v[-1] for v in by_a], [v[-1] for v in by_b]
    right_grad_other = []
    for c in range(CHUNKS):
        value = own_sums[c]
        if c == CHUNKS - 1:
            base = known(
                factors,
                proj_weight,
                [mine for mine, _ in left_grads],
                left_grad_other,
                own_sums[:c],
                last_a[:c],
                last_b[:c],
                right_grad_other,
            )
            value = after(value, base)
        total = arrived_total(value[:, ks:], last_a[c][:, ks:], last_b[c][:, ks:], n)
        right_grad_other.append(exchange(total.astype(jnp.bfloat16), 1))
    return tail(
        base, scaled, inverse, last, gain, proj_weight, own_sums[-1], last_a[-1], last_b[-1], right_grad_other[-1]
    )


def solution(mesh):
    placed = (P("row", "col", None), P("row", "col", None), P(), P(), P(), P())
    return jax.shard_map(
        shards, mesh=mesh, in_specs=placed, out_specs=P("row", "col", None), check_vma=False
    )
```

```python
import functools

import jax
import jax.numpy as jnp
from jax import lax
from jax.experimental import pallas as pl
from jax.experimental.pallas import tpu as pltpu
from jax.sharding import PartitionSpec as P

BLK = 128
CHUNKS = 2
STEP = 8
KEYS = 16
CORES = 2
VMEM_LIMIT = 18 * 1024 * 1024
PARAMS = pltpu.CompilerParams(vmem_limit_bytes=VMEM_LIMIT)
FRONT_COST = pl.CostEstimate(flops=1, bytes_accessed=18_000_000, transcendentals=0)
COST = pl.CostEstimate(flops=1, bytes_accessed=8_000_000, transcendentals=0)
WHOLE = pl.BlockSpec(memory_space=pltpu.VMEM)
BY_LAST = (((1,), (1,)), ((), ()))


def identity(size):
    return (
        lax.broadcasted_iota(jnp.int32, (size, size), 0) == lax.broadcasted_iota(jnp.int32, (size, size), 1)
    ).astype(jnp.bfloat16)


def column(vector_ref, rows):
    return jnp.broadcast_to(vector_ref[...], (rows, vector_ref.shape[1])).T


def unit_mask(mask_ref, rows, cols):
    row, col = lax.axis_index("row"), lax.axis_index("col")
    return mask_ref[(row * rows) // BLK, (col * cols) // BLK].astype(jnp.float32)


def in_hbm(*values):
    return [pltpu.with_memory_space_constraint(v, pltpu.HBM) for v in values]


def this_core():
    return lax.rem(lax.axis_index("col"), CORES)


def turn(pair, flipped, turned):
    flipped[...] = jnp.transpose(pair[...], (1, 0, 2))
    eye = identity(pair.shape[2])
    for key in range(pair.shape[1]):
        if key % 2:
            turned[key] = lax.dot_general(eye, flipped[key], BY_LAST, preferred_element_type=jnp.float32)
        else:
            turned[key] = flipped[key].T.astype(jnp.float32)


def normalize(values):
    centred = values - jnp.mean(values, axis=1, keepdims=True)
    inverse = lax.rsqrt(jnp.mean(centred * centred, axis=1, keepdims=True) + 1e-05)
    return centred * inverse, inverse


def set_columns(gain, bias, weight, gain_col, bias_col, weight_t):
    @pl.when(pl.program_id(0) == 0)
    def _():
        gain_col[...] = column(gain, gain_col.shape[1])
        bias_col[...] = column(bias, bias_col.shape[1])
        weight_t[...] = weight[...].astype(jnp.float32).T.astype(jnp.bfloat16)


def normalized(pair, gain_col, bias_col, flipped, turned, normed):
    turn(pair, flipped, turned)
    scaled, inverse = normalize(turned[...])
    normed[...] = (scaled * gain_col[...] + bias_col[...]).astype(jnp.bfloat16)
    return scaled, inverse


def split_channels(acts, whole, mine, theirs):
    half = mine.shape[0]
    whole[...] = jnp.transpose(acts[...], (1, 0, 2))
    core = this_core()
    mine[...] = whole[pl.ds(core * half, half)]
    theirs[...] = whole[pl.ds((1 - core) * half, half)]


def right_kernel(mask, pair, gain, bias, weight, mine, theirs, flipped, turned, normed, acts, whole, gain_col, bias_col, weight_t):
    rows, keys, _ = pair.shape
    hidden = acts.shape[1]
    set_columns(gain, bias, weight, gain_col, bias_col, weight_t)
    valid = unit_mask(mask, rows, pl.num_programs(0) * keys)
    normalized(pair, gain_col, bias_col, flipped, turned, normed)
    for key in range(keys):
        projected = jnp.dot(weight_t[...], normed[key], preferred_element_type=jnp.float32)
        acts[key] = (valid * jax.nn.sigmoid(projected[hidden:]) * projected[:hidden]).astype(jnp.bfloat16)
    split_channels(acts, whole, mine, theirs)


def last_rows(hidden):
    part = hidden // CORES // CHUNKS
    return [((2 + kind) * hidden + (core * CHUNKS + CHUNKS - 1) * part, part) for kind in range(2) for core in range(CORES)]


def left_forward_kernel(
    mask, pair, gain, bias, weight, mine, theirs, scaled_out, inverse_out, factors, last,
    flipped, turned, normed, acts, whole, gain_col, bias_col, weight_t,
):
    rows, keys, _ = pair.shape
    hidden = acts.shape[1]
    set_columns(gain, bias, weight, gain_col, bias_col, weight_t)
    valid = unit_mask(mask, rows, pl.num_programs(0) * keys)
    scaled, inverse = normalized(pair, gain_col, bias_col, flipped, turned, normed)
    scaled_out[...] = scaled.astype(jnp.bfloat16)
    inverse_out[...] = inverse
    for key in range(keys):
        projected = jnp.dot(weight_t[...], normed[key], preferred_element_type=jnp.float32)
        for side in range(2):
            first = 2 * side * hidden
            lin = projected[first : first + hidden]
            sig = jax.nn.sigmoid(projected[first + hidden : first + 2 * hidden])
            masked = valid * sig
            act = masked * lin
            if side == 0:
                acts[key] = act.astype(jnp.bfloat16)
            factors[key, first : first + hidden, :] = masked.astype(jnp.bfloat16)
            factors[key, first + hidden : first + 2 * hidden, :] = (act * (1.0 - sig)).astype(jnp.bfloat16)
    for i, (first, size) in enumerate(last_rows(hidden)):
        last[:, i * size : (i + 1) * size, :] = factors[:, first : first + size, :]
    split_channels(acts, whole, mine, theirs)


def front(pair, gain, bias, proj_weight, tile_mask, right):
    rows, cols, chans = pair.shape
    width = proj_weight.shape[1]
    hidden = width // 4
    half = hidden // CORES
    used = width // 2 if right else width
    vector = pl.BlockSpec((1, chans), lambda g: (0, 0))
    by_key = lambda *shape: pl.BlockSpec((KEYS,) + shape, lambda g: (g, 0, 0))
    out_shape = [jax.ShapeDtypeStruct((half, cols, rows), jnp.bfloat16)] * 2
    out_specs = [pl.BlockSpec((half, KEYS, rows), lambda g: (0, g, 0))] * 2
    if not right:
        out_shape += [
            jax.ShapeDtypeStruct((cols, chans, rows), jnp.bfloat16),
            jax.ShapeDtypeStruct((cols, 1, rows), jnp.float32),
            jax.ShapeDtypeStruct((cols, width, rows), jnp.bfloat16),
            jax.ShapeDtypeStruct((cols, 2 * hidden // CHUNKS, rows), jnp.bfloat16),
        ]
        out_specs += [by_key(chans, rows), by_key(1, rows), by_key(width, rows), by_key(2 * hidden // CHUNKS, rows)]
    return pl.pallas_call(
        right_kernel if right else left_forward_kernel,
        out_shape=out_shape,
        grid=(cols // KEYS,),
        in_specs=[
            pl.BlockSpec(memory_space=pltpu.SMEM),
            pl.BlockSpec((rows, KEYS, chans), lambda g: (0, g, 0)),
            vector,
            vector,
            pl.BlockSpec((chans, used), lambda g: (0, 1 if right else 0)),
        ],
        out_specs=out_specs,
        scratch_shapes=[
            pltpu.VMEM((KEYS, rows, chans), jnp.bfloat16),
            pltpu.VMEM((KEYS, chans, rows), jnp.float32),
            pltpu.VMEM((KEYS, chans, rows), jnp.bfloat16),
            pltpu.VMEM((KEYS, hidden, rows), jnp.bfloat16),
            pltpu.VMEM((hidden, KEYS, rows), jnp.bfloat16),
            pltpu.VMEM((chans, rows), jnp.float32),
            pltpu.VMEM((chans, rows), jnp.float32),
            pltpu.VMEM((used, chans), jnp.bfloat16),
        ],
        compiler_params=PARAMS,
        cost_estimate=FRONT_COST,
        name="right_front" if right else "left_front",
    )(tile_mask, *in_hbm(pair, gain, bias, proj_weight))


def half_kernel(theirs, raw, out, sem):
    half = out.shape[1]
    core = this_core()
    first = pl.multiple_of((1 - core if theirs else core) * half, half)
    copy = pltpu.make_async_copy(raw.at[:, pl.ds(first, half), :], out, sem)
    copy.start()
    copy.wait()


def take_half(raw, theirs):
    cols, hidden, rows = raw.shape
    return pl.pallas_call(
        functools.partial(half_kernel, theirs),
        out_shape=jax.ShapeDtypeStruct((cols, hidden // CORES, rows), raw.dtype),
        in_specs=[pl.BlockSpec(memory_space=pl.ANY)],
        out_specs=WHOLE,
        scratch_shapes=[pltpu.SemaphoreType.DMA],
        compiler_params=PARAMS,
        cost_estimate=COST,
        name="theirs" if theirs else "mine",
    )(*in_hbm(raw))


def pack_kernel(own, other, *outs):
    cols = other.shape[0]
    core = this_core()
    for block, place in ((own, core), (other, 1 - core)):
        flipped = jnp.transpose(block[...], (1, 0, 2))
        for chunk, out in enumerate(outs):
            chans = out.shape[0]
            out[:, pl.ds(pl.multiple_of(place * cols, cols), cols), :] = flipped[chunk * chans : (chunk + 1) * chans]


def pack(own, other):
    cols, half, rows = other.shape
    return pl.pallas_call(
        pack_kernel,
        out_shape=[jax.ShapeDtypeStruct((half // CHUNKS, CORES * cols, rows), jnp.bfloat16)] * CHUNKS,
        in_specs=[WHOLE] * 2,
        out_specs=[WHOLE] * CHUNKS,
        compiler_params=PARAMS,
        cost_estimate=COST,
        name="pack",
    )(own, other)


def chunk_spec(array, chans, chunk):
    first = chunk * chans // STEP if array.shape[0] > chans else 0
    return pl.BlockSpec((STEP,) + array.shape[1:], lambda g: (first + g, 0, 0))


def slot_mask(m, core, chips):
    width = chips.bit_length() - 1
    return m if core == 0 else sum(1 << (width - 1 - b) for b in range(width) if m >> b & 1)


def slot_chips(chips):
    chip = lax.axis_index("col") // CORES
    return [
        jnp.bitwise_xor(chip, jnp.where(this_core() == 0, m, slot_mask(m, 1, chips))) for m in range(chips)
    ]


def lanes(n):
    row = lax.axis_index("row")
    even = lax.rem(row, 2) == 0
    return even, jnp.where(even, row + 1 < n, True), jnp.where(even, row > 0, row + 1 < n)


def onward(by_a, by_b, up_sums, down_sums, t, n):
    row = lax.axis_index("row")
    even, use_a, use_b = lanes(n)
    up = jnp.where(row < t, up_sums.astype(jnp.float32), 0.0)
    down = jnp.where(row >= n - t, down_sums.astype(jnp.float32), 0.0)
    out_a = jnp.where(use_b, by_b.astype(jnp.float32), 0.0) + jnp.where(even, up, down)
    out_b = jnp.where(use_a, by_a.astype(jnp.float32), 0.0) + jnp.where(even, down, up)
    return out_a.astype(jnp.bfloat16), out_b.astype(jnp.bfloat16)


def first_kernel(chunk, left_mine, left_other, by_a, by_b, *refs):
    *blocks, next_a, next_b = refs
    n = len(blocks)
    holders, target = slot_chips(n), jnp.where(lax.axis_index("row") == 0, n - 1, 0)
    chans = next_a.shape[0]
    for c in range(chans):
        at = chunk * chans + c
        lhs = jnp.concatenate((left_mine[at], left_other[at]), axis=0)
        rhs = blocks[0][c]
        for m in range(1, n):
            rhs = jnp.where(holders[m] == target, blocks[m][c], rhs)
        sums = lax.dot_general(lhs, rhs, BY_LAST, preferred_element_type=jnp.float32).astype(jnp.bfloat16)
        next_a[c], next_b[c] = onward(by_a[at], by_b[at], sums, sums, 1, n)


def first_step(left_mine, left_other, by_a, by_b, blocks, chunk):
    shape = (left_mine.shape[0] // CHUNKS,) + by_a.shape[1:]
    args = (left_mine, left_other, by_a, by_b, *blocks)
    return pl.pallas_call(
        functools.partial(first_kernel, chunk),
        out_shape=[jax.ShapeDtypeStruct(shape, jnp.bfloat16)] * 2,
        in_specs=[WHOLE] * len(args),
        out_specs=[WHOLE] * 2,
        compiler_params=PARAMS,
        cost_estimate=COST,
        name="first_step",
    )(*args)


def partial_kernel(n, left_mine, left_other, *refs):
    blocks, outs, sums = refs[:n], refs[n : 2 * n], refs[2 * n]
    row, holders = lax.axis_index("row"), slot_chips(n)
    for c in range(STEP):
        lhs = jnp.concatenate((left_mine[c], left_other[c]), axis=0)
        for holder, block in zip(holders, blocks):
            away = lax.rem(holder - row + n, n)
            sums[away, c] = lax.dot_general(lhs, block[c], BY_LAST, preferred_element_type=jnp.float32).astype(jnp.bfloat16)
    for s, out in enumerate(outs):
        out[...] = sums[s]


def partial_products(left_mine, left_other, blocks, chunk):
    chans, rows, _ = blocks[0].shape
    ks = left_mine.shape[1]
    n = len(blocks)
    args = (left_mine, left_other, *blocks)
    return pl.pallas_call(
        functools.partial(partial_kernel, n),
        out_shape=[pltpu.HBM((chans, CORES * ks, rows), jnp.bfloat16)] * n,
        grid=(chans // STEP,),
        in_specs=[chunk_spec(v, chans, chunk) for v in args],
        out_specs=[pl.BlockSpec((STEP, CORES * ks, rows), lambda g: (g, 0, 0))] * n,
        scratch_shapes=[pltpu.VMEM((n, STEP, CORES * ks, rows), jnp.bfloat16)],
        compiler_params=PARAMS,
        cost_estimate=COST,
        name="right_partials",
    )(*args)


def left_kernel(n, own, *refs):
    by_a, by_b, refs = refs[: n - 1], refs[n - 1 : 2 * n - 2], refs[2 * n - 2 :]
    blocks, (mine, theirs, panel) = refs[:n], refs[n:]
    row, holders = lax.axis_index("row"), slot_chips(n)
    even = lanes(n)[0]
    ks = mine.shape[1]
    for c in range(STEP):
        for holder, block in zip(holders, blocks):
            panel[c, holder] = block[c]
        acts, grads = [own[c]], [panel[c, row]]
        for s in range(1, n):
            from_above = jnp.where(even, by_a[s - 1][c], by_b[s - 1][c])
            from_below = jnp.where(even, by_b[n - s - 1][c], by_a[n - s - 1][c])
            acts.append(jnp.where(row + s < n, from_above, from_below))
            grads.append(panel[c, lax.rem(row + s, n)])
        out = jnp.dot(
            jnp.concatenate(acts, axis=1), jnp.concatenate(grads, axis=0), preferred_element_type=jnp.float32
        )
        mine[c] = out[:ks]
        theirs[c] = out[ks:].astype(jnp.bfloat16)


def left_products(own, by_a, by_b, blocks, chunk):
    chans, ks, rows = by_a[-1].shape
    n = len(blocks)
    out = pl.BlockSpec((STEP, ks // CORES, rows), lambda g: (g, 0, 0))
    args = (own, *by_a, *by_b, *blocks)
    return pl.pallas_call(
        functools.partial(left_kernel, n),
        out_shape=[
            jax.ShapeDtypeStruct((chans, ks // CORES, rows), jnp.float32),
            jax.ShapeDtypeStruct((chans, ks // CORES, rows), jnp.bfloat16),
        ],
        grid=(chans // STEP,),
        in_specs=[chunk_spec(v, chans, chunk) for v in args],
        out_specs=[out] * 2,
        scratch_shapes=[pltpu.VMEM((STEP, n, rows, rows), jnp.bfloat16)],
        compiler_params=PARAMS,
        cost_estimate=COST,
        name="left_products",
    )(*args)


def arrived_total(own, by_a, by_b, n):
    _, use_a, use_b = lanes(n)
    total = own.astype(jnp.float32) + jnp.where(use_a, by_a.astype(jnp.float32), 0.0)
    return total + jnp.where(use_b, by_b.astype(jnp.float32), 0.0)


def put(flat, owner, value):
    size = value.shape[0] * value.shape[1]
    flat[pl.ds(pl.multiple_of(owner * size, size), size), :] = value.astype(jnp.float32).reshape(size, value.shape[2])


def known_kernel(n, factors, weight, *refs):
    known = CHUNKS - 1
    left_mine, left_other = refs[:CHUNKS], refs[CHUNKS : 2 * CHUNKS]
    partials, by_a, by_b, right_other = (refs[2 * CHUNKS + i * known : 2 * CHUNKS + (i + 1) * known] for i in range(4))
    out, grads, *flats = refs[2 * CHUNKS + 4 * known :]
    keys, width, _ = factors.shape
    hidden = width // 4
    part = hidden // CORES // CHUNKS
    core = this_core()

    @pl.when(pl.program_id(0) == 0)
    def _():
        grads[...] = jnp.zeros_like(grads)

    for chunk in range(CHUNKS):
        put(flats[chunk], core, left_mine[chunk][...])
        put(flats[chunk], 1 - core, left_other[chunk][...])
    for chunk in range(known):
        put(flats[CHUNKS + chunk], core, arrived_total(partials[chunk][...], by_a[chunk][...], by_b[chunk][...], n))
        put(flats[CHUNKS + chunk], 1 - core, right_other[chunk][...])
    for key in range(keys):
        for i, flat in enumerate(flats):
            side, chunk = divmod(i, CHUNKS)
            grad = flat[pl.ds(key, CORES * part, stride=keys), :]
            for owner in range(CORES):
                for kind in range(2):
                    first = (2 * side + kind) * hidden + (owner * CHUNKS + chunk) * part
                    place = slice(first, first + part)
                    factor = factors[key, place, :].astype(jnp.float32)
                    grads[key, place, :] = (grad[owner * part : (owner + 1) * part] * factor).astype(jnp.bfloat16)
    for key in range(keys):
        out[key] = jnp.dot(weight[...], grads[key], preferred_element_type=jnp.float32)


def known(factors, proj_weight, left_mine, left_other, partials, by_a, by_b, right_other):
    cols, width, rows = factors.shape
    chans, hidden = proj_weight.shape[0], width // 4
    part = hidden // CORES // CHUNKS
    by_key = lambda *shape: pl.BlockSpec((KEYS,) + shape, lambda g: (g, 0, 0))
    args = (*left_mine, *left_other, *partials, *by_a, *by_b, *right_other)
    return pl.pallas_call(
        functools.partial(known_kernel, lax.axis_size("row")),
        out_shape=jax.ShapeDtypeStruct((cols, chans, rows), jnp.float32),
        grid=(cols // KEYS,),
        in_specs=[by_key(width, rows), pl.BlockSpec((chans, width), lambda g: (0, 0))]
        + [pl.BlockSpec((part, KEYS, rows), lambda g: (0, g, 0))] * len(args),
        out_specs=by_key(chans, rows),
        scratch_shapes=[pltpu.VMEM((KEYS, width, rows), jnp.bfloat16)]
        + [pltpu.VMEM(((CORES * part + 1) * KEYS, rows), jnp.float32)] * (2 * CHUNKS - 1),
        compiler_params=PARAMS,
        cost_estimate=COST,
        name="known",
    )(factors, proj_weight, *args)


def tail_kernel(n, base, scaled, inverse, last, gain, weight, partials, by_a, by_b, right_other, out, results, flipped, grads, flat, gain_col):
    _, keys, chans = out.shape
    rows = scaled.shape[2]
    core = this_core()

    @pl.when(pl.program_id(0) == 0)
    def _():
        gain_col[...] = column(gain, rows)

    first_key = pl.program_id(0) * keys
    here = pl.ds(pl.multiple_of(first_key, keys), keys)
    put(flat, core, arrived_total(partials[:, here, :], by_a[:, here, :], by_b[:, here, :], n))
    put(flat, 1 - core, right_other[:, here, :])
    count = last.shape[1] // 2
    for key in range(keys):
        grad = flat[pl.ds(key, count, stride=keys), :]
        for kind in range(2):
            place = slice(kind * count, (kind + 1) * count)
            grads[key, place, :] = (grad * last[first_key + key, place, :].astype(jnp.float32)).astype(jnp.bfloat16)
    for key in range(keys):
        scaled_key = scaled[first_key + key].astype(jnp.float32)
        added = jnp.dot(weight[...], grads[key], preferred_element_type=jnp.float32)
        scaled_grad = (base[first_key + key] + added) * gain_col[...]
        result = inverse[first_key + key] * (
            scaled_grad
            - jnp.mean(scaled_grad, axis=0, keepdims=True)
            - scaled_key * jnp.mean(scaled_grad * scaled_key, axis=0, keepdims=True)
        )
        results[key] = result.astype(jnp.bfloat16)
    eye = identity(rows)
    for key in range(keys):
        if key % 2:
            turned = lax.dot_general(eye, results[key], BY_LAST, preferred_element_type=jnp.float32)
            flipped[key] = turned.astype(jnp.bfloat16)
        else:
            flipped[key] = results[key].T
    out[...] = jnp.transpose(flipped[...], (1, 0, 2))


def tail(base, scaled, inverse, last, gain, proj_weight, partials, by_a, by_b, right_other):
    cols, chans, rows = scaled.shape
    hidden, part = proj_weight.shape[1] // 4, partials.shape[0]
    weight = jnp.concatenate([proj_weight[:, first : first + size] for first, size in last_rows(hidden)], axis=1)
    return pl.pallas_call(
        functools.partial(tail_kernel, lax.axis_size("row")),
        out_shape=jax.ShapeDtypeStruct((rows, cols, chans), jnp.bfloat16),
        grid=(cols // KEYS,),
        in_specs=[WHOLE] * 10,
        out_specs=pl.BlockSpec((rows, KEYS, chans), lambda g: (0, g, 0)),
        scratch_shapes=[
            pltpu.VMEM((KEYS, chans, rows), jnp.bfloat16),
            pltpu.VMEM((KEYS, rows, chans), jnp.bfloat16),
            pltpu.VMEM((KEYS, last.shape[1], rows), jnp.bfloat16),
            pltpu.VMEM(((CORES * part + 1) * KEYS, rows), jnp.float32),
            pltpu.VMEM((chans, rows), jnp.float32),
        ],
        compiler_params=PARAMS,
        cost_estimate=COST,
        name="tail",
    )(base, scaled, inverse, last, gain, weight, partials, by_a, by_b, right_other)


def after(value, *others):
    return lax.optimization_barrier((value, others))[0]


def shards(pair, grad_x, norm_gain, norm_bias, proj_weight, tile_mask):
    n, n_col = lax.axis_size("row"), lax.axis_size("col")
    half = grad_x.shape[2] // CORES
    part = half // CHUNKS
    gain, bias = norm_gain[None, :], norm_bias[None, :]

    def exchange(value, mask):
        return lax.ppermute(value, "col", [(d, d ^ mask) for d in range(n_col)])

    def hop(value, first):
        pairs = {r: r + 1 for r in range(first, n - 1, 2)}
        pairs.update({above: r for r, above in pairs.items()})
        perm = [
            (r * n_col + d, pairs[r] * n_col + d if r in pairs else r * n_col + (d ^ 1)) for r in range(n) for d in range(n_col)
        ]
        return lax.ppermute(value, ("row", "col"), perm)

    raw = jnp.transpose(grad_x, (1, 2, 0))
    other = exchange(take_half(raw, True), 1)
    packed = pack(take_half(raw, False), other)

    chips = n_col // CORES

    def along(value, bit):
        mask = [CORES * slot_mask(bit, core, chips) for core in range(CORES)]
        return lax.ppermute(value, "col", [(d, d ^ mask[d % CORES]) for d in range(n_col)])

    panels = []
    for block in packed:
        slots = [after(block, panels[-1][1:]) if panels else block]
        for m in range(1, chips):
            bit = 1 << (m.bit_length() - 1)
            slots.append(along(slots[m ^ bit], bit))
        panels.append(slots)

    right_mine, right_theirs = front(after(pair, packed), gain, bias, proj_weight, tile_mask, True)
    own = jnp.concatenate((right_mine, exchange(right_theirs, 1)), axis=1)
    first_a, first_b = hop(own, 0), hop(own, 1)
    left_mine, left_theirs, *forward = front(after(pair, own, panels[0][-2]), gain, bias, proj_weight, tile_mask, False)
    left_other = exchange(left_theirs, 1)

    by_a, by_b, partials = [], [], []
    for c in range(CHUNKS):
        ready = after(left_other, partials[-1]) if partials else left_other
        next_a, next_b = first_step(left_mine, ready, first_a, first_b, panels[c], c)
        partials.append(partial_products(left_mine, left_other, panels[c], c))
        by_a.append([first_a, hop(next_a, 0)])
        by_b.append([first_b, hop(next_b, 1)])

    left_grads = []
    for t in range(2, n):
        for c in range(CHUNKS):
            value = by_a[c][-1]
            if t == n - 1 and c > 0:
                value = after(value, left_grads[c - 1])
            next_a, next_b = onward(value, by_b[c][-1], partials[c][n - t], partials[c][t], t, n)
            by_a[c].append(hop(next_a, 0))
            by_b[c].append(hop(next_b, 1))
            if t == n - 1:
                left_grads.append(left_products(own, by_a[c][: n - 1], by_b[c][: n - 1], panels[c], c))
    left_grad_other = [exchange(theirs, 1) for _, theirs in left_grads]
    ks = left_mine.shape[1]
    scaled, inverse, factors, last = forward
    own_sums, last_a, last_b = [sums[0] for sums in partials], [v[-1] for v in by_a], [v[-1] for v in by_b]
    right_grad_other = []
    for c in range(CHUNKS):
        value = own_sums[c]
        if c == CHUNKS - 1:
            base = known(
                factors,
                proj_weight,
                [mine for mine, _ in left_grads],
                left_grad_other,
                own_sums[:c],
                last_a[:c],
                last_b[:c],
                right_grad_other,
            )
            value = after(value, base)
        total = arrived_total(value[:, ks:], last_a[c][:, ks:], last_b[c][:, ks:], n)
        right_grad_other.append(exchange(total.astype(jnp.bfloat16), 1))
    return tail(
        base, scaled, inverse, last, gain, proj_weight, own_sums[-1], last_a[-1], last_b[-1], right_grad_other[-1]
    )


def solution(mesh):
    placed = (P("row", "col", None), P("row", "col", None), P(), P(), P(), P())
    return jax.shard_map(
        shards, mesh=mesh, in_specs=placed, out_specs=P("row", "col", None), check_vma=False
    )
```

```python
import functools

import jax
import jax.numpy as jnp
from jax import lax
from jax.experimental import pallas as pl
from jax.experimental.pallas import tpu as pltpu
from jax.sharding import PartitionSpec as P

BLK = 128
CHUNKS = 2
STEP = 8
KEYS = 16
CORES = 2
VMEM_LIMIT = 18 * 1024 * 1024
PARAMS = pltpu.CompilerParams(vmem_limit_bytes=VMEM_LIMIT)
FRONT_COST = pl.CostEstimate(flops=1, bytes_accessed=18_000_000, transcendentals=0)
COST = pl.CostEstimate(flops=1, bytes_accessed=8_000_000, transcendentals=0)
WHOLE = pl.BlockSpec(memory_space=pltpu.VMEM)
BY_LAST = (((1,), (1,)), ((), ()))


def identity(size):
    return (
        lax.broadcasted_iota(jnp.int32, (size, size), 0) == lax.broadcasted_iota(jnp.int32, (size, size), 1)
    ).astype(jnp.bfloat16)


def column(vector_ref, rows):
    return jnp.broadcast_to(vector_ref[...], (rows, vector_ref.shape[1])).T


def unit_mask(mask_ref, rows, cols):
    row, col = lax.axis_index("row"), lax.axis_index("col")
    return mask_ref[(row * rows) // BLK, (col * cols) // BLK].astype(jnp.float32)


def in_hbm(*values):
    return [pltpu.with_memory_space_constraint(v, pltpu.HBM) for v in values]


def this_core():
    return lax.rem(lax.axis_index("col"), CORES)


def turn(pair, flipped, turned):
    flipped[...] = jnp.transpose(pair[...], (1, 0, 2))
    eye = identity(pair.shape[2])
    for key in range(pair.shape[1]):
        if key % 2:
            turned[key] = lax.dot_general(eye, flipped[key], BY_LAST, preferred_element_type=jnp.float32)
        else:
            turned[key] = flipped[key].T.astype(jnp.float32)


def normalize(values):
    centred = values - jnp.mean(values, axis=1, keepdims=True)
    inverse = lax.rsqrt(jnp.mean(centred * centred, axis=1, keepdims=True) + 1e-05)
    return centred * inverse, inverse


def set_columns(gain, bias, weight, gain_col, bias_col, weight_t):
    @pl.when(pl.program_id(0) == 0)
    def _():
        gain_col[...] = column(gain, gain_col.shape[1])
        bias_col[...] = column(bias, bias_col.shape[1])
        weight_t[...] = weight[...].astype(jnp.float32).T.astype(jnp.bfloat16)


def normalized(pair, gain_col, bias_col, flipped, turned, normed):
    turn(pair, flipped, turned)
    scaled, inverse = normalize(turned[...])
    normed[...] = (scaled * gain_col[...] + bias_col[...]).astype(jnp.bfloat16)
    return scaled, inverse


def split_channels(acts, whole, mine, theirs):
    half = mine.shape[0]
    whole[...] = jnp.transpose(acts[...], (1, 0, 2))
    core = this_core()
    mine[...] = whole[pl.ds(core * half, half)]
    theirs[...] = whole[pl.ds((1 - core) * half, half)]


def right_kernel(mask, pair, gain, bias, weight, mine, theirs, flipped, turned, normed, acts, whole, gain_col, bias_col, weight_t):
    rows, keys, _ = pair.shape
    hidden = acts.shape[1]
    set_columns(gain, bias, weight, gain_col, bias_col, weight_t)
    valid = unit_mask(mask, rows, pl.num_programs(0) * keys)
    normalized(pair, gain_col, bias_col, flipped, turned, normed)
    for key in range(keys):
        projected = jnp.dot(weight_t[...], normed[key], preferred_element_type=jnp.float32)
        acts[key] = (valid * jax.nn.sigmoid(projected[hidden:]) * projected[:hidden]).astype(jnp.bfloat16)
    split_channels(acts, whole, mine, theirs)


def last_rows(hidden):
    part = hidden // CORES // CHUNKS
    return [((2 + kind) * hidden + (core * CHUNKS + CHUNKS - 1) * part, part) for kind in range(2) for core in range(CORES)]


def left_forward_kernel(
    mask, pair, gain, bias, weight, mine, theirs, scaled_out, inverse_out, factors, last,
    flipped, turned, normed, acts, whole, gain_col, bias_col, weight_t,
):
    rows, keys, _ = pair.shape
    hidden = acts.shape[1]
    set_columns(gain, bias, weight, gain_col, bias_col, weight_t)
    valid = unit_mask(mask, rows, pl.num_programs(0) * keys)
    scaled, inverse = normalized(pair, gain_col, bias_col, flipped, turned, normed)
    scaled_out[...] = scaled.astype(jnp.bfloat16)
    inverse_out[...] = inverse
    for key in range(keys):
        projected = jnp.dot(weight_t[...], normed[key], preferred_element_type=jnp.float32)
        for side in range(2):
            first = 2 * side * hidden
            lin = projected[first : first + hidden]
            sig = jax.nn.sigmoid(projected[first + hidden : first + 2 * hidden])
            masked = valid * sig
            act = masked * lin
            if side == 0:
                acts[key] = act.astype(jnp.bfloat16)
            factors[key, first : first + hidden, :] = masked.astype(jnp.bfloat16)
            factors[key, first + hidden : first + 2 * hidden, :] = (act * (1.0 - sig)).astype(jnp.bfloat16)
    for i, (first, size) in enumerate(last_rows(hidden)):
        last[:, i * size : (i + 1) * size, :] = factors[:, first : first + size, :]
    split_channels(acts, whole, mine, theirs)


def front(pair, gain, bias, proj_weight, tile_mask, right):
    rows, cols, chans = pair.shape
    width = proj_weight.shape[1]
    hidden = width // 4
    half = hidden // CORES
    used = width // 2 if right else width
    vector = pl.BlockSpec((1, chans), lambda g: (0, 0))
    by_key = lambda *shape: pl.BlockSpec((KEYS,) + shape, lambda g: (g, 0, 0))
    out_shape = [jax.ShapeDtypeStruct((half, cols, rows), jnp.bfloat16)] * 2
    out_specs = [pl.BlockSpec((half, KEYS, rows), lambda g: (0, g, 0))] * 2
    if not right:
        out_shape += [
            jax.ShapeDtypeStruct((cols, chans, rows), jnp.bfloat16),
            jax.ShapeDtypeStruct((cols, 1, rows), jnp.float32),
            jax.ShapeDtypeStruct((cols, width, rows), jnp.bfloat16),
            jax.ShapeDtypeStruct((cols, 2 * hidden // CHUNKS, rows), jnp.bfloat16),
        ]
        out_specs += [by_key(chans, rows), by_key(1, rows), by_key(width, rows), by_key(2 * hidden // CHUNKS, rows)]
    return pl.pallas_call(
        right_kernel if right else left_forward_kernel,
        out_shape=out_shape,
        grid=(cols // KEYS,),
        in_specs=[
            pl.BlockSpec(memory_space=pltpu.SMEM),
            pl.BlockSpec((rows, KEYS, chans), lambda g: (0, g, 0)),
            vector,
            vector,
            pl.BlockSpec((chans, used), lambda g: (0, 1 if right else 0)),
        ],
        out_specs=out_specs,
        scratch_shapes=[
            pltpu.VMEM((KEYS, rows, chans), jnp.bfloat16),
            pltpu.VMEM((KEYS, chans, rows), jnp.float32),
            pltpu.VMEM((KEYS, chans, rows), jnp.bfloat16),
            pltpu.VMEM((KEYS, hidden, rows), jnp.bfloat16),
            pltpu.VMEM((hidden, KEYS, rows), jnp.bfloat16),
            pltpu.VMEM((chans, rows), jnp.float32),
            pltpu.VMEM((chans, rows), jnp.float32),
            pltpu.VMEM((used, chans), jnp.bfloat16),
        ],
        compiler_params=PARAMS,
        cost_estimate=FRONT_COST,
        name="right_front" if right else "left_front",
    )(tile_mask, *in_hbm(pair, gain, bias, proj_weight))


def half_kernel(theirs, raw, out, sem):
    half = out.shape[1]
    core = this_core()
    first = pl.multiple_of((1 - core if theirs else core) * half, half)
    copy = pltpu.make_async_copy(raw.at[:, pl.ds(first, half), :], out, sem)
    copy.start()
    copy.wait()


def take_half(raw, theirs):
    cols, hidden, rows = raw.shape
    return pl.pallas_call(
        functools.partial(half_kernel, theirs),
        out_shape=jax.ShapeDtypeStruct((cols, hidden // CORES, rows), raw.dtype),
        in_specs=[pl.BlockSpec(memory_space=pl.ANY)],
        out_specs=WHOLE,
        scratch_shapes=[pltpu.SemaphoreType.DMA],
        compiler_params=PARAMS,
        cost_estimate=COST,
        name="theirs" if theirs else "mine",
    )(*in_hbm(raw))


def pack_kernel(own, other, *outs):
    cols = other.shape[0]
    core = this_core()
    for block, place in ((own, core), (other, 1 - core)):
        flipped = jnp.transpose(block[...], (1, 0, 2))
        for chunk, out in enumerate(outs):
            chans = out.shape[0]
            out[:, pl.ds(pl.multiple_of(place * cols, cols), cols), :] = flipped[chunk * chans : (chunk + 1) * chans]


def pack(own, other):
    cols, half, rows = other.shape
    return pl.pallas_call(
        pack_kernel,
        out_shape=[jax.ShapeDtypeStruct((half // CHUNKS, CORES * cols, rows), jnp.bfloat16)] * CHUNKS,
        in_specs=[WHOLE] * 2,
        out_specs=[WHOLE] * CHUNKS,
        compiler_params=PARAMS,
        cost_estimate=COST,
        name="pack",
    )(own, other)


def chunk_spec(array, chans, chunk):
    first = chunk * chans // STEP if array.shape[0] > chans else 0
    return pl.BlockSpec((STEP,) + array.shape[1:], lambda g: (first + g, 0, 0))


def slot_mask(m, core, chips):
    width = chips.bit_length() - 1
    return m if core == 0 else sum(1 << (width - 1 - b) for b in range(width) if m >> b & 1)


def slot_chips(chips):
    chip = lax.axis_index("col") // CORES
    return [
        jnp.bitwise_xor(chip, jnp.where(this_core() == 0, m, slot_mask(m, 1, chips))) for m in range(chips)
    ]


def lanes(n):
    row = lax.axis_index("row")
    even = lax.rem(row, 2) == 0
    return even, jnp.where(even, row + 1 < n, True), jnp.where(even, row > 0, row + 1 < n)


def onward(by_a, by_b, up_sums, down_sums, t, n):
    row = lax.axis_index("row")
    even, use_a, use_b = lanes(n)
    up = jnp.where(row < t, up_sums.astype(jnp.float32), 0.0)
    down = jnp.where(row >= n - t, down_sums.astype(jnp.float32), 0.0)
    out_a = jnp.where(use_b, by_b.astype(jnp.float32), 0.0) + jnp.where(even, up, down)
    out_b = jnp.where(use_a, by_a.astype(jnp.float32), 0.0) + jnp.where(even, down, up)
    return out_a.astype(jnp.bfloat16), out_b.astype(jnp.bfloat16)


def first_kernel(chunk, left_mine, left_other, by_a, by_b, *refs):
    *blocks, next_a, next_b = refs
    n = len(blocks)
    holders, target = slot_chips(n), jnp.where(lax.axis_index("row") == 0, n - 1, 0)
    chans = next_a.shape[0]
    for c in range(chans):
        at = chunk * chans + c
        lhs = jnp.concatenate((left_mine[at], left_other[at]), axis=0)
        rhs = blocks[0][c]
        for m in range(1, n):
            rhs = jnp.where(holders[m] == target, blocks[m][c], rhs)
        sums = lax.dot_general(lhs, rhs, BY_LAST, preferred_element_type=jnp.float32).astype(jnp.bfloat16)
        next_a[c], next_b[c] = onward(by_a[at], by_b[at], sums, sums, 1, n)


def first_step(left_mine, left_other, by_a, by_b, blocks, chunk):
    shape = (left_mine.shape[0] // CHUNKS,) + by_a.shape[1:]
    args = (left_mine, left_other, by_a, by_b, *blocks)
    return pl.pallas_call(
        functools.partial(first_kernel, chunk),
        out_shape=[jax.ShapeDtypeStruct(shape, jnp.bfloat16)] * 2,
        in_specs=[WHOLE] * len(args),
        out_specs=[WHOLE] * 2,
        compiler_params=PARAMS,
        cost_estimate=COST,
        name="first_step",
    )(*args)


def partial_kernel(n, left_mine, left_other, *refs):
    blocks, outs, sums = refs[:n], refs[n : 2 * n], refs[2 * n]
    row, holders = lax.axis_index("row"), slot_chips(n)
    for c in range(STEP):
        lhs = jnp.concatenate((left_mine[c], left_other[c]), axis=0)
        for holder, block in zip(holders, blocks):
            away = lax.rem(holder - row + n, n)
            sums[away, c] = lax.dot_general(lhs, block[c], BY_LAST, preferred_element_type=jnp.float32).astype(jnp.bfloat16)
    for s, out in enumerate(outs):
        out[...] = sums[s]


def partial_products(left_mine, left_other, blocks, chunk):
    chans, rows, _ = blocks[0].shape
    ks = left_mine.shape[1]
    n = len(blocks)
    args = (left_mine, left_other, *blocks)
    return pl.pallas_call(
        functools.partial(partial_kernel, n),
        out_shape=[
            (jax.ShapeDtypeStruct if s in (2, n - 2) else pltpu.HBM)((chans, CORES * ks, rows), jnp.bfloat16)
            for s in range(n)
        ],
        grid=(chans // STEP,),
        in_specs=[chunk_spec(v, chans, chunk) for v in args],
        out_specs=[pl.BlockSpec((STEP, CORES * ks, rows), lambda g: (g, 0, 0))] * n,
        scratch_shapes=[pltpu.VMEM((n, STEP, CORES * ks, rows), jnp.bfloat16)],
        compiler_params=PARAMS,
        cost_estimate=COST,
        name="right_partials",
    )(*args)


def advance_kernel(t, n, by_a, by_b, up_sums, down_sums, next_a, next_b):
    next_a[...], next_b[...] = onward(by_a[...], by_b[...], up_sums[...], down_sums[...], t, n)


def advance(by_a, by_b, sums, t):
    n = len(sums)
    return pl.pallas_call(
        functools.partial(advance_kernel, t, n),
        out_shape=[jax.ShapeDtypeStruct(by_a.shape, by_a.dtype)] * 2,
        in_specs=[WHOLE] * 4,
        out_specs=[WHOLE] * 2,
        compiler_params=PARAMS,
        cost_estimate=COST,
        name="advance",
    )(by_a, by_b, sums[n - t], sums[t])


def left_kernel(n, own, *refs):
    by_a, by_b, refs = refs[: n - 1], refs[n - 1 : 2 * n - 2], refs[2 * n - 2 :]
    blocks, (mine, theirs, panel) = refs[:n], refs[n:]
    row, holders = lax.axis_index("row"), slot_chips(n)
    even = lanes(n)[0]
    ks = mine.shape[1]
    for c in range(STEP):
        for holder, block in zip(holders, blocks):
            panel[c, holder] = block[c]
        acts, grads = [own[c]], [panel[c, row]]
        for s in range(1, n):
            from_above = jnp.where(even, by_a[s - 1][c], by_b[s - 1][c])
            from_below = jnp.where(even, by_b[n - s - 1][c], by_a[n - s - 1][c])
            acts.append(jnp.where(row + s < n, from_above, from_below))
            grads.append(panel[c, lax.rem(row + s, n)])
        out = jnp.dot(
            jnp.concatenate(acts, axis=1), jnp.concatenate(grads, axis=0), preferred_element_type=jnp.float32
        )
        mine[c] = out[:ks]
        theirs[c] = out[ks:].astype(jnp.bfloat16)


def left_products(own, by_a, by_b, blocks, chunk):
    chans, ks, rows = by_a[-1].shape
    n = len(blocks)
    out = pl.BlockSpec((STEP, ks // CORES, rows), lambda g: (g, 0, 0))
    args = (own, *by_a, *by_b, *blocks)
    return pl.pallas_call(
        functools.partial(left_kernel, n),
        out_shape=[
            jax.ShapeDtypeStruct((chans, ks // CORES, rows), jnp.float32),
            jax.ShapeDtypeStruct((chans, ks // CORES, rows), jnp.bfloat16),
        ],
        grid=(chans // STEP,),
        in_specs=[chunk_spec(v, chans, chunk) for v in args],
        out_specs=[out] * 2,
        scratch_shapes=[pltpu.VMEM((STEP, n, rows, rows), jnp.bfloat16)],
        compiler_params=PARAMS,
        cost_estimate=COST,
        name="left_products",
    )(*args)


def arrived_total(own, by_a, by_b, n):
    _, use_a, use_b = lanes(n)
    total = own.astype(jnp.float32) + jnp.where(use_a, by_a.astype(jnp.float32), 0.0)
    return total + jnp.where(use_b, by_b.astype(jnp.float32), 0.0)


def put(flat, owner, value):
    size = value.shape[0] * value.shape[1]
    flat[pl.ds(pl.multiple_of(owner * size, size), size), :] = value.astype(jnp.float32).reshape(size, value.shape[2])


def known_kernel(n, factors, weight, *refs):
    known = CHUNKS - 1
    left_mine, left_other = refs[:CHUNKS], refs[CHUNKS : 2 * CHUNKS]
    partials, by_a, by_b, right_other = (refs[2 * CHUNKS + i * known : 2 * CHUNKS + (i + 1) * known] for i in range(4))
    out, grads, *flats = refs[2 * CHUNKS + 4 * known :]
    keys, width, _ = factors.shape
    hidden = width // 4
    part = hidden // CORES // CHUNKS
    core = this_core()

    @pl.when(pl.program_id(0) == 0)
    def _():
        grads[...] = jnp.zeros_like(grads)

    for chunk in range(CHUNKS):
        put(flats[chunk], core, left_mine[chunk][...])
        put(flats[chunk], 1 - core, left_other[chunk][...])
    for chunk in range(known):
        put(flats[CHUNKS + chunk], core, arrived_total(partials[chunk][...], by_a[chunk][...], by_b[chunk][...], n))
        put(flats[CHUNKS + chunk], 1 - core, right_other[chunk][...])
    for key in range(keys):
        for i, flat in enumerate(flats):
            side, chunk = divmod(i, CHUNKS)
            grad = flat[pl.ds(key, CORES * part, stride=keys), :]
            for owner in range(CORES):
                for kind in range(2):
                    first = (2 * side + kind) * hidden + (owner * CHUNKS + chunk) * part
                    place = slice(first, first + part)
                    factor = factors[key, place, :].astype(jnp.float32)
                    grads[key, place, :] = (grad[owner * part : (owner + 1) * part] * factor).astype(jnp.bfloat16)
    for key in range(keys):
        out[key] = jnp.dot(weight[...], grads[key], preferred_element_type=jnp.float32)


def known(factors, proj_weight, left_mine, left_other, partials, by_a, by_b, right_other):
    cols, width, rows = factors.shape
    chans, hidden = proj_weight.shape[0], width // 4
    part = hidden // CORES // CHUNKS
    by_key = lambda *shape: pl.BlockSpec((KEYS,) + shape, lambda g: (g, 0, 0))
    args = (*left_mine, *left_other, *partials, *by_a, *by_b, *right_other)
    return pl.pallas_call(
        functools.partial(known_kernel, lax.axis_size("row")),
        out_shape=jax.ShapeDtypeStruct((cols, chans, rows), jnp.float32),
        grid=(cols // KEYS,),
        in_specs=[by_key(width, rows), pl.BlockSpec((chans, width), lambda g: (0, 0))]
        + [pl.BlockSpec((part, KEYS, rows), lambda g: (0, g, 0))] * len(args),
        out_specs=by_key(chans, rows),
        scratch_shapes=[pltpu.VMEM((KEYS, width, rows), jnp.bfloat16)]
        + [pltpu.VMEM(((CORES * part + 1) * KEYS, rows), jnp.float32)] * (2 * CHUNKS - 1),
        compiler_params=PARAMS,
        cost_estimate=COST,
        name="known",
    )(factors, proj_weight, *args)


def tail_kernel(n, base, scaled, inverse, last, gain, weight, partials, by_a, by_b, right_other, out, results, flipped, grads, flat, gain_col):
    _, keys, chans = out.shape
    rows = scaled.shape[2]
    core = this_core()

    @pl.when(pl.program_id(0) == 0)
    def _():
        gain_col[...] = column(gain, rows)

    first_key = pl.program_id(0) * keys
    here = pl.ds(pl.multiple_of(first_key, keys), keys)
    put(flat, core, arrived_total(partials[:, here, :], by_a[:, here, :], by_b[:, here, :], n))
    put(flat, 1 - core, right_other[:, here, :])
    count = last.shape[1] // 2
    for key in range(keys):
        grad = flat[pl.ds(key, count, stride=keys), :]
        for kind in range(2):
            place = slice(kind * count, (kind + 1) * count)
            grads[key, place, :] = (grad * last[first_key + key, place, :].astype(jnp.float32)).astype(jnp.bfloat16)
    for key in range(keys):
        scaled_key = scaled[first_key + key].astype(jnp.float32)
        added = jnp.dot(weight[...], grads[key], preferred_element_type=jnp.float32)
        scaled_grad = (base[first_key + key] + added) * gain_col[...]
        result = inverse[first_key + key] * (
            scaled_grad
            - jnp.mean(scaled_grad, axis=0, keepdims=True)
            - scaled_key * jnp.mean(scaled_grad * scaled_key, axis=0, keepdims=True)
        )
        results[key] = result.astype(jnp.bfloat16)
    eye = identity(rows)
    for key in range(keys):
        if key % 2:
            turned = lax.dot_general(eye, results[key], BY_LAST, preferred_element_type=jnp.float32)
            flipped[key] = turned.astype(jnp.bfloat16)
        else:
            flipped[key] = results[key].T
    out[...] = jnp.transpose(flipped[...], (1, 0, 2))


def tail(base, scaled, inverse, last, gain, proj_weight, partials, by_a, by_b, right_other):
    cols, chans, rows = scaled.shape
    hidden, part = proj_weight.shape[1] // 4, partials.shape[0]
    weight = jnp.concatenate([proj_weight[:, first : first + size] for first, size in last_rows(hidden)], axis=1)
    return pl.pallas_call(
        functools.partial(tail_kernel, lax.axis_size("row")),
        out_shape=jax.ShapeDtypeStruct((rows, cols, chans), jnp.bfloat16),
        grid=(cols // KEYS,),
        in_specs=[WHOLE] * 10,
        out_specs=pl.BlockSpec((rows, KEYS, chans), lambda g: (0, g, 0)),
        scratch_shapes=[
            pltpu.VMEM((KEYS, chans, rows), jnp.bfloat16),
            pltpu.VMEM((KEYS, rows, chans), jnp.bfloat16),
            pltpu.VMEM((KEYS, last.shape[1], rows), jnp.bfloat16),
            pltpu.VMEM(((CORES * part + 1) * KEYS, rows), jnp.float32),
            pltpu.VMEM((chans, rows), jnp.float32),
        ],
        compiler_params=PARAMS,
        cost_estimate=COST,
        name="tail",
    )(base, scaled, inverse, last, gain, weight, partials, by_a, by_b, right_other)


def after(value, *others):
    return lax.optimization_barrier((value, others))[0]


def shards(pair, grad_x, norm_gain, norm_bias, proj_weight, tile_mask):
    n, n_col = lax.axis_size("row"), lax.axis_size("col")
    half = grad_x.shape[2] // CORES
    part = half // CHUNKS
    gain, bias = norm_gain[None, :], norm_bias[None, :]

    def exchange(value, mask):
        return lax.ppermute(value, "col", [(d, d ^ mask) for d in range(n_col)])

    def hop(value, first):
        pairs = {r: r + 1 for r in range(first, n - 1, 2)}
        pairs.update({above: r for r, above in pairs.items()})
        perm = [
            (r * n_col + d, pairs[r] * n_col + d if r in pairs else r * n_col + (d ^ 1)) for r in range(n) for d in range(n_col)
        ]
        return lax.ppermute(value, ("row", "col"), perm)

    raw = jnp.transpose(grad_x, (1, 2, 0))
    other = exchange(take_half(raw, True), 1)
    packed = pack(take_half(raw, False), other)

    chips = n_col // CORES

    def along(value, bit):
        mask = [CORES * slot_mask(bit, core, chips) for core in range(CORES)]
        return lax.ppermute(value, "col", [(d, d ^ mask[d % CORES]) for d in range(n_col)])

    panels = []
    for block in packed:
        slots = [after(block, panels[-1][1:]) if panels else block]
        for m in range(1, chips):
            bit = 1 << (m.bit_length() - 1)
            slots.append(along(slots[m ^ bit], bit))
        panels.append(slots)

    right_mine, right_theirs = front(after(pair, packed), gain, bias, proj_weight, tile_mask, True)
    own = jnp.concatenate((right_mine, exchange(right_theirs, 1)), axis=1)
    first_a, first_b = hop(own, 0), hop(own, 1)
    left_mine, left_theirs, *forward = front(after(pair, own, panels[0][-2]), gain, bias, proj_weight, tile_mask, False)
    left_other = exchange(left_theirs, 1)

    by_a, by_b, partials = [], [], []
    for c in range(CHUNKS):
        ready = after(left_other, partials[-1]) if partials else left_other
        next_a, next_b = first_step(left_mine, ready, first_a, first_b, panels[c], c)
        partials.append(partial_products(left_mine, left_other, panels[c], c))
        by_a.append([first_a, hop(next_a, 0)])
        by_b.append([first_b, hop(next_b, 1)])

    left_grads = []
    for t in range(2, n):
        for c in range(CHUNKS):
            value = by_a[c][-1]
            if t == n - 1 and c > 0:
                value = after(value, left_grads[c - 1])
            if t == 2:
                next_a, next_b = advance(value, by_b[c][-1], partials[c], t)
            else:
                next_a, next_b = onward(value, by_b[c][-1], partials[c][n - t], partials[c][t], t, n)
            by_a[c].append(hop(next_a, 0))
            by_b[c].append(hop(next_b, 1))
            if t == n - 1:
                left_grads.append(left_products(own, by_a[c][: n - 1], by_b[c][: n - 1], panels[c], c))
    left_grad_other = [exchange(theirs, 1) for _, theirs in left_grads]
    ks = left_mine.shape[1]
    scaled, inverse, factors, last = forward
    own_sums, last_a, last_b = [sums[0] for sums in partials], [v[-1] for v in by_a], [v[-1] for v in by_b]
    right_grad_other = []
    for c in range(CHUNKS):
        value = own_sums[c]
        if c == CHUNKS - 1:
            base = known(
                factors,
                proj_weight,
                [mine for mine, _ in left_grads],
                left_grad_other,
                own_sums[:c],
                last_a[:c],
                last_b[:c],
                right_grad_other,
            )
            value = after(value, base)
        total = arrived_total(value[:, ks:], last_a[c][:, ks:], last_b[c][:, ks:], n)
        right_grad_other.append(exchange(total.astype(jnp.bfloat16), 1))
    return tail(
        base, scaled, inverse, last, gain, proj_weight, own_sums[-1], last_a[-1], last_b[-1], right_grad_other[-1]
    )


def solution(mesh):
    placed = (P("row", "col", None), P("row", "col", None), P(), P(), P(), P())
    return jax.shard_map(
        shards, mesh=mesh, in_specs=placed, out_specs=P("row", "col", None), check_vma=False
    )
```

```python
import functools

import jax
import jax.numpy as jnp
from jax import lax
from jax.experimental import pallas as pl
from jax.experimental.pallas import tpu as pltpu
from jax.sharding import PartitionSpec as P

BLK = 128
CHUNKS = 2
STEP = 8
KEYS = 16
CORES = 2
VMEM_LIMIT = 18 * 1024 * 1024
PARAMS = pltpu.CompilerParams(vmem_limit_bytes=VMEM_LIMIT)
FRONT_COST = pl.CostEstimate(flops=1, bytes_accessed=18_000_000, transcendentals=0)
COST = pl.CostEstimate(flops=1, bytes_accessed=8_000_000, transcendentals=0)
WHOLE = pl.BlockSpec(memory_space=pltpu.VMEM)
BY_LAST = (((1,), (1,)), ((), ()))


def identity(size):
    return (
        lax.broadcasted_iota(jnp.int32, (size, size), 0) == lax.broadcasted_iota(jnp.int32, (size, size), 1)
    ).astype(jnp.bfloat16)


def column(vector_ref, rows):
    return jnp.broadcast_to(vector_ref[...], (rows, vector_ref.shape[1])).T


def unit_mask(mask_ref, rows, cols):
    row, col = lax.axis_index("row"), lax.axis_index("col")
    return mask_ref[(row * rows) // BLK, (col * cols) // BLK].astype(jnp.float32)


def in_hbm(*values):
    return [pltpu.with_memory_space_constraint(v, pltpu.HBM) for v in values]


def this_core():
    return lax.rem(lax.axis_index("col"), CORES)


def turn(pair, flipped, turned):
    flipped[...] = jnp.transpose(pair[...], (1, 0, 2))
    eye = identity(pair.shape[2])
    for key in range(pair.shape[1]):
        if key % 2:
            turned[key] = lax.dot_general(eye, flipped[key], BY_LAST, preferred_element_type=jnp.float32)
        else:
            turned[key] = flipped[key].T.astype(jnp.float32)


def normalize(values):
    centred = values - jnp.mean(values, axis=1, keepdims=True)
    inverse = lax.rsqrt(jnp.mean(centred * centred, axis=1, keepdims=True) + 1e-05)
    return centred * inverse, inverse


def set_columns(gain, bias, weight, gain_col, bias_col, weight_t):
    @pl.when(pl.program_id(0) == 0)
    def _():
        gain_col[...] = column(gain, gain_col.shape[1])
        bias_col[...] = column(bias, bias_col.shape[1])
        weight_t[...] = weight[...].astype(jnp.float32).T.astype(jnp.bfloat16)


def normalized(pair, gain_col, bias_col, flipped, turned, normed):
    turn(pair, flipped, turned)
    scaled, inverse = normalize(turned[...])
    normed[...] = (scaled * gain_col[...] + bias_col[...]).astype(jnp.bfloat16)
    return scaled, inverse


def split_channels(acts, whole, mine, theirs):
    half = mine.shape[0]
    whole[...] = jnp.transpose(acts[...], (1, 0, 2))
    core = this_core()
    mine[...] = whole[pl.ds(core * half, half)]
    theirs[...] = whole[pl.ds((1 - core) * half, half)]


def right_kernel(mask, pair, gain, bias, weight, mine, theirs, flipped, turned, normed, acts, whole, gain_col, bias_col, weight_t):
    rows, keys, _ = pair.shape
    hidden = acts.shape[1]
    set_columns(gain, bias, weight, gain_col, bias_col, weight_t)
    valid = unit_mask(mask, rows, pl.num_programs(0) * keys)
    normalized(pair, gain_col, bias_col, flipped, turned, normed)
    for key in range(keys):
        projected = jnp.dot(weight_t[...], normed[key], preferred_element_type=jnp.float32)
        acts[key] = (valid * jax.nn.sigmoid(projected[hidden:]) * projected[:hidden]).astype(jnp.bfloat16)
    split_channels(acts, whole, mine, theirs)


def last_rows(hidden):
    part = hidden // CORES // CHUNKS
    return [((2 + kind) * hidden + (core * CHUNKS + CHUNKS - 1) * part, part) for kind in range(2) for core in range(CORES)]


def left_forward_kernel(
    mask, pair, gain, bias, weight, mine, theirs, scaled_out, inverse_out, factors, last,
    flipped, turned, normed, acts, whole, gain_col, bias_col, weight_t,
):
    rows, keys, _ = pair.shape
    hidden = acts.shape[1]
    set_columns(gain, bias, weight, gain_col, bias_col, weight_t)
    valid = unit_mask(mask, rows, pl.num_programs(0) * keys)
    scaled, inverse = normalized(pair, gain_col, bias_col, flipped, turned, normed)
    scaled_out[...] = scaled.astype(jnp.bfloat16)
    inverse_out[...] = inverse
    for key in range(keys):
        projected = jnp.dot(weight_t[...], normed[key], preferred_element_type=jnp.float32)
        for side in range(2):
            first = 2 * side * hidden
            lin = projected[first : first + hidden]
            sig = jax.nn.sigmoid(projected[first + hidden : first + 2 * hidden])
            masked = valid * sig
            act = masked * lin
            if side == 0:
                acts[key] = act.astype(jnp.bfloat16)
            factors[key, first : first + hidden, :] = masked.astype(jnp.bfloat16)
            factors[key, first + hidden : first + 2 * hidden, :] = (act * (1.0 - sig)).astype(jnp.bfloat16)
    for i, (first, size) in enumerate(last_rows(hidden)):
        last[:, i * size : (i + 1) * size, :] = factors[:, first : first + size, :]
    split_channels(acts, whole, mine, theirs)


def front(pair, gain, bias, proj_weight, tile_mask, right):
    rows, cols, chans = pair.shape
    width = proj_weight.shape[1]
    hidden = width // 4
    half = hidden // CORES
    used = width // 2 if right else width
    vector = pl.BlockSpec((1, chans), lambda g: (0, 0))
    by_key = lambda *shape: pl.BlockSpec((KEYS,) + shape, lambda g: (g, 0, 0))
    out_shape = [jax.ShapeDtypeStruct((half, cols, rows), jnp.bfloat16)] * 2
    out_specs = [pl.BlockSpec((half, KEYS, rows), lambda g: (0, g, 0))] * 2
    if not right:
        out_shape += [
            jax.ShapeDtypeStruct((cols, chans, rows), jnp.bfloat16),
            jax.ShapeDtypeStruct((cols, 1, rows), jnp.float32),
            jax.ShapeDtypeStruct((cols, width, rows), jnp.bfloat16),
            jax.ShapeDtypeStruct((cols, 2 * hidden // CHUNKS, rows), jnp.bfloat16),
        ]
        out_specs += [by_key(chans, rows), by_key(1, rows), by_key(width, rows), by_key(2 * hidden // CHUNKS, rows)]
    return pl.pallas_call(
        right_kernel if right else left_forward_kernel,
        out_shape=out_shape,
        grid=(cols // KEYS,),
        in_specs=[
            pl.BlockSpec(memory_space=pltpu.SMEM),
            pl.BlockSpec((rows, KEYS, chans), lambda g: (0, g, 0)),
            vector,
            vector,
            pl.BlockSpec((chans, used), lambda g: (0, 1 if right else 0)),
        ],
        out_specs=out_specs,
        scratch_shapes=[
            pltpu.VMEM((KEYS, rows, chans), jnp.bfloat16),
            pltpu.VMEM((KEYS, chans, rows), jnp.float32),
            pltpu.VMEM((KEYS, chans, rows), jnp.bfloat16),
            pltpu.VMEM((KEYS, hidden, rows), jnp.bfloat16),
            pltpu.VMEM((hidden, KEYS, rows), jnp.bfloat16),
            pltpu.VMEM((chans, rows), jnp.float32),
            pltpu.VMEM((chans, rows), jnp.float32),
            pltpu.VMEM((used, chans), jnp.bfloat16),
        ],
        compiler_params=PARAMS,
        cost_estimate=FRONT_COST,
        name="right_front" if right else "left_front",
    )(tile_mask, *in_hbm(pair, gain, bias, proj_weight))


def half_kernel(theirs, raw, out, sem):
    half = out.shape[1]
    core = this_core()
    first = pl.multiple_of((1 - core if theirs else core) * half, half)
    copy = pltpu.make_async_copy(raw.at[:, pl.ds(first, half), :], out, sem)
    copy.start()
    copy.wait()


def take_half(raw, theirs):
    cols, hidden, rows = raw.shape
    return pl.pallas_call(
        functools.partial(half_kernel, theirs),
        out_shape=jax.ShapeDtypeStruct((cols, hidden // CORES, rows), raw.dtype),
        in_specs=[pl.BlockSpec(memory_space=pl.ANY)],
        out_specs=WHOLE,
        scratch_shapes=[pltpu.SemaphoreType.DMA],
        compiler_params=PARAMS,
        cost_estimate=COST,
        name="theirs" if theirs else "mine",
    )(*in_hbm(raw))


def pack_kernel(own, other, *outs):
    cols = other.shape[0]
    core = this_core()
    for block, place in ((own, core), (other, 1 - core)):
        flipped = jnp.transpose(block[...], (1, 0, 2))
        for chunk, out in enumerate(outs):
            chans = out.shape[0]
            out[:, pl.ds(pl.multiple_of(place * cols, cols), cols), :] = flipped[chunk * chans : (chunk + 1) * chans]


def pack(own, other):
    cols, half, rows = other.shape
    return pl.pallas_call(
        pack_kernel,
        out_shape=[jax.ShapeDtypeStruct((half // CHUNKS, CORES * cols, rows), jnp.bfloat16)] * CHUNKS,
        in_specs=[WHOLE] * 2,
        out_specs=[WHOLE] * CHUNKS,
        compiler_params=PARAMS,
        cost_estimate=COST,
        name="pack",
    )(own, other)


def chunk_spec(array, chans, chunk):
    first = chunk * chans // STEP if array.shape[0] > chans else 0
    return pl.BlockSpec((STEP,) + array.shape[1:], lambda g: (first + g, 0, 0))


def slot_mask(m, core, chips):
    width = chips.bit_length() - 1
    return m if core == 0 else sum(1 << (width - 1 - b) for b in range(width) if m >> b & 1)


def slot_chips(chips):
    chip = lax.axis_index("col") // CORES
    return [
        jnp.bitwise_xor(chip, jnp.where(this_core() == 0, m, slot_mask(m, 1, chips))) for m in range(chips)
    ]


def lanes(n):
    row = lax.axis_index("row")
    even = lax.rem(row, 2) == 0
    return even, jnp.where(even, row + 1 < n, True), jnp.where(even, row > 0, row + 1 < n)


def onward(by_a, by_b, up_sums, down_sums, t, n):
    row = lax.axis_index("row")
    even, use_a, use_b = lanes(n)
    up = jnp.where(row < t, up_sums.astype(jnp.float32), 0.0)
    down = jnp.where(row >= n - t, down_sums.astype(jnp.float32), 0.0)
    out_a = jnp.where(use_b, by_b.astype(jnp.float32), 0.0) + jnp.where(even, up, down)
    out_b = jnp.where(use_a, by_a.astype(jnp.float32), 0.0) + jnp.where(even, down, up)
    return out_a.astype(jnp.bfloat16), out_b.astype(jnp.bfloat16)


def first_kernel(chunk, left_mine, left_other, by_a, by_b, *refs):
    *blocks, next_a, next_b = refs
    n = len(blocks)
    holders, target = slot_chips(n), jnp.where(lax.axis_index("row") == 0, n - 1, 0)
    chans = next_a.shape[0]
    for c in range(chans):
        at = chunk * chans + c
        lhs = jnp.concatenate((left_mine[at], left_other[at]), axis=0)
        rhs = blocks[0][c]
        for m in range(1, n):
            rhs = jnp.where(holders[m] == target, blocks[m][c], rhs)
        sums = lax.dot_general(lhs, rhs, BY_LAST, preferred_element_type=jnp.float32).astype(jnp.bfloat16)
        next_a[c], next_b[c] = onward(by_a[at], by_b[at], sums, sums, 1, n)


def first_step(left_mine, left_other, by_a, by_b, blocks, chunk):
    shape = (left_mine.shape[0] // CHUNKS,) + by_a.shape[1:]
    args = (left_mine, left_other, by_a, by_b, *blocks)
    return pl.pallas_call(
        functools.partial(first_kernel, chunk),
        out_shape=[jax.ShapeDtypeStruct(shape, jnp.bfloat16)] * 2,
        in_specs=[WHOLE] * len(args),
        out_specs=[WHOLE] * 2,
        compiler_params=PARAMS,
        cost_estimate=COST,
        name="first_step",
    )(*args)


def partial_kernel(n, left_mine, left_other, *refs):
    blocks, outs, sums = refs[:n], refs[n : 2 * n], refs[2 * n]
    row, holders = lax.axis_index("row"), slot_chips(n)
    for c in range(STEP):
        lhs = jnp.concatenate((left_mine[c], left_other[c]), axis=0)
        for holder, block in zip(holders, blocks):
            away = lax.rem(holder - row + n, n)
            sums[away, c] = lax.dot_general(lhs, block[c], BY_LAST, preferred_element_type=jnp.float32).astype(jnp.bfloat16)
    for s, out in enumerate(outs):
        out[...] = sums[s]


def partial_products(left_mine, left_other, blocks, chunk):
    chans, rows, _ = blocks[0].shape
    ks = left_mine.shape[1]
    n = len(blocks)
    args = (left_mine, left_other, *blocks)
    return pl.pallas_call(
        functools.partial(partial_kernel, n),
        out_shape=[
            (jax.ShapeDtypeStruct if s in (2, n - 2) else pltpu.HBM)((chans, CORES * ks, rows), jnp.bfloat16)
            for s in range(n)
        ],
        grid=(chans // STEP,),
        in_specs=[chunk_spec(v, chans, chunk) for v in args],
        out_specs=[pl.BlockSpec((STEP, CORES * ks, rows), lambda g: (g, 0, 0))] * n,
        scratch_shapes=[pltpu.VMEM((n, STEP, CORES * ks, rows), jnp.bfloat16)],
        compiler_params=PARAMS,
        cost_estimate=COST,
        name="right_partials",
    )(*args)


def advance_kernel(t, n, by_a, by_b, up_sums, down_sums, next_a, next_b):
    next_a[...], next_b[...] = onward(by_a[...], by_b[...], up_sums[...], down_sums[...], t, n)


def advance(by_a, by_b, sums, t):
    n = len(sums)
    return pl.pallas_call(
        functools.partial(advance_kernel, t, n),
        out_shape=[jax.ShapeDtypeStruct(by_a.shape, by_a.dtype)] * 2,
        in_specs=[WHOLE] * 4,
        out_specs=[WHOLE] * 2,
        compiler_params=PARAMS,
        cost_estimate=COST,
        name="advance",
    )(by_a, by_b, sums[n - t], sums[t])


def left_kernel(n, own, *refs):
    by_a, by_b, refs = refs[: n - 1], refs[n - 1 : 2 * n - 2], refs[2 * n - 2 :]
    blocks, (mine, theirs, panel) = refs[:n], refs[n:]
    row, holders = lax.axis_index("row"), slot_chips(n)
    even = lanes(n)[0]
    ks = mine.shape[1]
    for c in range(STEP):
        for holder, block in zip(holders, blocks):
            panel[c, holder] = block[c]
        acts, grads = [own[c]], [panel[c, row]]
        for s in range(1, n):
            from_above = jnp.where(even, by_a[s - 1][c], by_b[s - 1][c])
            from_below = jnp.where(even, by_b[n - s - 1][c], by_a[n - s - 1][c])
            acts.append(jnp.where(row + s < n, from_above, from_below))
            grads.append(panel[c, lax.rem(row + s, n)])
        out = jnp.dot(
            jnp.concatenate(acts, axis=1), jnp.concatenate(grads, axis=0), preferred_element_type=jnp.float32
        )
        mine[c] = out[:ks]
        theirs[c] = out[ks:].astype(jnp.bfloat16)


def left_products(own, by_a, by_b, blocks, chunk):
    chans, ks, rows = by_a[-1].shape
    n = len(blocks)
    out = pl.BlockSpec((STEP, ks // CORES, rows), lambda g: (g, 0, 0))
    args = (own, *by_a, *by_b, *blocks)
    return pl.pallas_call(
        functools.partial(left_kernel, n),
        out_shape=[
            jax.ShapeDtypeStruct((chans, ks // CORES, rows), jnp.float32),
            jax.ShapeDtypeStruct((chans, ks // CORES, rows), jnp.bfloat16),
        ],
        grid=(chans // STEP,),
        in_specs=[chunk_spec(v, chans, chunk) for v in args],
        out_specs=[out] * 2,
        scratch_shapes=[pltpu.VMEM((STEP, n, rows, rows), jnp.bfloat16)],
        compiler_params=PARAMS,
        cost_estimate=COST,
        name="left_products",
    )(*in_hbm(*args))


def arrived_total(own, by_a, by_b, n):
    _, use_a, use_b = lanes(n)
    total = own.astype(jnp.float32) + jnp.where(use_a, by_a.astype(jnp.float32), 0.0)
    return total + jnp.where(use_b, by_b.astype(jnp.float32), 0.0)


def put(flat, owner, value):
    size = value.shape[0] * value.shape[1]
    flat[pl.ds(pl.multiple_of(owner * size, size), size), :] = value.astype(jnp.float32).reshape(size, value.shape[2])


def known_kernel(n, factors, weight, *refs):
    known = CHUNKS - 1
    left_mine, left_other = refs[:CHUNKS], refs[CHUNKS : 2 * CHUNKS]
    partials, by_a, by_b, right_other = (refs[2 * CHUNKS + i * known : 2 * CHUNKS + (i + 1) * known] for i in range(4))
    out, grads, *flats = refs[2 * CHUNKS + 4 * known :]
    keys, width, _ = factors.shape
    hidden = width // 4
    part = hidden // CORES // CHUNKS
    core = this_core()

    @pl.when(pl.program_id(0) == 0)
    def _():
        grads[...] = jnp.zeros_like(grads)

    for chunk in range(CHUNKS):
        put(flats[chunk], core, left_mine[chunk][...])
        put(flats[chunk], 1 - core, left_other[chunk][...])
    for chunk in range(known):
        put(flats[CHUNKS + chunk], core, arrived_total(partials[chunk][...], by_a[chunk][...], by_b[chunk][...], n))
        put(flats[CHUNKS + chunk], 1 - core, right_other[chunk][...])
    for key in range(keys):
        for i, flat in enumerate(flats):
            side, chunk = divmod(i, CHUNKS)
            grad = flat[pl.ds(key, CORES * part, stride=keys), :]
            for owner in range(CORES):
                for kind in range(2):
                    first = (2 * side + kind) * hidden + (owner * CHUNKS + chunk) * part
                    place = slice(first, first + part)
                    factor = factors[key, place, :].astype(jnp.float32)
                    grads[key, place, :] = (grad[owner * part : (owner + 1) * part] * factor).astype(jnp.bfloat16)
    for key in range(keys):
        out[key] = jnp.dot(weight[...], grads[key], preferred_element_type=jnp.float32)


def known(factors, proj_weight, left_mine, left_other, partials, by_a, by_b, right_other):
    cols, width, rows = factors.shape
    chans, hidden = proj_weight.shape[0], width // 4
    part = hidden // CORES // CHUNKS
    by_key = lambda *shape: pl.BlockSpec((KEYS,) + shape, lambda g: (g, 0, 0))
    args = (*left_mine, *left_other, *partials, *by_a, *by_b, *right_other)
    return pl.pallas_call(
        functools.partial(known_kernel, lax.axis_size("row")),
        out_shape=jax.ShapeDtypeStruct((cols, chans, rows), jnp.float32),
        grid=(cols // KEYS,),
        in_specs=[by_key(width, rows), pl.BlockSpec((chans, width), lambda g: (0, 0))]
        + [pl.BlockSpec((part, KEYS, rows), lambda g: (0, g, 0))] * len(args),
        out_specs=by_key(chans, rows),
        scratch_shapes=[pltpu.VMEM((KEYS, width, rows), jnp.bfloat16)]
        + [pltpu.VMEM(((CORES * part + 1) * KEYS, rows), jnp.float32)] * (2 * CHUNKS - 1),
        compiler_params=PARAMS,
        cost_estimate=COST,
        name="known",
    )(factors, proj_weight, *args)


def tail_kernel(n, base, scaled, inverse, last, gain, weight, partials, by_a, by_b, right_other, out, results, flipped, grads, flat, gain_col):
    _, keys, chans = out.shape
    rows = scaled.shape[2]
    core = this_core()

    @pl.when(pl.program_id(0) == 0)
    def _():
        gain_col[...] = column(gain, rows)

    first_key = pl.program_id(0) * keys
    here = pl.ds(pl.multiple_of(first_key, keys), keys)
    put(flat, core, arrived_total(partials[:, here, :], by_a[:, here, :], by_b[:, here, :], n))
    put(flat, 1 - core, right_other[:, here, :])
    count = last.shape[1] // 2
    for key in range(keys):
        grad = flat[pl.ds(key, count, stride=keys), :]
        for kind in range(2):
            place = slice(kind * count, (kind + 1) * count)
            grads[key, place, :] = (grad * last[first_key + key, place, :].astype(jnp.float32)).astype(jnp.bfloat16)
    for key in range(keys):
        scaled_key = scaled[first_key + key].astype(jnp.float32)
        added = jnp.dot(weight[...], grads[key], preferred_element_type=jnp.float32)
        scaled_grad = (base[first_key + key] + added) * gain_col[...]
        result = inverse[first_key + key] * (
            scaled_grad
            - jnp.mean(scaled_grad, axis=0, keepdims=True)
            - scaled_key * jnp.mean(scaled_grad * scaled_key, axis=0, keepdims=True)
        )
        results[key] = result.astype(jnp.bfloat16)
    eye = identity(rows)
    for key in range(keys):
        if key % 2:
            turned = lax.dot_general(eye, results[key], BY_LAST, preferred_element_type=jnp.float32)
            flipped[key] = turned.astype(jnp.bfloat16)
        else:
            flipped[key] = results[key].T
    out[...] = jnp.transpose(flipped[...], (1, 0, 2))


def tail(base, scaled, inverse, last, gain, proj_weight, partials, by_a, by_b, right_other):
    cols, chans, rows = scaled.shape
    hidden, part = proj_weight.shape[1] // 4, partials.shape[0]
    weight = jnp.concatenate([proj_weight[:, first : first + size] for first, size in last_rows(hidden)], axis=1)
    return pl.pallas_call(
        functools.partial(tail_kernel, lax.axis_size("row")),
        out_shape=jax.ShapeDtypeStruct((rows, cols, chans), jnp.bfloat16),
        grid=(cols // KEYS,),
        in_specs=[WHOLE] * 10,
        out_specs=pl.BlockSpec((rows, KEYS, chans), lambda g: (0, g, 0)),
        scratch_shapes=[
            pltpu.VMEM((KEYS, chans, rows), jnp.bfloat16),
            pltpu.VMEM((KEYS, rows, chans), jnp.bfloat16),
            pltpu.VMEM((KEYS, last.shape[1], rows), jnp.bfloat16),
            pltpu.VMEM(((CORES * part + 1) * KEYS, rows), jnp.float32),
            pltpu.VMEM((chans, rows), jnp.float32),
        ],
        compiler_params=PARAMS,
        cost_estimate=COST,
        name="tail",
    )(base, scaled, inverse, last, gain, weight, partials, by_a, by_b, right_other)


def after(value, *others):
    return lax.optimization_barrier((value, others))[0]


def shards(pair, grad_x, norm_gain, norm_bias, proj_weight, tile_mask):
    n, n_col = lax.axis_size("row"), lax.axis_size("col")
    half = grad_x.shape[2] // CORES
    part = half // CHUNKS
    gain, bias = norm_gain[None, :], norm_bias[None, :]

    def exchange(value, mask):
        return lax.ppermute(value, "col", [(d, d ^ mask) for d in range(n_col)])

    def hop(value, first):
        pairs = {r: r + 1 for r in range(first, n - 1, 2)}
        pairs.update({above: r for r, above in pairs.items()})
        perm = [
            (r * n_col + d, pairs[r] * n_col + d if r in pairs else r * n_col + (d ^ 1)) for r in range(n) for d in range(n_col)
        ]
        return lax.ppermute(value, ("row", "col"), perm)

    raw = jnp.transpose(grad_x, (1, 2, 0))
    other = exchange(take_half(raw, True), 1)
    packed = pack(take_half(raw, False), other)

    chips = n_col // CORES

    def along(value, bit):
        mask = [CORES * slot_mask(bit, core, chips) for core in range(CORES)]
        return lax.ppermute(value, "col", [(d, d ^ mask[d % CORES]) for d in range(n_col)])

    panels = []
    for block in packed:
        slots = [after(block, panels[-1][1:]) if panels else block]
        for m in range(1, chips):
            bit = 1 << (m.bit_length() - 1)
            slots.append(along(slots[m ^ bit], bit))
        panels.append(slots)

    right_mine, right_theirs = front(after(pair, packed), gain, bias, proj_weight, tile_mask, True)
    own = jnp.concatenate((right_mine, exchange(right_theirs, 1)), axis=1)
    first_a, first_b = hop(own, 0), hop(own, 1)
    left_mine, left_theirs, *forward = front(after(pair, own, panels[0][-2]), gain, bias, proj_weight, tile_mask, False)
    left_other = exchange(left_theirs, 1)

    by_a, by_b, partials = [], [], []
    for c in range(CHUNKS):
        ready = after(left_other, partials[-1]) if partials else left_other
        next_a, next_b = first_step(left_mine, ready, first_a, first_b, panels[c], c)
        partials.append(partial_products(left_mine, left_other, panels[c], c))
        by_a.append([first_a, hop(next_a, 0)])
        by_b.append([first_b, hop(next_b, 1)])

    left_grads = []
    for t in range(2, n):
        for c in range(CHUNKS):
            value = by_a[c][-1]
            if t == n - 1 and c > 0:
                value = after(value, left_grads[c - 1])
            next_a, next_b = advance(value, by_b[c][-1], partials[c], t)
            by_a[c].append(hop(next_a, 0))
            by_b[c].append(hop(next_b, 1))
            if t == n - 1:
                left_grads.append(left_products(own, by_a[c][: n - 1], by_b[c][: n - 1], panels[c], c))
    left_grad_other = [exchange(theirs, 1) for _, theirs in left_grads]
    ks = left_mine.shape[1]
    scaled, inverse, factors, last = forward
    own_sums, last_a, last_b = [sums[0] for sums in partials], [v[-1] for v in by_a], [v[-1] for v in by_b]
    right_grad_other = []
    for c in range(CHUNKS):
        value = own_sums[c]
        if c == CHUNKS - 1:
            base = known(
                factors,
                proj_weight,
                [mine for mine, _ in left_grads],
                left_grad_other,
                own_sums[:c],
                last_a[:c],
                last_b[:c],
                right_grad_other,
            )
            value = after(value, base)
        total = arrived_total(value[:, ks:], last_a[c][:, ks:], last_b[c][:, ks:], n)
        right_grad_other.append(exchange(total.astype(jnp.bfloat16), 1))
    return tail(
        base, scaled, inverse, last, gain, proj_weight, own_sums[-1], last_a[-1], last_b[-1], right_grad_other[-1]
    )


def solution(mesh):
    placed = (P("row", "col", None), P("row", "col", None), P(), P(), P(), P())
    return jax.shard_map(
        shards, mesh=mesh, in_specs=placed, out_specs=P("row", "col", None), check_vma=False
    )
```
